32 devices in a mesh: prow: 4 (over x, core), pcol: 8 (over z, y).
Axes of the slice: x: 2, y: 2, z: 4, core: 2. Of those that a mesh axis runs over, the one named last changes fastest.
Arguments:
- matrix: float32 [8192, 5120], P('prow', 'pcol'), may hold values from -6 to 6
- pivots: int32 [512], replicated, may hold values from 0 to 8191, as said below
- lower_inverse: float32 [512, 512], replicated, as said below
- upper_inverse: float32 [512, 512], replicated, as said below
Outputs:
- factored: float32 [8192, 5120], P('prow', 'pcol')
The draws below stay inside these ranges and needn't reach their ends.
Inputs may be any that keep to these rules, and one draw needn't show every extreme that they name: The 512 pivots are distinct. `lower_inverse`: unit diagonal, zeros above it. `upper_inverse`: zeros below the diagonal, a positive diagonal.
All inputs are finite; a program needn't handle non-finite values.
Results may differ from the reference program's by a relative error of at most 0.00005.
Values sent between devices are 32-bit elements; how exact they have to be, the bound alone decides.
No kernel may reach another device: no remote copies, remote signals or barrier semaphores. Data moves between devices by JAX's collectives and lax.ppermute only.
A program may use at most 128 MiB of HBM per device.

```python
import jax
import jax.numpy as jnp
from jax import lax

NB = 512
ROWS = 8192
COLS = 5120


def draw_pivots(key, part):
    inner_key = jax.random.fold_in(key, 11)
    order_key = jax.random.fold_in(key, 23)
    inner = 1 + jax.random.permutation(inner_key, ROWS - 2)[:NB - 2]
    ends = jnp.array([0, ROWS - 1], dtype=jnp.int32)
    chosen = jnp.concatenate([ends, inner.astype(jnp.int32)], axis=0)
    placed = jax.random.permutation(order_key, NB)
    return chosen[placed].astype(jnp.int32)


def draw_lower_inverse(key, part):
    entries = jax.random.normal(key, (NB, NB), jnp.float32)
    strict = jnp.tril(entries, -1) * NB ** (-0.5)
    return (strict + jnp.eye(NB, dtype=jnp.float32)).astype(jnp.float32)


def draw_upper_inverse(key, part):
    first_key, second_key = jax.random.split(key)
    entries = jax.random.normal(first_key, (NB, NB), jnp.float32)
    diag = jnp.exp(jax.random.uniform(second_key, (NB,), jnp.float32, 0.0, jnp.log(2.0)))
    strict = jnp.triu(entries, 1) * NB ** (-0.5)
    return (0.05 * (strict + jnp.diag(diag))).astype(jnp.float32)


def block_scale(own_key, extent, pieces, low, largest):
    def one(position, blocks):
        steps = jax.random.uniform(jax.random.fold_in(jax.random.fold_in(own_key, 6), position), (blocks,), jnp.float32, low / len(pieces), largest / len(pieces))
        return jnp.repeat(jnp.exp(steps), extent[position] // blocks).reshape((-1,) + (1,) * (len(extent) - position - 1))

    factor_of = one(*pieces[0])
    for cut in pieces[1:]:
        factor_of = factor_of * one(*cut)
    return factor_of


def gaussian(rng, shape, deviation, bound, pieces=(), held_as=jnp.bfloat16):
    drawn = deviation * jax.random.normal(rng, shape, jnp.float32)
    if pieces:
        drawn = drawn * block_scale(rng, shape, pieces, -0.22, 0.18)
    return jnp.clip(drawn, -bound, bound).astype(held_as)


def setup_inputs(seed: int = 0) -> dict:
    splits = jax.random.split(jax.random.key(seed), 5)
    return {
        "matrix": gaussian(splits[0], (ROWS, COLS), 1.0, 6.0, ((0, 4), (1, 8)), jnp.float32),
        "pivots": draw_pivots(jax.random.fold_in(splits[4], 71), 0),
        "lower_inverse": draw_lower_inverse(jax.random.fold_in(splits[4], 71), 0),
        "upper_inverse": draw_upper_inverse(jax.random.fold_in(splits[4], 71), 0),
    }


def row_sources(pivots, panel_width):
    below = pivots >= panel_width
    vac_rank = jnp.cumsum(below.astype(jnp.int32)) - 1
    slot_ids = jnp.arange(panel_width, dtype=jnp.int32)
    chosen_top = jnp.any(pivots[:, None] == slot_ids[None, :], axis=0)
    freed_rows = jnp.logical_not(chosen_top)
    freed_rank = jnp.cumsum(freed_rows.astype(jnp.int32)) - 1
    pairing = freed_rows[None, :] & (freed_rank[None, :] == vac_rank[:, None])
    source_rows = jnp.sum(jnp.where(pairing, slot_ids[None, :], 0), axis=1).astype(jnp.int32)
    return below, source_rows


def reference(matrix, pivots, lower_inverse, upper_inverse):
    below, source_rows = row_sources(pivots, NB)
    row_order = jnp.arange(ROWS, dtype=jnp.int32)
    row_order = row_order.at[:NB].set(pivots)
    targets = jnp.where(below, pivots, ROWS).astype(jnp.int32)
    row_order = row_order.at[targets].set(source_rows, mode="drop")
    swapped = jnp.take(matrix, row_order, axis=0)
    u_rows = jnp.dot(lower_inverse, swapped[:NB], precision=lax.Precision.HIGHEST)
    lower_factor = jnp.dot(swapped[NB:, :NB], upper_inverse, precision=lax.Precision.HIGHEST)
    trailing = swapped[NB:, NB:] - jnp.dot(lower_factor, u_rows[:, NB:], precision=lax.Precision.HIGHEST)
    upper_band = jnp.concatenate([swapped[:NB, :NB], u_rows[:, NB:]], axis=1)
    lower_band = jnp.concatenate([lower_factor, trailing], axis=1)
    return jnp.concatenate([upper_band, lower_band], axis=0)
```

```python
import functools

import jax
import jax.numpy as jnp
from jax import lax
from jax.experimental import pallas as pl
from jax.experimental.pallas import tpu as pltpu
from jax.sharding import PartitionSpec as P

HIGHEST = lax.Precision.HIGHEST
VMEM = pl.BlockSpec(memory_space=pltpu.VMEM)
SMEM = pl.BlockSpec(memory_space=pltpu.SMEM)
ANY = pl.BlockSpec(memory_space=pl.ANY)
LANES = 128
PICK, FROM, ROW, COUNT = 0, 1, 2, 3


def call(kernel, out, ins, outs, scratch=(), vmem=40 << 20, flops=0, moved=0):
    return pl.pallas_call(
        kernel,
        out_shape=out,
        in_specs=ins,
        out_specs=outs,
        scratch_shapes=list(scratch),
        compiler_params=pltpu.CompilerParams(vmem_limit_bytes=vmem),
        cost_estimate=pl.CostEstimate(
            flops=flops, bytes_accessed=moved, transcendentals=0
        ),
    )


def index_kernel(where_ref, pivots_ref, table_ref, owner_ref, *, row_dev):
    nb = pivots_ref.shape[1]
    start = where_ref[0] * row_dev
    first = where_ref[0] == 0
    down = lax.broadcasted_iota(jnp.int32, (nb, nb), 0)
    across = lax.broadcasted_iota(jnp.int32, (nb, nb), 1)
    piv_row = jnp.broadcast_to(pivots_ref[...], (nb, nb))

    def column(full):
        return jnp.sum(jnp.where(down == across, full, 0.0), axis=1, keepdims=True)

    piv_f = piv_row.astype(jnp.float32)
    piv_col = jnp.broadcast_to(column(piv_f), (nb, nb))
    upto = (down <= across).astype(jnp.bfloat16)
    below = (piv_row >= nb).astype(jnp.float32)
    vacancy = jnp.dot(
        below[:8].astype(jnp.bfloat16), upto, preferred_element_type=jnp.float32
    )[:1]
    taken = jnp.max((piv_row == down).astype(jnp.float32), axis=1, keepdims=True)
    freed = jnp.broadcast_to(1.0 - taken, (nb, LANES))
    rank = jnp.dot(
        (across <= down).astype(jnp.bfloat16),
        freed.astype(jnp.bfloat16),
        preferred_element_type=jnp.float32,
    )[:, :1]
    down_f = down.astype(jnp.float32)
    pair = (rank == vacancy) & (freed[:, :1] > 0.5)
    source = jnp.sum(jnp.where(pair, down_f, 0.0), axis=0, keepdims=True)
    source_col = jnp.broadcast_to(column(jnp.broadcast_to(source, (nb, nb))), (nb, nb))

    own_row = (pivots_ref[...] >= start) & (pivots_ref[...] < start + row_dev)
    pick = jnp.where(own_row, pivots_ref[...] - start, source.astype(jnp.int32))
    moved_row = (own_row & (pivots_ref[...] >= nb)).astype(jnp.float32)
    start_f = start.astype(jnp.float32)
    moved_col = (
        (piv_col >= start_f) & (piv_col < start_f + row_dev) & (piv_col >= nb)
    )
    order = jnp.sum(
        jnp.where(piv_f < piv_col, jnp.broadcast_to(moved_row, (nb, nb)), 0.0),
        axis=1,
        keepdims=True,
    )
    placed = moved_col & (order == across.astype(jnp.float32))
    origin = jnp.where(first, source_col, down_f)
    listed_from = jnp.sum(jnp.where(placed, origin, 0.0), axis=0, keepdims=True)
    listed_row = jnp.sum(
        jnp.where(placed, piv_col - start_f, 0.0), axis=0, keepdims=True
    )
    count = jnp.sum(moved_row, axis=1, keepdims=True)
    table_ref[...] = jnp.zeros_like(table_ref)
    table_ref[PICK : PICK + 1, :] = pick
    table_ref[FROM : FROM + 1, :] = listed_from.astype(jnp.int32)
    table_ref[ROW : ROW + 1, :] = listed_row.astype(jnp.int32)
    table_ref[COUNT : COUNT + 1, :] = jnp.broadcast_to(
        count.astype(jnp.int32), (1, nb)
    )
    owner_ref[...] = piv_col[:, :LANES].astype(jnp.int32) // row_dev


def gather_kernel(table_ref, matrix_ref, out_ref):
    nb = out_ref.shape[0]

    @pl.loop(0, nb, step=8)
    def _(base):
        for k in range(8):
            j = base + k
            out_ref[pl.ds(j, 1), :] = matrix_ref[pl.ds(table_ref[PICK, j], 1), :]


def merge_kernel(where_ref, owner_ref, held_ref, *refs, log, halves):
    arrived, (merged_ref, half_ref) = refs[: 2 if halves else 1], refs[-2:]
    me = where_ref[0]
    mine, theirs = me >> log, (me >> log) ^ 1
    odd = me & 1
    nb, cols = held_ref.shape
    half = nb // 2

    def merge(rows, piece):
        group = owner_ref[rows, :] >> log
        take = (group == theirs) | ((theirs == 0) & (group != mine))
        for q in range(cols // LANES):
            lane = slice(q * LANES, (q + 1) * LANES)
            merged_ref[rows, lane] = jnp.where(take, piece[:, lane], held_ref[rows, lane])

    low, high = slice(0, half), slice(half, nb)
    if halves:
        @pl.when(odd == 0)
        def _():
            merge(low, arrived[0])
            merge(high, arrived[1])

        @pl.when(odd == 1)
        def _():
            merge(low, arrived[1])
            merge(high, arrived[0])
    else:
        merge(slice(0, nb), arrived[0])

    @pl.when(odd == 0)
    def _():
        half_ref[...] = merged_ref[low, :]

    @pl.when(odd == 1)
    def _():
        half_ref[...] = merged_ref[high, :]


def factor_kernel(where_ref, top_in_ref, lower_ref, upper_ref, weights_ref, top_ref):
    nb, cols = top_in_ref.shape
    u = jnp.dot(
        lower_ref[...], top_in_ref[...], precision=HIGHEST,
        preferred_element_type=jnp.float32,
    )
    top_ref[...] = u
    weights_ref[...] = jnp.dot(
        upper_ref[...], u, precision=HIGHEST, preferred_element_type=jnp.float32
    )

    @pl.when(where_ref[1] == 0)
    def _():
        top_ref[:, :nb] = top_in_ref[:, :nb]
        weights_ref[:, :nb] = -upper_ref[...]


def final_kernel(
    where_ref, table_ref, choice_ref, displaced_ref, weights_ref, top_ref, matrix_ref,
    *refs, counts, chunk, extra, block,
):
    n_bufs = sum(counts)
    bufs = refs[:n_bufs]
    out_ref = refs[n_bufs]
    mat, pan, low, w_hi, w_lo, result, in_sem, mat_sem, out_sem = refs[n_bufs + 1 :]
    rows, cols = matrix_ref.shape
    nb = weights_ref.shape[0]
    first_row, first_col = where_ref[0] == 0, where_ref[1] == 0
    full = rows // (2 * chunk)

    load = pltpu.make_async_copy(matrix_ref, mat, mat_sem)
    load.start()

    def place(i, h):
        if i < full:
            return pan.at[pl.ds((2 * i + h) * chunk, chunk), :]
        return low.at[pl.ds((2 * (i - full) + h) * chunk, chunk), :]

    @pl.when(first_col)
    def _():
        pltpu.make_async_copy(matrix_ref.at[:, pl.ds(0, nb)], pan, in_sem).start()
        pltpu.make_async_copy(displaced_ref.at[:, pl.ds(0, nb)], low, in_sem).start()

    @pl.when(jnp.logical_not(first_col))
    def _():
        for i in range(full + extra):
            for h in range(2):
                for b in candidates(i, h, counts):
                    @pl.when(choice_ref[2 * i + h] == b)
                    def _():
                        pltpu.make_async_copy(bufs[b], place(i, h), in_sem).start()

    w = weights_ref[...]
    w_hi[...] = w.astype(jnp.bfloat16)
    w_lo[...] = (w - w_hi[...].astype(jnp.float32)).astype(jnp.bfloat16)

    pltpu.make_async_copy(matrix_ref.at[:, pl.ds(0, nb)], pan, in_sem).wait()
    pltpu.make_async_copy(displaced_ref.at[:, pl.ds(0, nb)], low, in_sem).wait()
    load.wait()

    count = table_ref[COUNT, 0]

    def swap(from_mat, from_pan):
        def body(k, _):
            to, at = table_ref[ROW, k], table_ref[FROM, k]
            mat[pl.ds(to, 1), :] = from_mat[pl.ds(at, 1), :]
            pan[pl.ds(to, 1), :] = from_pan[pl.ds(at, 1), :]
            return 0

        lax.fori_loop(0, count, body, 0)

    @pl.when(first_row)
    def _():
        swap(mat, pan)

    @pl.when(jnp.logical_not(first_row))
    def _():
        swap(displaced_ref, low)

    @pl.when(first_col)
    def _():
        mat[:, :nb] = jnp.zeros((rows, nb), jnp.float32)

    copies = []
    for b in range(rows // block):
        span = pl.ds(b * block, block)

        def update():
            p = pan[span, :]
            p_hi = p.astype(jnp.bfloat16)
            p_lo = (p - p_hi.astype(jnp.float32)).astype(jnp.bfloat16)
            dot = functools.partial(jnp.dot, preferred_element_type=jnp.float32)
            total = dot(p_lo, w_hi[...]) + dot(p_hi, w_lo[...]) + dot(p_hi, w_hi[...])
            result[span, :] = mat[span, :] - total

        if (b + 1) * block <= nb:
            pl.when(jnp.logical_not(first_row))(update)

            @pl.when(first_row)
            def _():
                result[span, :] = top_ref[span, :]
        else:
            update()
        copy = pltpu.make_async_copy(result.at[span, :], out_ref.at[span, :], out_sem)
        copy.start()
        copies.append(copy)
    for copy in copies:
        copy.wait()


def candidates(i, h, counts):
    n_feed, n_chain, n_cross, n_back = counts
    depth = n_chain - n_feed + 1
    chain, cross = n_feed, n_feed + n_chain
    back = cross + n_cross
    if h == 0:
        found = [i]
        for z in range(1, depth):
            found += [chain + i + z, cross + i + z]
    else:
        found = [back + i]
        for z in range(1, depth):
            found += [chain + i + z - 1, cross + i + z - 1]
    return found


def choice_table(n_cols, counts):
    n_feed, n_chain, n_cross, n_back = counts
    chain, cross = n_feed, n_feed + n_chain
    back = cross + n_cross
    table = []
    for p in range(n_cols):
        z, y = divmod(p, 2)
        row = []
        for i in range(n_feed):
            if z == 0:
                row += [i, back + i] if y else [0, 0]
            elif y:
                row += [chain + i + z, cross + i + z - 1]
            else:
                row += [cross + i + z, chain + i + z - 1]
        table.append(row)
    return table


def spread(pieces, col, n_cols):
    total, depth = len(pieces), n_cols // 2
    pass_feed = [(0, 1)]
    pass_chain = [(p, p + 2) for p in range(n_cols - 2)]
    pass_cross = [(p, p ^ 1) for p in range(2, n_cols)]
    pass_back = [(3, 1)]
    send = functools.partial(lax.ppermute, axis_name="pcol")
    feed, chain, cross, back = [], [], [], []
    for s in range(total + depth):
        if s < total + depth - 1:
            own = pieces[s][1] if s < total else pieces[0][1]
            if s == 0:
                entry = own
            else:
                entry = chain[s - 1]
                if s - 1 < total:
                    entry = jnp.where(col < 2, feed[s - 1], entry)
                if s < total:
                    entry = jnp.where(col == 0, own, entry)
        if s < total:
            feed.append(send(pieces[s][0], perm=pass_feed))
        if s >= 1:
            cross.append(send(chain[s - 1], perm=pass_cross))
        if s < total + depth - 1:
            chain.append(send(entry, perm=pass_chain))
        if 2 <= s < total + 2:
            back.append(send(cross[s - 2], perm=pass_back))
    return feed, chain, cross, back


def local(matrix, pivots, lower_inverse, upper_inverse, *, n_rows, n_cols, parts):
    row_dev, cols = matrix.shape
    nb = pivots.shape[0]
    f32 = jnp.float32
    row, col = lax.axis_index("prow"), lax.axis_index("pcol")
    here = jnp.stack([row, col]).astype(jnp.int32)

    table, owner = call(
        functools.partial(index_kernel, row_dev=row_dev),
        (jax.ShapeDtypeStruct((8, nb), jnp.int32), jax.ShapeDtypeStruct((nb, LANES), jnp.int32)),
        [SMEM, VMEM], (VMEM, VMEM),
    )(here, pivots.reshape(1, nb))

    slot = jax.ShapeDtypeStruct((nb, cols), f32)
    half_slot = jax.ShapeDtypeStruct((nb // 2, cols), f32)
    held = call(gather_kernel, slot, [SMEM, VMEM], VMEM)(table, matrix)
    displaced = held
    log = 0
    half = None
    while (1 << log) < n_rows:
        d = 1 << log
        far = [(p, p ^ d) for p in range(n_rows)]
        if log == 0:
            arrived = [lax.ppermute(held, "prow", far)]
            whole = arrived[0]
        else:
            near = [(p, p ^ 1) for p in range(n_rows)]
            one = lax.ppermute(half, "prow", far)
            two = lax.ppermute(one, "prow", near)
            arrived = [one, two]
            whole = jnp.concatenate(
                [jnp.where(row % 2 == 0, one, two), jnp.where(row % 2 == 0, two, one)], axis=0
            )
        held, half = call(
            functools.partial(merge_kernel, log=log, halves=log > 0),
            (slot, half_slot), [SMEM] + [VMEM] * (2 + len(arrived)), (VMEM, VMEM),
        )(here, owner, held, *arrived)
        displaced = jnp.where((row >> log) == 1, whole, displaced)
        log += 1

    weights, top = call(
        factor_kernel, (slot, slot), [SMEM, VMEM, VMEM, VMEM], (VMEM, VMEM),
        flops=4 * nb * nb * cols * 6,
    )(here, held, lower_inverse, upper_inverse)

    chunk = row_dev // (2 * parts)
    extra = nb // (2 * chunk)
    pieces = []
    for i in range(parts + extra):
        source, at = (matrix, i) if i < parts else (displaced, i - parts)
        pieces.append(tuple(
            lax.slice(source, ((2 * at + h) * chunk, 0), ((2 * at + h + 1) * chunk, nb))
            for h in range(2)
        ))
    sent = spread(pieces, col, n_cols)
    counts = tuple(len(group) for group in sent)
    bufs = [b for group in sent for b in group]
    choice = jnp.asarray(choice_table(n_cols, counts), jnp.int32)[col]

    block = 256
    return call(
        functools.partial(
            final_kernel, counts=counts, chunk=chunk, extra=extra, block=block
        ),
        jax.ShapeDtypeStruct(matrix.shape, f32),
        [SMEM, SMEM, SMEM, VMEM, VMEM, VMEM, ANY] + [ANY] * len(bufs),
        ANY,
        [
            pltpu.VMEM((row_dev, cols), f32),
            pltpu.VMEM((row_dev, nb), f32),
            pltpu.VMEM((nb, nb), f32),
            pltpu.VMEM((nb, cols), jnp.bfloat16),
            pltpu.VMEM((nb, cols), jnp.bfloat16),
            pltpu.VMEM((row_dev, cols), f32),
            pltpu.SemaphoreType.DMA,
            pltpu.SemaphoreType.DMA,
            pltpu.SemaphoreType.DMA,
        ],
        flops=2 * row_dev * nb * cols * 3,
        moved=4 * row_dev * (2 * cols + nb),
    )(here, table, choice, displaced, weights, top, matrix, *bufs)


def solution(mesh):
    n_rows, n_cols = mesh.shape["prow"], mesh.shape["pcol"]
    return jax.shard_map(
        functools.partial(local, n_rows=n_rows, n_cols=n_cols, parts=8),
        mesh=mesh,
        in_specs=(P("prow", "pcol"), P(), P(), P()),
        out_specs=P("prow", "pcol"),
        check_vma=False,
    )
```

```python
import functools

import jax
import jax.numpy as jnp
from jax import lax
from jax.experimental import pallas as pl
from jax.experimental.pallas import tpu as pltpu
from jax.sharding import PartitionSpec as P

HIGHEST = lax.Precision.HIGHEST
VMEM = pl.BlockSpec(memory_space=pltpu.VMEM)
SMEM = pl.BlockSpec(memory_space=pltpu.SMEM)
ANY = pl.BlockSpec(memory_space=pl.ANY)
LANES = 128
PICK, FROM, ROW, COUNT = 0, 1, 2, 3


def call(kernel, out, ins, outs, scratch=(), vmem=40 << 20, flops=0, moved=0):
    return pl.pallas_call(
        kernel,
        out_shape=out,
        in_specs=ins,
        out_specs=outs,
        scratch_shapes=list(scratch),
        compiler_params=pltpu.CompilerParams(vmem_limit_bytes=vmem),
        cost_estimate=pl.CostEstimate(
            flops=flops, bytes_accessed=moved, transcendentals=0
        ),
    )


def index_kernel(where_ref, pivots_ref, table_ref, owner_ref, *, row_dev):
    nb = pivots_ref.shape[1]
    start = where_ref[0] * row_dev
    first = where_ref[0] == 0
    down = lax.broadcasted_iota(jnp.int32, (nb, nb), 0)
    across = lax.broadcasted_iota(jnp.int32, (nb, nb), 1)
    piv_row = jnp.broadcast_to(pivots_ref[...], (nb, nb))

    def column(full):
        return jnp.sum(jnp.where(down == across, full, 0.0), axis=1, keepdims=True)

    piv_f = piv_row.astype(jnp.float32)
    piv_col = jnp.broadcast_to(column(piv_f), (nb, nb))
    upto = (down <= across).astype(jnp.bfloat16)
    below = (piv_row >= nb).astype(jnp.float32)
    vacancy = jnp.dot(
        below[:8].astype(jnp.bfloat16), upto, preferred_element_type=jnp.float32
    )[:1]
    taken = jnp.max((piv_row == down).astype(jnp.float32), axis=1, keepdims=True)
    freed = jnp.broadcast_to(1.0 - taken, (nb, LANES))
    rank = jnp.dot(
        (across <= down).astype(jnp.bfloat16),
        freed.astype(jnp.bfloat16),
        preferred_element_type=jnp.float32,
    )[:, :1]
    down_f = down.astype(jnp.float32)
    pair = (rank == vacancy) & (freed[:, :1] > 0.5)
    source = jnp.sum(jnp.where(pair, down_f, 0.0), axis=0, keepdims=True)
    source_col = jnp.broadcast_to(column(jnp.broadcast_to(source, (nb, nb))), (nb, nb))

    own_row = (pivots_ref[...] >= start) & (pivots_ref[...] < start + row_dev)
    pick = jnp.where(own_row, pivots_ref[...] - start, source.astype(jnp.int32))
    moved_row = (own_row & (pivots_ref[...] >= nb)).astype(jnp.float32)
    start_f = start.astype(jnp.float32)
    moved_col = (
        (piv_col >= start_f) & (piv_col < start_f + row_dev) & (piv_col >= nb)
    )
    order = jnp.sum(
        jnp.where(piv_f < piv_col, jnp.broadcast_to(moved_row, (nb, nb)), 0.0),
        axis=1,
        keepdims=True,
    )
    placed = moved_col & (order == across.astype(jnp.float32))
    origin = jnp.where(first, source_col, down_f)
    listed_from = jnp.sum(jnp.where(placed, origin, 0.0), axis=0, keepdims=True)
    listed_row = jnp.sum(
        jnp.where(placed, piv_col - start_f, 0.0), axis=0, keepdims=True
    )
    count = jnp.sum(moved_row, axis=1, keepdims=True)
    table_ref[...] = jnp.zeros_like(table_ref)
    table_ref[PICK : PICK + 1, :] = pick
    table_ref[FROM : FROM + 1, :] = listed_from.astype(jnp.int32)
    table_ref[ROW : ROW + 1, :] = listed_row.astype(jnp.int32)
    table_ref[COUNT : COUNT + 1, :] = jnp.broadcast_to(
        count.astype(jnp.int32), (1, nb)
    )
    owner_ref[...] = piv_col[:, :LANES].astype(jnp.int32) // row_dev


def gather_kernel(table_ref, matrix_ref, out_ref):
    nb = out_ref.shape[0]

    @pl.loop(0, nb, step=8)
    def _(base):
        for k in range(8):
            j = base + k
            out_ref[pl.ds(j, 1), :] = matrix_ref[pl.ds(table_ref[PICK, j], 1), :]


def merge_kernel(where_ref, owner_ref, held_ref, *refs, log, halves):
    arrived, (merged_ref, half_ref) = refs[: 2 if halves else 1], refs[-2:]
    me = where_ref[0]
    mine, theirs = me >> log, (me >> log) ^ 1
    odd = me & 1
    nb, cols = held_ref.shape
    half = nb // 2

    def merge(rows, piece):
        group = owner_ref[rows, :] >> log
        take = (group == theirs) | ((theirs == 0) & (group != mine))
        for q in range(cols // LANES):
            lane = slice(q * LANES, (q + 1) * LANES)
            merged_ref[rows, lane] = jnp.where(take, piece[:, lane], held_ref[rows, lane])

    low, high = slice(0, half), slice(half, nb)
    if halves:
        @pl.when(odd == 0)
        def _():
            merge(low, arrived[0])
            merge(high, arrived[1])

        @pl.when(odd == 1)
        def _():
            merge(low, arrived[1])
            merge(high, arrived[0])
    else:
        merge(slice(0, nb), arrived[0])

    @pl.when(odd == 0)
    def _():
        half_ref[...] = merged_ref[low, :]

    @pl.when(odd == 1)
    def _():
        half_ref[...] = merged_ref[high, :]


def factor_kernel(where_ref, top_in_ref, lower_ref, upper_ref, weights_ref, top_ref):
    nb, cols = top_in_ref.shape
    u = jnp.dot(
        lower_ref[...], top_in_ref[...], precision=HIGHEST,
        preferred_element_type=jnp.float32,
    )
    top_ref[...] = u
    weights_ref[...] = jnp.dot(
        upper_ref[...], u, precision=HIGHEST, preferred_element_type=jnp.float32
    )

    @pl.when(where_ref[1] == 0)
    def _():
        top_ref[:, :nb] = top_in_ref[:, :nb]
        weights_ref[:, :nb] = -upper_ref[...]


def swap_kernel(where_ref, table_ref, displaced_ref, matrix_ref, swapped_ref, *pieces):
    nb = pieces[0].shape[1]
    size = pieces[0].shape[0]
    swapped_ref[...] = matrix_ref[...]

    def swap(origin):
        def body(k, _):
            to, at = table_ref[ROW, k], table_ref[FROM, k]
            swapped_ref[pl.ds(to, 1), :] = origin[pl.ds(at, 1), :]
            return 0

        lax.fori_loop(0, table_ref[COUNT, 0], body, 0)

    @pl.when(where_ref[0] == 0)
    def _():
        swap(matrix_ref)

    @pl.when(where_ref[0] > 0)
    def _():
        swap(displaced_ref)

    @pl.when(where_ref[1] == 0)
    def _():
        for p, piece in enumerate(pieces):
            piece[...] = swapped_ref[p * size : (p + 1) * size, :nb]


def pick_kernel(where_ref, *refs):
    options, out_ref, sem = refs[:-2], refs[-2], refs[-1]
    for p, option in enumerate(options):
        @pl.when(where_ref[1] == p)
        def _():
            copy = pltpu.make_async_copy(option, out_ref, sem)
            copy.start()
            copy.wait()


def final_kernel(where_ref, weights_ref, top_ref, swapped_ref, panel_ref, out_ref, w_hi, w_lo):
    nb = weights_ref.shape[0]
    block, cols = out_ref.shape
    step = pl.program_id(0)
    on_top = (where_ref[0] == 0) & ((step + 1) * block <= nb)

    @pl.when(step == 0)
    def _():
        w = weights_ref[...]
        hi = w.astype(jnp.bfloat16)
        w_hi[...] = hi
        w_lo[...] = (w - hi.astype(jnp.float32)).astype(jnp.bfloat16)

    @pl.when(on_top)
    def _():
        out_ref[...] = top_ref[pl.ds(pl.multiple_of(step * block, block), block), :]

    @pl.when(jnp.logical_not(on_top))
    def _():
        p = panel_ref[...]
        p_hi = p.astype(jnp.bfloat16)
        p_lo = (p - p_hi.astype(jnp.float32)).astype(jnp.bfloat16)
        dot = functools.partial(jnp.dot, preferred_element_type=jnp.float32)
        total = dot(p_lo, w_hi[...]) + dot(p_hi, w_lo[...]) + dot(p_hi, w_hi[...])
        keep = where_ref[1] > 0
        out_ref[:, :nb] = jnp.where(keep, swapped_ref[:, :nb], 0.0) - total[:, :nb]
        out_ref[:, nb:] = swapped_ref[:, nb:] - total[:, nb:]


def local(matrix, pivots, lower_inverse, upper_inverse, *, n_rows, n_cols):
    row_dev, cols = matrix.shape
    nb = pivots.shape[0]
    f32 = jnp.float32
    row, col = lax.axis_index("prow"), lax.axis_index("pcol")
    here = jnp.stack([row, col]).astype(jnp.int32)

    table, owner = call(
        functools.partial(index_kernel, row_dev=row_dev),
        (jax.ShapeDtypeStruct((8, nb), jnp.int32), jax.ShapeDtypeStruct((nb, LANES), jnp.int32)),
        [SMEM, VMEM], (VMEM, VMEM),
    )(here, pivots.reshape(1, nb))

    slot = jax.ShapeDtypeStruct((nb, cols), f32)
    half_slot = jax.ShapeDtypeStruct((nb // 2, cols), f32)
    held = call(gather_kernel, slot, [SMEM, VMEM], VMEM)(table, matrix)
    displaced = held
    log = 0
    half = None
    while (1 << log) < n_rows:
        d = 1 << log
        far = [(p, p ^ d) for p in range(n_rows)]
        if log == 0:
            arrived = [lax.ppermute(held, "prow", far)]
            whole = arrived[0]
        else:
            near = [(p, p ^ 1) for p in range(n_rows)]
            one = lax.ppermute(half, "prow", far)
            two = lax.ppermute(one, "prow", near)
            arrived = [one, two]
            whole = jnp.concatenate(
                [jnp.where(row % 2 == 0, one, two), jnp.where(row % 2 == 0, two, one)], axis=0
            )
        held, half = call(
            functools.partial(merge_kernel, log=log, halves=log > 0),
            (slot, half_slot), [SMEM] + [VMEM] * (2 + len(arrived)), (VMEM, VMEM),
        )(here, owner, held, *arrived)
        displaced = jnp.where((row >> log) == 1, whole, displaced)
        log += 1

    weights, top = call(
        factor_kernel, (slot, slot), [SMEM, VMEM, VMEM, VMEM], (VMEM, VMEM),
        flops=4 * nb * nb * cols * 6,
    )(here, held, lower_inverse, upper_inverse)

    size = row_dev // n_cols
    piece = jax.ShapeDtypeStruct((size, nb), f32)
    swapped, *pieces = call(
        swap_kernel, (jax.ShapeDtypeStruct(matrix.shape, f32),) + (piece,) * n_cols,
        [SMEM, SMEM, VMEM, VMEM], (VMEM,) * (1 + n_cols),
    )(here, table, displaced, matrix)
    parts = [pieces[0]] + [
        lax.ppermute(pieces[p], "pcol", [(0, p)]) for p in range(1, n_cols)
    ]
    mine = call(
        pick_kernel, piece, [SMEM] + [ANY] * n_cols, ANY, [pltpu.SemaphoreType.DMA]
    )(here, *parts)
    panel = lax.all_gather(mine, "pcol", axis=0, tiled=True)

    block = 256
    whole = pl.BlockSpec((nb, cols), lambda i: (0, 0))
    wide = pl.BlockSpec((block, cols), lambda i: (i, 0))
    return pl.pallas_call(
        final_kernel,
        grid=(row_dev // block,),
        out_shape=jax.ShapeDtypeStruct(matrix.shape, f32),
        in_specs=[SMEM, whole, whole, wide, pl.BlockSpec((block, nb), lambda i: (i, 0))],
        out_specs=wide,
        scratch_shapes=[pltpu.VMEM((nb, cols), jnp.bfloat16)] * 2,
        compiler_params=pltpu.CompilerParams(vmem_limit_bytes=40 << 20),
        cost_estimate=pl.CostEstimate(
            flops=2 * row_dev * nb * cols * 3,
            bytes_accessed=4 * row_dev * (2 * cols + nb),
            transcendentals=0,
        ),
    )(here, weights, top, swapped, panel)


def solution(mesh):
    n_rows, n_cols = mesh.shape["prow"], mesh.shape["pcol"]
    return jax.shard_map(
        functools.partial(local, n_rows=n_rows, n_cols=n_cols),
        mesh=mesh,
        in_specs=(P("prow", "pcol"), P(), P(), P()),
        out_specs=P("prow", "pcol"),
        check_vma=False,
    )
```

```python
import functools

import jax
import jax.numpy as jnp
from jax import lax
from jax.experimental import pallas as pl
from jax.experimental.pallas import tpu as pltpu
from jax.sharding import PartitionSpec as P

HIGHEST = lax.Precision.HIGHEST
VMEM = pl.BlockSpec(memory_space=pltpu.VMEM)
SMEM = pl.BlockSpec(memory_space=pltpu.SMEM)
ANY = pl.BlockSpec(memory_space=pl.ANY)
LANES = 128
PICK, FROM, ROW, COUNT, TOP = 0, 1, 2, 3, 4


def call(kernel, out, ins, outs, scratch=(), vmem=16 << 20, flops=0, moved=0):
    return pl.pallas_call(
        kernel,
        out_shape=out,
        in_specs=ins,
        out_specs=outs,
        scratch_shapes=list(scratch),
        compiler_params=pltpu.CompilerParams(vmem_limit_bytes=vmem),
        cost_estimate=pl.CostEstimate(
            flops=flops, bytes_accessed=moved, transcendentals=0
        ),
    )


def index_kernel(where_ref, pivots_ref, table_ref, owner_ref, *, row_dev):
    nb = pivots_ref.shape[1]
    start = where_ref[0] * row_dev
    first = where_ref[0] == 0
    down = lax.broadcasted_iota(jnp.int32, (nb, nb), 0)
    across = lax.broadcasted_iota(jnp.int32, (nb, nb), 1)
    piv_row = jnp.broadcast_to(pivots_ref[...], (nb, nb))

    def column(full):
        return jnp.sum(jnp.where(down == across, full, 0.0), axis=1, keepdims=True)

    piv_f = piv_row.astype(jnp.float32)
    piv_col = jnp.broadcast_to(column(piv_f), (nb, nb))
    upto = (down <= across).astype(jnp.bfloat16)
    below = (piv_row >= nb).astype(jnp.float32)
    vacancy = jnp.dot(
        below[:8].astype(jnp.bfloat16), upto, preferred_element_type=jnp.float32
    )[:1]
    taken = jnp.max((piv_row == down).astype(jnp.float32), axis=1, keepdims=True)
    freed = jnp.broadcast_to(1.0 - taken, (nb, LANES))
    rank = jnp.dot(
        (across <= down).astype(jnp.bfloat16),
        freed.astype(jnp.bfloat16),
        preferred_element_type=jnp.float32,
    )[:, :1]
    down_f = down.astype(jnp.float32)
    pair = (rank == vacancy) & (freed[:, :1] > 0.5)
    source = jnp.sum(jnp.where(pair, down_f, 0.0), axis=0, keepdims=True)
    source_col = jnp.broadcast_to(column(jnp.broadcast_to(source, (nb, nb))), (nb, nb))

    own_row = (pivots_ref[...] >= start) & (pivots_ref[...] < start + row_dev)
    pick = jnp.where(own_row, pivots_ref[...] - start, source.astype(jnp.int32))
    moved_row = (own_row & (pivots_ref[...] >= nb)).astype(jnp.float32)
    start_f = start.astype(jnp.float32)
    moved_col = (
        (piv_col >= start_f) & (piv_col < start_f + row_dev) & (piv_col >= nb)
    )
    order = jnp.sum(
        jnp.where(piv_f < piv_col, jnp.broadcast_to(moved_row, (nb, nb)), 0.0),
        axis=1,
        keepdims=True,
    )
    placed = moved_col & (order == across.astype(jnp.float32))
    origin = jnp.where(first, source_col, down_f)
    listed_from = jnp.sum(jnp.where(placed, origin, 0.0), axis=0, keepdims=True)
    listed_row = jnp.sum(
        jnp.where(placed, piv_col - start_f, 0.0), axis=0, keepdims=True
    )
    listed_top = jnp.sum(jnp.where(placed, source_col, 0.0), axis=0, keepdims=True)
    count = jnp.sum(moved_row, axis=1, keepdims=True)
    table_ref[...] = jnp.zeros_like(table_ref)
    table_ref[PICK : PICK + 1, :] = pick
    table_ref[FROM : FROM + 1, :] = listed_from.astype(jnp.int32)
    table_ref[ROW : ROW + 1, :] = listed_row.astype(jnp.int32)
    table_ref[TOP : TOP + 1, :] = listed_top.astype(jnp.int32)
    table_ref[COUNT : COUNT + 1, :] = jnp.broadcast_to(
        count.astype(jnp.int32), (1, nb)
    )
    owner_ref[...] = piv_col[:, :LANES].astype(jnp.int32) // row_dev


def gather_kernel(table_ref, matrix_ref, out_ref):
    nb = out_ref.shape[0]

    @pl.loop(0, nb, step=8)
    def _(base):
        for k in range(8):
            j = base + k
            out_ref[pl.ds(j, 1), :] = matrix_ref[pl.ds(table_ref[PICK, j], 1), :]


def merge_kernel(where_ref, owner_ref, held_ref, *refs, log, halves):
    arrived, (merged_ref, half_ref) = refs[: 2 if halves else 1], refs[-2:]
    me = where_ref[0]
    mine, theirs = me >> log, (me >> log) ^ 1
    odd = me & 1
    nb, cols = held_ref.shape
    half = nb // 2

    def merge(rows, piece):
        group = owner_ref[rows, :] >> log
        take = (group == theirs) | ((theirs == 0) & (group != mine))
        for q in range(cols // LANES):
            lane = slice(q * LANES, (q + 1) * LANES)
            merged_ref[rows, lane] = jnp.where(take, piece[:, lane], held_ref[rows, lane])

    low, high = slice(0, half), slice(half, nb)
    if halves:
        @pl.when(odd == 0)
        def _():
            merge(low, arrived[0])
            merge(high, arrived[1])

        @pl.when(odd == 1)
        def _():
            merge(low, arrived[1])
            merge(high, arrived[0])
    else:
        merge(slice(0, nb), arrived[0])

    @pl.when(odd == 0)
    def _():
        half_ref[...] = merged_ref[low, :]

    @pl.when(odd == 1)
    def _():
        half_ref[...] = merged_ref[high, :]


def factor_kernel(where_ref, top_in_ref, lower_ref, upper_ref, weights_ref, top_ref):
    nb, cols = top_in_ref.shape
    u = jnp.dot(
        lower_ref[...], top_in_ref[...], precision=HIGHEST,
        preferred_element_type=jnp.float32,
    )
    top_ref[...] = u
    weights_ref[...] = jnp.dot(
        upper_ref[...], u, precision=HIGHEST, preferred_element_type=jnp.float32
    )

    @pl.when(where_ref[1] == 0)
    def _():
        top_ref[:, :nb] = top_in_ref[:, :nb]
        weights_ref[:, :nb] = -upper_ref[...]


def fetch(choice_ref, bufs, place, sem, n_cols, parts, pairs):
    for i in range(pairs):
        for h in range(2):
            for b in sorted({arrival(p, i, h, n_cols, parts) for p in range(1, n_cols)}):
                @pl.when(choice_ref[2 * i + h] == b)
                def _():
                    pltpu.make_async_copy(bufs[b], place(i, h), sem).start()


def old_top_kernel(where_ref, choice_ref, matrix_ref, *refs, used, n_cols, parts, pairs):
    bufs, top_ref, sem = dict(zip(used, refs)), refs[-2], refs[-1]
    nb = top_ref.shape[0]
    chunk = nb // (2 * pairs)
    from_matrix = pltpu.make_async_copy(
        matrix_ref.at[pl.ds(0, nb), pl.ds(0, nb)], top_ref, sem
    )

    @pl.when(where_ref[0] == 0)
    def _():
        @pl.when(where_ref[1] == 0)
        def _():
            from_matrix.start()

        @pl.when(where_ref[1] > 0)
        def _():
            fetch(
                choice_ref, bufs,
                lambda i, h: top_ref.at[pl.ds((2 * i + h) * chunk, chunk), :],
                sem, n_cols, parts, pairs,
            )

        from_matrix.wait()


def final_kernel(
    where_ref, table_ref, choice_ref, displaced_ref, weights_ref, top_ref, matrix_ref,
    *refs, n_bufs, n_tops, n_cols, parts, block,
):
    bufs, tops, out_ref = refs[:n_bufs], refs[n_bufs : n_bufs + n_tops], refs[n_bufs + n_tops]
    mat, pan, low, w_hi, w_lo, result, in_sem, low_sem, mat_sem, out_sem = refs[
        n_bufs + n_tops + 1 :
    ]
    rows, cols = matrix_ref.shape
    nb = weights_ref.shape[0]
    half = nb // 2
    chunk = rows // (2 * parts)
    row = where_ref[0]
    first_row, first_col = row == 0, where_ref[1] == 0

    load = pltpu.make_async_copy(matrix_ref, mat, mat_sem)
    load.start()
    whole_panel = pltpu.make_async_copy(matrix_ref.at[:, pl.ds(0, nb)], pan, in_sem)

    @pl.when(first_col)
    def _():
        whole_panel.start()

    @pl.when(jnp.logical_not(first_col))
    def _():
        fetch(
            choice_ref, bufs, lambda i, h: pan.at[pl.ds((2 * i + h) * chunk, chunk), :],
            in_sem, n_cols, parts, parts,
        )

    @pl.when(row == 1)
    def _():
        pltpu.make_async_copy(tops[0], low, low_sem).start()

    for log in range(1, (n_tops + 1) // 2):
        for odd in range(2):
            @pl.when(((row >> log) == 1) & ((row & 1) == odd))
            def _():
                for part, ref in enumerate(tops[2 * log - 1 : 2 * log + 1]):
                    at = half * (part ^ odd)
                    pltpu.make_async_copy(ref, low.at[pl.ds(at, half), :], low_sem).start()

    w = weights_ref[...]
    w_hi[...] = w.astype(jnp.bfloat16)
    w_lo[...] = (w - w_hi[...].astype(jnp.float32)).astype(jnp.bfloat16)

    whole_panel.wait()
    load.wait()
    count = table_ref[COUNT, 0]

    def swap(from_mat, from_pan):
        def body(k, _):
            to = table_ref[ROW, k]
            mat[pl.ds(to, 1), :] = from_mat[pl.ds(table_ref[FROM, k], 1), :]
            pan[pl.ds(to, 1), :] = from_pan[pl.ds(table_ref[TOP, k], 1), :]
            return 0

        lax.fori_loop(0, count, body, 0)

    @pl.when(first_row)
    def _():
        swap(mat, pan)

    @pl.when(jnp.logical_not(first_row))
    def _():
        pltpu.make_async_copy(tops[0], low, low_sem).wait()
        swap(displaced_ref, low)

    @pl.when(first_col)
    def _():
        mat[:, :nb] = jnp.zeros((rows, nb), jnp.float32)

    copies = []
    for b in range(rows // block):
        span = pl.ds(b * block, block)

        def update():
            p = pan[span, :]
            p_hi = p.astype(jnp.bfloat16)
            p_lo = (p - p_hi.astype(jnp.float32)).astype(jnp.bfloat16)
            dot = functools.partial(jnp.dot, preferred_element_type=jnp.float32)
            total = dot(p_lo, w_hi[...]) + dot(p_hi, w_lo[...]) + dot(p_hi, w_hi[...])
            result[span, :] = mat[span, :] - total

        if (b + 1) * block <= nb:
            pl.when(jnp.logical_not(first_row))(update)

            @pl.when(first_row)
            def _():
                result[span, :] = top_ref[span, :]
        else:
            update()
        copy = pltpu.make_async_copy(result.at[span, :], out_ref.at[span, :], out_sem)
        copy.start()
        copies.append(copy)
    for copy in copies:
        copy.wait()


LAG = 2


def steps(n_cols, parts):
    depth = n_cols // 2
    return parts + LAG * (depth - 1), max(2 * parts, parts + LAG * depth)


def arrival(p, i, h, n_cols, parts):
    z, y = divmod(p, 2)
    cross = steps(n_cols, parts)[0]
    if z == 0:
        return cross + i + h * parts
    if y == 0:
        return cross + i + LAG * (z + 1) if h == 0 else i + LAG * (z - 1)
    return i + LAG * z if h == 0 else cross + i + LAG * z


def spread(pieces, col, n_cols, riders):
    parts = len(pieces)
    n_chain, n_cross = steps(n_cols, parts)
    along = [(p, p + 2) for p in range(n_cols - 2)]
    across = [(0, 1)] + [(p, p ^ 1) for p in range(2, n_cols)]
    chain, cross = [], []
    waiting = [(rider, next(rider)(chain, cross)) for rider in riders]
    for s in range(n_cross):
        ahead = pieces[min(s, parts - 1)][1]
        aside = pieces[s][0] if s < parts else pieces[min(s - parts, parts - 1)][1]
        if s >= LAG:
            came = chain[s - LAG] if s - LAG < n_chain else chain[-1]
            due = [k for k, (_, (at, _)) in enumerate(waiting) if at == s]
            tied = [waiting[k][1][1] for k in due]
            (came, fed), tied = lax.optimization_barrier(((came, cross[s - LAG]), tied))
            ahead = jnp.where(col == 0, ahead, jnp.where(col == 1, fed, came))
            aside = jnp.where(col == 0, aside, came)
        if s < n_chain:
            chain.append(lax.ppermute(ahead, "pcol", along))
        cross.append(lax.ppermute(aside, "pcol", across))
        if s >= LAG:
            for k, values in zip(due, tied):
                rider = waiting[k][0]
                waiting[k] = (rider, resume(rider, values, chain, cross))
    results = []
    for rider, (at, values) in waiting:
        while at != DONE:
            at, values = resume(rider, values, chain, cross)
        results.append(values)
    return chain, cross, results


DONE = -1


def resume(rider, values, chain, cross):
    return rider.send(values)(chain, cross)


def give(at, values):
    return lambda chain, cross: (at, values)


def local(matrix, pivots, lower_inverse, upper_inverse, *, n_rows, n_cols, parts):
    row_dev, cols = matrix.shape
    nb = pivots.shape[0]
    f32 = jnp.float32
    row, col = lax.axis_index("prow"), lax.axis_index("pcol")
    here = jnp.stack([row, col]).astype(jnp.int32)
    odd = row % 2 == 1

    chunk = row_dev // (2 * parts)
    flat = [
        lax.slice(matrix, (k * chunk, 0), ((k + 1) * chunk, nb)) for k in range(2 * parts)
    ]
    flat = flat[:2] + list(lax.optimization_barrier(tuple(flat[2:])))
    choice = jnp.asarray(
        [
            [0] * (2 * parts) if p == 0 else
            [arrival(p, i, h, n_cols, parts) for i in range(parts) for h in range(2)]
            for p in range(n_cols)
        ],
        jnp.int32,
    )[col]

    pairs = nb // (2 * chunk)
    used = sorted({
        arrival(p, i, h, n_cols, parts)
        for p in range(1, n_cols) for i in range(pairs) for h in range(2)
    })
    n_chain = steps(n_cols, parts)[0]
    last = max(b - n_chain if b >= n_chain else b for b in used)

    def both_halves(one, two):
        return jnp.concatenate([jnp.where(odd, two, one), jnp.where(odd, one, two)], axis=0)

    def old_top_rider():
        at = last + LAG

        def start(chain, cross):
            return at, [chain[b] if b < n_chain else cross[b - n_chain] for b in used]

        arrived = yield give(at - 1, ())
        arrived = yield start
        old_top = call(
            functools.partial(
                old_top_kernel, used=used, n_cols=n_cols, parts=parts, pairs=pairs
            ),
            jax.ShapeDtypeStruct((nb, nb), f32),
            [SMEM, SMEM, ANY] + [ANY] * len(used), ANY, [pltpu.SemaphoreType.DMA],
            vmem=4 << 20,
        )(here, choice, matrix, *arrived)
        tops = []
        log = 0
        while (1 << log) < n_rows:
            d = 1 << log
            far = [(p, p + d) for p in range(d)]
            if log == 0:
                at += 2
                whole = yield give(at, lax.ppermute(old_top, "prow", far))
                tops.append(whole)
            else:
                half = jnp.where(odd, old_top[nb // 2 :], old_top[: nb // 2])
                at += 3
                one = yield give(at, lax.ppermute(half, "prow", far))
                two = lax.ppermute(one, "prow", [(p, p ^ 1) for p in range(d, 2 * d)])
                tops += [one, two]
                whole = both_halves(one, two)
            old_top = jnp.where((row >> log) == 1, whole, old_top)
            log += 1
        yield give(DONE, tops)

    slot = jax.ShapeDtypeStruct((nb, cols), f32)
    half_slot = jax.ShapeDtypeStruct((nb // 2, cols), f32)

    def exchange_rider():
        table, owner = yield give(2, call(
            functools.partial(index_kernel, row_dev=row_dev),
            (jax.ShapeDtypeStruct((8, nb), jnp.int32), jax.ShapeDtypeStruct((nb, LANES), jnp.int32)),
            [SMEM, VMEM], (VMEM, VMEM),
        )(here, pivots.reshape(1, nb)))
        held = yield give(3, call(gather_kernel, slot, [SMEM, VMEM], VMEM)(table, matrix))
        at = 5
        displaced = held
        log = 0
        half = None
        while (1 << log) < n_rows:
            d = 1 << log
            far = [(p, p ^ d) for p in range(n_rows)]
            if log == 0:
                whole = yield give(at, lax.ppermute(held, "prow", far))
                arrived = [whole]
            else:
                near = [(p, p ^ 1) for p in range(n_rows)]
                one = yield give(at + 4, lax.ppermute(half, "prow", far))
                at += 5
                two = yield give(at, lax.ppermute(one, "prow", near))
                arrived = [one, two]
                whole = both_halves(one, two)
            held, half = call(
                functools.partial(merge_kernel, log=log, halves=log > 0),
                (slot, half_slot), [SMEM] + [VMEM] * (2 + len(arrived)), (VMEM, VMEM),
            )(here, owner, held, *arrived)
            displaced = jnp.where((row >> log) == 1, whole, displaced)
            log += 1
        held, displaced = yield give(at + 1, (held, displaced))
        weights, top = yield give(at + 2, call(
            factor_kernel, (slot, slot), [SMEM, VMEM, VMEM, VMEM], (VMEM, VMEM),
            flops=4 * nb * nb * cols * 6,
        )(here, held, lower_inverse, upper_inverse))
        yield give(DONE, (table, displaced, weights, top))

    chain, cross, (tops, (table, displaced, weights, top)) = spread(
        [(flat[2 * i], flat[2 * i + 1]) for i in range(parts)], col, n_cols,
        [old_top_rider(), exchange_rider()],
    )
    bufs = chain + cross

    return call(
        functools.partial(
            final_kernel, n_bufs=len(bufs), n_tops=len(tops), n_cols=n_cols, parts=parts,
            block=256,
        ),
        jax.ShapeDtypeStruct(matrix.shape, f32),
        [SMEM, SMEM, SMEM, VMEM, VMEM, VMEM, ANY] + [ANY] * (len(bufs) + len(tops)),
        ANY,
        [
            pltpu.VMEM((row_dev, cols), f32),
            pltpu.VMEM((row_dev, nb), f32),
            pltpu.VMEM((nb, nb), f32),
            pltpu.VMEM((nb, cols), jnp.bfloat16),
            pltpu.VMEM((nb, cols), jnp.bfloat16),
            pltpu.VMEM((row_dev, cols), f32),
        ] + [pltpu.SemaphoreType.DMA] * 4,
        vmem=30 << 20,
        flops=2 * row_dev * nb * cols * 3,
        moved=4 * row_dev * (2 * cols + nb),
    )(here, table, choice, displaced, weights, top, matrix, *bufs, *tops)


def solution(mesh):
    n_rows, n_cols = mesh.shape["prow"], mesh.shape["pcol"]
    return jax.shard_map(
        functools.partial(local, n_rows=n_rows, n_cols=n_cols, parts=8),
        mesh=mesh,
        in_specs=(P("prow", "pcol"), P(), P(), P()),
        out_specs=P("prow", "pcol"),
        check_vma=False,
    )
```

```python
import functools

import jax
import jax.numpy as jnp
from jax import lax
from jax.experimental import pallas as pl
from jax.experimental.pallas import tpu as pltpu
from jax.sharding import PartitionSpec as P

HIGHEST = lax.Precision.HIGHEST
VMEM = pl.BlockSpec(memory_space=pltpu.VMEM)
SMEM = pl.BlockSpec(memory_space=pltpu.SMEM)
ANY = pl.BlockSpec(memory_space=pl.ANY)
LANES = 128
PICK, FROM, ROW, COUNT, TOP = 0, 1, 2, 3, 4


def call(kernel, out, ins, outs, scratch=(), vmem=16 << 20, flops=0, moved=0):
    return pl.pallas_call(
        kernel,
        out_shape=out,
        in_specs=ins,
        out_specs=outs,
        scratch_shapes=list(scratch),
        compiler_params=pltpu.CompilerParams(vmem_limit_bytes=vmem),
        cost_estimate=pl.CostEstimate(
            flops=flops, bytes_accessed=moved, transcendentals=0
        ),
    )


def index_kernel(where_ref, pivots_ref, table_ref, owner_ref, *, row_dev):
    nb = pivots_ref.shape[1]
    start = where_ref[0] * row_dev
    first = where_ref[0] == 0
    down = lax.broadcasted_iota(jnp.int32, (nb, nb), 0)
    across = lax.broadcasted_iota(jnp.int32, (nb, nb), 1)
    piv_row = jnp.broadcast_to(pivots_ref[...], (nb, nb))

    def column(full):
        return jnp.sum(jnp.where(down == across, full, 0.0), axis=1, keepdims=True)

    piv_f = piv_row.astype(jnp.float32)
    piv_col = jnp.broadcast_to(column(piv_f), (nb, nb))
    upto = (down <= across).astype(jnp.bfloat16)
    below = (piv_row >= nb).astype(jnp.float32)
    vacancy = jnp.dot(
        below[:8].astype(jnp.bfloat16), upto, preferred_element_type=jnp.float32
    )[:1]
    taken = jnp.max((piv_row == down).astype(jnp.float32), axis=1, keepdims=True)
    freed = jnp.broadcast_to(1.0 - taken, (nb, LANES))
    rank = jnp.dot(
        (across <= down).astype(jnp.bfloat16),
        freed.astype(jnp.bfloat16),
        preferred_element_type=jnp.float32,
    )[:, :1]
    down_f = down.astype(jnp.float32)
    pair = (rank == vacancy) & (freed[:, :1] > 0.5)
    source = jnp.sum(jnp.where(pair, down_f, 0.0), axis=0, keepdims=True)
    source_col = jnp.broadcast_to(column(jnp.broadcast_to(source, (nb, nb))), (nb, nb))

    own_row = (pivots_ref[...] >= start) & (pivots_ref[...] < start + row_dev)
    pick = jnp.where(own_row, pivots_ref[...] - start, source.astype(jnp.int32))
    moved_row = (own_row & (pivots_ref[...] >= nb)).astype(jnp.float32)
    start_f = start.astype(jnp.float32)
    moved_col = (
        (piv_col >= start_f) & (piv_col < start_f + row_dev) & (piv_col >= nb)
    )
    order = jnp.sum(
        jnp.where(piv_f < piv_col, jnp.broadcast_to(moved_row, (nb, nb)), 0.0),
        axis=1,
        keepdims=True,
    )
    placed = moved_col & (order == across.astype(jnp.float32))
    origin = jnp.where(first, source_col, down_f)
    listed_from = jnp.sum(jnp.where(placed, origin, 0.0), axis=0, keepdims=True)
    listed_row = jnp.sum(
        jnp.where(placed, piv_col - start_f, 0.0), axis=0, keepdims=True
    )
    listed_top = jnp.sum(jnp.where(placed, source_col, 0.0), axis=0, keepdims=True)
    count = jnp.sum(moved_row, axis=1, keepdims=True)
    table_ref[...] = jnp.zeros_like(table_ref)
    table_ref[PICK : PICK + 1, :] = pick
    table_ref[FROM : FROM + 1, :] = listed_from.astype(jnp.int32)
    table_ref[ROW : ROW + 1, :] = listed_row.astype(jnp.int32)
    table_ref[TOP : TOP + 1, :] = listed_top.astype(jnp.int32)
    table_ref[COUNT : COUNT + 1, :] = jnp.broadcast_to(
        count.astype(jnp.int32), (1, nb)
    )
    owner_ref[...] = piv_col[:, :LANES].astype(jnp.int32) // row_dev


def gather_kernel(table_ref, matrix_ref, out_ref):
    nb = out_ref.shape[0]

    @pl.loop(0, nb, step=8)
    def _(base):
        for k in range(8):
            j = base + k
            out_ref[pl.ds(j, 1), :] = matrix_ref[pl.ds(table_ref[PICK, j], 1), :]


def merge_kernel(where_ref, owner_ref, held_ref, *refs, log, halves):
    arrived, (merged_ref, half_ref) = refs[: 2 if halves else 1], refs[-2:]
    me = where_ref[0]
    mine, theirs = me >> log, (me >> log) ^ 1
    odd = me & 1
    nb, cols = held_ref.shape
    half = nb // 2

    def merge(rows, piece):
        group = owner_ref[rows, :] >> log
        take = (group == theirs) | ((theirs == 0) & (group != mine))
        for q in range(cols // LANES):
            lane = slice(q * LANES, (q + 1) * LANES)
            merged_ref[rows, lane] = jnp.where(take, piece[:, lane], held_ref[rows, lane])

    low, high = slice(0, half), slice(half, nb)
    if halves:
        @pl.when(odd == 0)
        def _():
            merge(low, arrived[0])
            merge(high, arrived[1])

        @pl.when(odd == 1)
        def _():
            merge(low, arrived[1])
            merge(high, arrived[0])
    else:
        merge(slice(0, nb), arrived[0])

    @pl.when(odd == 0)
    def _():
        half_ref[...] = merged_ref[low, :]

    @pl.when(odd == 1)
    def _():
        half_ref[...] = merged_ref[high, :]


def factor_kernel(where_ref, top_in_ref, lower_ref, upper_ref, weights_ref, top_ref):
    nb, cols = top_in_ref.shape
    u = jnp.dot(
        lower_ref[...], top_in_ref[...], precision=HIGHEST,
        preferred_element_type=jnp.float32,
    )
    top_ref[...] = u
    weights_ref[...] = jnp.dot(
        upper_ref[...], u, precision=HIGHEST, preferred_element_type=jnp.float32
    )

    @pl.when(where_ref[1] == 0)
    def _():
        top_ref[:, :nb] = top_in_ref[:, :nb]
        weights_ref[:, :nb] = -upper_ref[...]


def old_top_kernel(where_ref, matrix_ref, near_ref, far_ref, top_ref, sem):
    nb = top_ref.shape[0]
    from_matrix = pltpu.make_async_copy(
        matrix_ref.at[pl.ds(0, nb), pl.ds(0, nb)], top_ref, sem
    )

    @pl.when(where_ref[0] == 0)
    def _():
        fetch_panel(where_ref, matrix_ref, [near_ref, far_ref], top_ref, sem)
        from_matrix.wait()


def fetch_panel(where_ref, matrix_ref, bufs, out_ref, sem):
    rows, nb = out_ref.shape
    half = rows // len(bufs)
    col = where_ref[1]

    @pl.when(col == 0)
    def _():
        pltpu.make_async_copy(
            matrix_ref.at[pl.ds(0, rows), pl.ds(0, nb)], out_ref, sem
        ).start()

    for y in range(2):
        @pl.when((col > 0) & ((col & 1) == y))
        def _():
            for k, buf in enumerate(bufs):
                at = half * (k if y else k ^ 1)
                pltpu.make_async_copy(buf, out_ref.at[pl.ds(at, half), :], sem).start()


def final_kernel(
    where_ref, table_ref, displaced_ref, weights_ref, top_ref, matrix_ref,
    *refs, n_bufs, n_tops, block,
):
    bufs, tops, out_ref = refs[:n_bufs], refs[n_bufs : n_bufs + n_tops], refs[n_bufs + n_tops]
    mat, pan, low, w_hi, w_lo, result, in_sem, low_sem, mat_sem, out_sem = refs[
        n_bufs + n_tops + 1 :
    ]
    rows, cols = matrix_ref.shape
    nb = weights_ref.shape[0]
    half = nb // 2
    row = where_ref[0]
    first_row, first_col = row == 0, where_ref[1] == 0

    load = pltpu.make_async_copy(matrix_ref, mat, mat_sem)
    load.start()
    whole_panel = pltpu.make_async_copy(matrix_ref.at[:, pl.ds(0, nb)], pan, in_sem)

    fetch_panel(where_ref, matrix_ref, bufs, pan, in_sem)

    @pl.when(row == 1)
    def _():
        pltpu.make_async_copy(tops[0], low, low_sem).start()

    for log in range(1, (n_tops + 1) // 2):
        for odd in range(2):
            @pl.when(((row >> log) == 1) & ((row & 1) == odd))
            def _():
                for part, ref in enumerate(tops[2 * log - 1 : 2 * log + 1]):
                    at = half * (part ^ odd)
                    pltpu.make_async_copy(ref, low.at[pl.ds(at, half), :], low_sem).start()

    w = weights_ref[...]
    w_hi[...] = w.astype(jnp.bfloat16)
    w_lo[...] = (w - w_hi[...].astype(jnp.float32)).astype(jnp.bfloat16)

    whole_panel.wait()
    load.wait()
    count = table_ref[COUNT, 0]

    def swap(from_mat, from_pan):
        def body(k, _):
            to = table_ref[ROW, k]
            mat[pl.ds(to, 1), :] = from_mat[pl.ds(table_ref[FROM, k], 1), :]
            pan[pl.ds(to, 1), :] = from_pan[pl.ds(table_ref[TOP, k], 1), :]
            return 0

        lax.fori_loop(0, count, body, 0)

    @pl.when(first_row)
    def _():
        swap(mat, pan)

    @pl.when(jnp.logical_not(first_row))
    def _():
        pltpu.make_async_copy(tops[0], low, low_sem).wait()
        swap(displaced_ref, low)

    @pl.when(first_col)
    def _():
        mat[:, :nb] = jnp.zeros((rows, nb), jnp.float32)

    copies = []
    for b in range(rows // block):
        span = pl.ds(b * block, block)

        def update():
            p = pan[span, :]
            p_hi = p.astype(jnp.bfloat16)
            p_lo = (p - p_hi.astype(jnp.float32)).astype(jnp.bfloat16)
            dot = functools.partial(jnp.dot, preferred_element_type=jnp.float32)
            total = dot(p_lo, w_hi[...]) + dot(p_hi, w_lo[...]) + dot(p_hi, w_hi[...])
            result[span, :] = mat[span, :] - total

        if (b + 1) * block <= nb:
            pl.when(jnp.logical_not(first_row))(update)

            @pl.when(first_row)
            def _():
                result[span, :] = top_ref[span, :]
        else:
            update()
        copy = pltpu.make_async_copy(result.at[span, :], out_ref.at[span, :], out_sem)
        copy.start()
        copies.append(copy)
    for copy in copies:
        copy.wait()


def tie(*values):
    return lax.optimization_barrier(values)


def local(matrix, pivots, lower_inverse, upper_inverse, *, n_rows, n_cols, groups):
    row_dev, cols = matrix.shape
    nb = pivots.shape[0]
    f32 = jnp.float32
    row, col = lax.axis_index("prow"), lax.axis_index("pcol")
    here = jnp.stack([row, col]).astype(jnp.int32)
    odd = row % 2 == 1
    slot = jax.ShapeDtypeStruct((nb, cols), f32)
    half_slot = jax.ShapeDtypeStruct((nb // 2, cols), f32)

    depth = n_cols // 2
    half_rows = row_dev // (2 * groups)
    piece_rows = half_rows // depth
    lanes = [[z * 2 + y for z in range(depth)] for y in range(2)]
    across = [(0, 1)] + [(p, p ^ 1) for p in range(2, n_cols)]

    def panel_rows(start, size):
        return lax.slice(matrix, (start, 0), (start + size, nb))

    def scatter(line):
        pieces = [line[z * piece_rows : (z + 1) * piece_rows] for z in range(depth)]
        mine = pieces[0]
        for z in range(1, depth):
            came = lax.ppermute(pieces[z], "pcol", [(0, 2 * z), (1, 2 * z + 1)])
            mine = jnp.where(col // 2 == z, came, mine)
        return mine

    def gather(piece):
        return lax.all_gather(piece, "pcol", axis=0, tiled=True, axis_index_groups=lanes)

    def exchange():
        table, owner = call(
            functools.partial(index_kernel, row_dev=row_dev),
            (jax.ShapeDtypeStruct((8, nb), jnp.int32), jax.ShapeDtypeStruct((nb, LANES), jnp.int32)),
            [SMEM, VMEM], (VMEM, VMEM),
        )(here, pivots.reshape(1, nb))
        held = call(gather_kernel, slot, [SMEM, VMEM], VMEM)(table, matrix)
        (held,) = yield (held,)
        displaced = held
        log = 0
        half = None
        while (1 << log) < n_rows:
            d = 1 << log
            far = [(p, p ^ d) for p in range(n_rows)]
            if log == 0:
                (whole,) = yield (lax.ppermute(held, "prow", far),)
                arrived = [whole]
            else:
                near = [(p, p ^ 1) for p in range(n_rows)]
                (one,) = yield (lax.ppermute(half, "prow", far),)
                (one,) = yield (one,)
                (two,) = yield (lax.ppermute(one, "prow", near),)
                arrived = [one, two]
                whole = both_halves(one, two)
            held, half = call(
                functools.partial(merge_kernel, log=log, halves=log > 0),
                (slot, half_slot), [SMEM] + [VMEM] * (2 + len(arrived)), (VMEM, VMEM),
            )(here, owner, held, *arrived)
            displaced = jnp.where((row >> log) == 1, whole, displaced)
            log += 1
        weights, top = call(
            factor_kernel, (slot, slot), [SMEM, VMEM, VMEM, VMEM], (VMEM, VMEM),
            flops=4 * nb * nb * cols * 6,
        )(here, held, lower_inverse, upper_inverse)
        return table, displaced, weights, top

    def both_halves(one, two):
        return jnp.concatenate([jnp.where(odd, two, one), jnp.where(odd, one, two)], axis=0)

    def spread_top():
        (near, far_half) = yield None
        old_top = call(
            old_top_kernel, jax.ShapeDtypeStruct((nb, nb), f32),
            [SMEM, ANY, ANY, ANY], ANY, [pltpu.SemaphoreType.DMA], vmem=4 << 20,
        )(here, matrix, near, far_half)
        tops = []
        log = 0
        while (1 << log) < n_rows:
            d = 1 << log
            far = [(p, p + d) for p in range(d)]
            if log == 0:
                (whole,) = yield (lax.ppermute(old_top, "prow", far),)
                tops.append(whole)
            else:
                half = jnp.where(odd, old_top[nb // 2 :], old_top[: nb // 2])
                (one,) = yield (lax.ppermute(half, "prow", far),)
                two = lax.ppermute(one, "prow", [(p, p ^ 1) for p in range(d, 2 * d)])
                tops += [one, two]
                whole = both_halves(one, two)
            old_top = jnp.where((row >> log) == 1, whole, old_top)
            log += 1
        return tops

    rows_side, top_side = Rider(exchange()), Rider(spread_top())
    fed = lax.ppermute(panel_rows(0, half_rows), "pcol", [(0, 1)])
    mine, along, other = None, [], []
    for g in range(groups + 2):
        if g == 3:
            top_side.value = (along[0], other[0])
        line, crossed = along[g - 2] if g > 1 else None, other[g - 3] if g > 3 else None
        bundle = (fed, mine, line, crossed, rows_side.value, top_side.value)
        fed, mine, line, crossed, rows_side.value, top_side.value = tie(*bundle)
        if g > 3:
            other[g - 3] = crossed
        if g > 1:
            other.append(lax.ppermute(line, "pcol", across))
        if 0 < g <= groups:
            along.append(gather(mine))
        if g < groups:
            run = jnp.where(
                col == 0, panel_rows((2 * g + 1) * half_rows, half_rows), fed
            )
            if g + 1 < groups:
                run, ahead = tie(run, panel_rows(2 * (g + 1) * half_rows, half_rows))
            mine = scatter(run)
            fed = lax.ppermute(ahead, "pcol", [(0, 1)]) if g + 1 < groups else None
        else:
            mine = None
        rows_side.go()
        if g >= 3:
            top_side.go()
    table, displaced, weights, top = rows_side.finish()
    tops = top_side.finish()
    bufs = [b for pair in zip(along, other) for b in pair]

    return call(
        functools.partial(final_kernel, n_bufs=len(bufs), n_tops=len(tops), block=256),
        jax.ShapeDtypeStruct(matrix.shape, f32),
        [SMEM, SMEM, VMEM, VMEM, VMEM, ANY] + [ANY] * (len(bufs) + len(tops)),
        ANY,
        [
            pltpu.VMEM((row_dev, cols), f32),
            pltpu.VMEM((row_dev, nb), f32),
            pltpu.VMEM((nb, nb), f32),
            pltpu.VMEM((nb, cols), jnp.bfloat16),
            pltpu.VMEM((nb, cols), jnp.bfloat16),
            pltpu.VMEM((row_dev, cols), f32),
        ] + [pltpu.SemaphoreType.DMA] * 4,
        vmem=30 << 20,
        flops=2 * row_dev * nb * cols * 3,
        moved=4 * row_dev * (2 * cols + nb),
    )(here, table, displaced, weights, top, matrix, *bufs, *tops)


class Rider:
    def __init__(self, stages):
        self.stages, self.result = stages, None
        self.value = next(stages)

    def go(self):
        if self.result is None:
            try:
                self.value = self.stages.send(self.value)
            except StopIteration as end:
                self.value, self.result = None, end.value

    def finish(self):
        while self.result is None:
            self.go()
        return self.result


def solution(mesh):
    n_rows, n_cols = mesh.shape["prow"], mesh.shape["pcol"]
    return jax.shard_map(
        functools.partial(local, n_rows=n_rows, n_cols=n_cols, groups=4),
        mesh=mesh,
        in_specs=(P("prow", "pcol"), P(), P(), P()),
        out_specs=P("prow", "pcol"),
        check_vma=False,
    )
```

```python
import functools

import jax
import jax.numpy as jnp
from jax import lax
from jax.experimental import pallas as pl
from jax.experimental.pallas import tpu as pltpu
from jax.sharding import PartitionSpec as P

HIGHEST = lax.Precision.HIGHEST
VMEM = pl.BlockSpec(memory_space=pltpu.VMEM)
SMEM = pl.BlockSpec(memory_space=pltpu.SMEM)
ANY = pl.BlockSpec(memory_space=pl.ANY)
LANES = 128
PICK, FROM, ROW, BOUND, TOP = 0, 1, 2, 3, 4
BLOCK = 256


def call(kernel, out, ins, outs, scratch=(), vmem=16 << 20, flops=0, moved=0):
    return pl.pallas_call(
        kernel,
        out_shape=out,
        in_specs=ins,
        out_specs=outs,
        scratch_shapes=list(scratch),
        compiler_params=pltpu.CompilerParams(vmem_limit_bytes=vmem),
        cost_estimate=pl.CostEstimate(
            flops=flops, bytes_accessed=moved, transcendentals=0
        ),
    )


def index_kernel(where_ref, pivots_ref, table_ref, owner_ref, *, row_dev):
    nb = pivots_ref.shape[1]
    start = where_ref[0] * row_dev
    first = where_ref[0] == 0
    down = lax.broadcasted_iota(jnp.int32, (nb, nb), 0)
    across = lax.broadcasted_iota(jnp.int32, (nb, nb), 1)
    piv_row = jnp.broadcast_to(pivots_ref[...], (nb, nb))

    def column(full):
        return jnp.sum(jnp.where(down == across, full, 0.0), axis=1, keepdims=True)

    piv_f = piv_row.astype(jnp.float32)
    piv_col = jnp.broadcast_to(column(piv_f), (nb, nb))
    upto = (down <= across).astype(jnp.bfloat16)
    below = (piv_row >= nb).astype(jnp.float32)
    vacancy = jnp.dot(
        below[:8].astype(jnp.bfloat16), upto, preferred_element_type=jnp.float32
    )[:1]
    taken = jnp.max((piv_row == down).astype(jnp.float32), axis=1, keepdims=True)
    freed = jnp.broadcast_to(1.0 - taken, (nb, LANES))
    rank = jnp.dot(
        (across <= down).astype(jnp.bfloat16),
        freed.astype(jnp.bfloat16),
        preferred_element_type=jnp.float32,
    )[:, :1]
    down_f = down.astype(jnp.float32)
    pair = (rank == vacancy) & (freed[:, :1] > 0.5)
    source = jnp.sum(jnp.where(pair, down_f, 0.0), axis=0, keepdims=True)
    source_col = jnp.broadcast_to(column(jnp.broadcast_to(source, (nb, nb))), (nb, nb))

    own_row = (pivots_ref[...] >= start) & (pivots_ref[...] < start + row_dev)
    pick = jnp.where(own_row, pivots_ref[...] - start, source.astype(jnp.int32))
    moved_row = (own_row & (pivots_ref[...] >= nb)).astype(jnp.float32)
    start_f = start.astype(jnp.float32)
    moved_col = (
        (piv_col >= start_f) & (piv_col < start_f + row_dev) & (piv_col >= nb)
    )
    order = jnp.sum(
        jnp.where(piv_f < piv_col, jnp.broadcast_to(moved_row, (nb, nb)), 0.0),
        axis=1,
        keepdims=True,
    )
    placed = moved_col & (order == across.astype(jnp.float32))
    origin = jnp.where(first, source_col, down_f)
    listed_from = jnp.sum(jnp.where(placed, origin, 0.0), axis=0, keepdims=True)
    listed_row = jnp.sum(
        jnp.where(placed, piv_col - start_f, 0.0), axis=0, keepdims=True
    )
    listed_top = jnp.sum(jnp.where(placed, source_col, 0.0), axis=0, keepdims=True)
    early = moved_col & (piv_col - start_f < (across.astype(jnp.float32) + 1.0) * BLOCK)
    bound = jnp.sum(jnp.where(early, 1.0, 0.0), axis=0, keepdims=True)
    table_ref[...] = jnp.zeros_like(table_ref)
    table_ref[PICK : PICK + 1, :] = pick
    table_ref[FROM : FROM + 1, :] = listed_from.astype(jnp.int32)
    table_ref[ROW : ROW + 1, :] = listed_row.astype(jnp.int32)
    table_ref[TOP : TOP + 1, :] = listed_top.astype(jnp.int32)
    table_ref[BOUND : BOUND + 1, :] = bound.astype(jnp.int32)
    owner_ref[...] = piv_col[:, :LANES].astype(jnp.int32) // row_dev


def gather_kernel(table_ref, matrix_ref, out_ref):
    nb = out_ref.shape[0]

    @pl.loop(0, nb, step=8)
    def _(base):
        for k in range(8):
            j = base + k
            out_ref[pl.ds(j, 1), :] = matrix_ref[pl.ds(table_ref[PICK, j], 1), :]


def merge_kernel(where_ref, owner_ref, held_ref, *refs, log, halves):
    arrived, (merged_ref, half_ref) = refs[: 2 if halves else 1], refs[-2:]
    me = where_ref[0]
    mine, theirs = me >> log, (me >> log) ^ 1
    odd = me & 1
    nb, cols = held_ref.shape
    half = nb // 2

    def merge(rows, piece):
        group = owner_ref[rows, :] >> log
        take = (group == theirs) | ((theirs == 0) & (group != mine))
        for q in range(cols // LANES):
            lane = slice(q * LANES, (q + 1) * LANES)
            merged_ref[rows, lane] = jnp.where(take, piece[:, lane], held_ref[rows, lane])

    low, high = slice(0, half), slice(half, nb)
    if halves:
        @pl.when(odd == 0)
        def _():
            merge(low, arrived[0])
            merge(high, arrived[1])

        @pl.when(odd == 1)
        def _():
            merge(low, arrived[1])
            merge(high, arrived[0])
    else:
        merge(slice(0, nb), arrived[0])

    @pl.when(odd == 0)
    def _():
        half_ref[...] = merged_ref[low, :]

    @pl.when(odd == 1)
    def _():
        half_ref[...] = merged_ref[high, :]


def split(x):
    hi = x.astype(jnp.bfloat16)
    return hi, (x - hi.astype(jnp.float32)).astype(jnp.bfloat16)


def product(a, b):
    dot = functools.partial(jnp.dot, preferred_element_type=jnp.float32)
    return dot(a[1], b[0]) + dot(a[0], b[1]) + dot(a[0], b[0])


def factor_kernel(
    where_ref, owner_ref, held_ref, one_ref, two_ref, before_ref, lower_ref, upper_ref,
    weights_ref, top_ref, displaced_ref, new_top, *, log,
):
    me = where_ref[0]
    mine, theirs = me >> log, (me >> log) ^ 1
    nb, cols = held_ref.shape
    half = nb // 2

    def merge(rows, piece):
        group = owner_ref[rows, :] >> log
        take = (group == theirs) | ((theirs == 0) & (group != mine))
        for q in range(cols // LANES):
            lane = slice(q * LANES, (q + 1) * LANES)
            new_top[rows, lane] = jnp.where(take, piece[:, lane], held_ref[rows, lane])

        @pl.when(mine == 1)
        def _():
            displaced_ref[rows, :] = piece[...]

    @pl.when(mine != 1)
    def _():
        displaced_ref[...] = before_ref[...]

    for odd, (first, second) in enumerate([(one_ref, two_ref), (two_ref, one_ref)]):
        @pl.when((me & 1) == odd)
        def _():
            merge(slice(0, half), first)
            merge(slice(half, nb), second)

    u = product(split(lower_ref[...]), split(new_top[...]))
    top_ref[...] = u
    weights_ref[...] = product(split(upper_ref[...]), split(u))

    @pl.when(where_ref[1] == 0)
    def _():
        top_ref[:, :nb] = new_top[:, :nb]
        weights_ref[:, :nb] = -upper_ref[...]


def chunk_span(k, rows, chunk):
    start = k * chunk
    size = min(chunk, rows - start)
    return start, size, chunk - size


def fetch(where_ref, choice_ref, matrix_ref, bufs, out_ref, sem_of, n_cols, parts, chunk):
    rows, nb = out_ref.shape
    for k in range(-(-rows // chunk)):
        start, size, skip = chunk_span(k, matrix_ref.shape[0], chunk)
        size = min(size, rows - start)
        to = out_ref.at[pl.ds(start, size), :]

        @pl.when(where_ref[1] == 0)
        def _():
            pltpu.make_async_copy(
                matrix_ref.at[pl.ds(start, size), pl.ds(0, nb)], to, sem_of(k)
            ).start()

        for b in sorted({arrival(p, k // 2, k % 2, n_cols, parts) for p in range(1, n_cols)}):
            @pl.when((where_ref[1] > 0) & (choice_ref[k] == b))
            def _():
                pltpu.make_async_copy(
                    bufs[b].at[pl.ds(skip, size), :], to, sem_of(k)
                ).start()


def old_top_kernel(where_ref, choice_ref, matrix_ref, *refs, used, n_cols, parts, chunk):
    bufs, top_ref, sem = dict(zip(used, refs)), refs[-2], refs[-1]
    nb = top_ref.shape[0]

    @pl.when(where_ref[0] == 0)
    def _():
        fetch(
            where_ref, choice_ref, matrix_ref, bufs, top_ref, lambda k: sem,
            n_cols, parts, chunk,
        )
        pltpu.make_async_copy(
            matrix_ref.at[pl.ds(0, nb), pl.ds(0, nb)], top_ref, sem
        ).wait()


def final_kernel(
    where_ref, table_ref, choice_ref, displaced_ref, weights_ref, top_ref, matrix_ref,
    *refs, n_bufs, n_tops, n_cols, parts, chunk,
):
    bufs, tops, out_ref = refs[:n_bufs], refs[n_bufs : n_bufs + n_tops], refs[n_bufs + n_tops]
    mat, pan, low, w_hi, w_lo, result, pan_sem, low_sem, mat_sem, out_sem = refs[
        n_bufs + n_tops + 1 :
    ]
    rows, cols = matrix_ref.shape
    nb = weights_ref.shape[0]
    half = nb // 2
    row = where_ref[0]
    first_row, first_col = row == 0, where_ref[1] == 0
    blocks = [pl.ds(b * BLOCK, BLOCK) for b in range(rows // BLOCK)]

    @pl.when(row == 1)
    def _():
        pltpu.make_async_copy(tops[0], low, low_sem).start()

    for log in range(1, (n_tops + 1) // 2):
        for odd in range(2):
            @pl.when(((row >> log) == 1) & ((row & 1) == odd))
            def _():
                for part, ref in enumerate(tops[2 * log - 1 : 2 * log + 1]):
                    at = half * (part ^ odd)
                    pltpu.make_async_copy(ref, low.at[pl.ds(at, half), :], low_sem).start()

    loads = [
        pltpu.make_async_copy(matrix_ref.at[span, :], mat.at[span, :], mat_sem.at[b])
        for b, span in enumerate(blocks)
    ]
    loads[0].start()
    fetch(
        where_ref, choice_ref, matrix_ref, bufs, pan, lambda k: pan_sem.at[k],
        n_cols, parts, chunk,
    )
    for load in loads[1:]:
        load.start()

    w_hi[...], w_lo[...] = split(weights_ref[...])

    @pl.when(jnp.logical_not(first_row))
    def _():
        pltpu.make_async_copy(tops[0], low, low_sem).wait()

    def swap(from_mat, from_pan, low_k, high_k):
        def body(k, _):
            to = table_ref[ROW, k]
            mat[pl.ds(to, 1), :] = from_mat[pl.ds(table_ref[FROM, k], 1), :]
            pan[pl.ds(to, 1), :] = from_pan[pl.ds(table_ref[TOP, k], 1), :]
            return 0

        lax.fori_loop(low_k, high_k, body, 0)

    copies = []
    ready = 0
    for b, span in enumerate(blocks):
        loads[b].wait()
        while ready < 2 * parts and ready * chunk < (b + 1) * BLOCK:
            start, size, _ = chunk_span(ready, rows, chunk)
            to = pan.at[pl.ds(start, size), :]
            pltpu.make_async_copy(
                matrix_ref.at[pl.ds(start, size), pl.ds(0, nb)], to, pan_sem.at[ready]
            ).wait()
            ready += 1
        low_k = table_ref[BOUND, b - 1] if b else 0
        high_k = table_ref[BOUND, b]

        @pl.when(jnp.logical_not(first_row))
        def _():
            swap(displaced_ref, low, low_k, high_k)

        def update():
            total = product(split(pan[span, :]), (w_hi[...], w_lo[...]))
            kept = jnp.where(first_col, 0.0, mat[span, :nb])
            result[span, :nb] = kept - total[:, :nb]
            result[span, nb:] = mat[span, nb:] - total[:, nb:]

        if (b + 1) * BLOCK <= nb:
            pl.when(jnp.logical_not(first_row))(update)

            @pl.when(first_row)
            def _():
                result[span, :] = top_ref[span, :]
        else:
            @pl.when(first_row)
            def _():
                swap(mat, pan, low_k, high_k)

            update()
        copy = pltpu.make_async_copy(result.at[span, :], out_ref.at[span, :], out_sem)
        copy.start()
        copies.append(copy)
    for copy in copies:
        copy.wait()


LAG = 2


def steps(n_cols, parts):
    depth = n_cols // 2
    return parts + LAG * (depth - 1), max(2 * parts, parts + LAG * depth)


def arrival(p, i, h, n_cols, parts):
    z, y = divmod(p, 2)
    cross = steps(n_cols, parts)[0]
    if z == 0:
        return cross + i + h * parts
    if y == 0:
        return cross + i + LAG * (z + 1) if h == 0 else i + LAG * (z - 1)
    return i + LAG * z if h == 0 else cross + i + LAG * z


def spread(pieces, col, n_cols, riders):
    parts = len(pieces)
    n_chain, n_cross = steps(n_cols, parts)
    along = [(p, p + 2) for p in range(n_cols - 2)]
    across = [(0, 1)] + [(p, p ^ 1) for p in range(2, n_cols)]
    chain, cross = [], []
    waiting = [(rider, next(rider)(chain, cross)) for rider in riders]
    for s in range(n_cross):
        ahead = pieces[min(s, parts - 1)][1]
        aside = pieces[s][0] if s < parts else pieces[min(s - parts, parts - 1)][1]
        if s >= LAG:
            came = chain[s - LAG] if s - LAG < n_chain else chain[-1]
            due = [k for k, (_, (at, _)) in enumerate(waiting) if at == s]
            tied = [waiting[k][1][1] for k in due]
            (came, fed), tied = lax.optimization_barrier(((came, cross[s - LAG]), tied))
            ahead = jnp.where(col == 0, ahead, jnp.where(col == 1, fed, came))
            aside = jnp.where(col == 0, aside, came)
        if s < n_chain:
            chain.append(lax.ppermute(ahead, "pcol", along))
        cross.append(lax.ppermute(aside, "pcol", across))
        if s >= LAG:
            for k, values in zip(due, tied):
                rider = waiting[k][0]
                waiting[k] = (rider, resume(rider, values, chain, cross))
    results = []
    for rider, (at, values) in waiting:
        while at != DONE:
            at, values = resume(rider, values, chain, cross)
        results.append(values)
    return chain, cross, results


DONE = -1


def resume(rider, values, chain, cross):
    return rider.send(values)(chain, cross)


def give(at, values):
    return lambda chain, cross: (at, values)


def local(matrix, pivots, lower_inverse, upper_inverse, *, n_rows, n_cols, parts):
    row_dev, cols = matrix.shape
    nb = pivots.shape[0]
    f32 = jnp.float32
    row, col = lax.axis_index("prow"), lax.axis_index("pcol")
    here = jnp.stack([row, col]).astype(jnp.int32)
    odd = row % 2 == 1

    chunk = -(-row_dev // (16 * parts)) * 8
    firsts = [k * chunk - chunk_span(k, row_dev, chunk)[2] for k in range(2 * parts)]
    flat = [lax.slice(matrix, (k, 0), (k + chunk, nb)) for k in firsts]
    flat = flat[:2] + list(lax.optimization_barrier(tuple(flat[2:])))
    choice = jnp.asarray(
        [
            [0] * (2 * parts) if p == 0 else
            [arrival(p, i, h, n_cols, parts) for i in range(parts) for h in range(2)]
            for p in range(n_cols)
        ],
        jnp.int32,
    )[col]

    pairs = -(-nb // (2 * chunk))
    used = sorted({
        arrival(p, i, h, n_cols, parts)
        for p in range(1, n_cols) for i in range(pairs) for h in range(2)
    })
    n_chain = steps(n_cols, parts)[0]
    last = max(b - n_chain if b >= n_chain else b for b in used)

    def both_halves(one, two):
        return jnp.concatenate([jnp.where(odd, two, one), jnp.where(odd, one, two)], axis=0)

    def old_top_rider():
        at = last + LAG

        def start(chain, cross):
            return at, [chain[b] if b < n_chain else cross[b - n_chain] for b in used]

        arrived = yield give(at - 1, ())
        arrived = yield start
        old_top = call(
            functools.partial(
                old_top_kernel, used=used, n_cols=n_cols, parts=parts, chunk=chunk
            ),
            jax.ShapeDtypeStruct((nb, nb), f32),
            [SMEM, SMEM, ANY] + [ANY] * len(used), ANY, [pltpu.SemaphoreType.DMA],
            vmem=4 << 20,
        )(here, choice, matrix, *arrived)
        tops = []
        log = 0
        while (1 << log) < n_rows:
            d = 1 << log
            far = [(p, p + d) for p in range(d)]
            if log == 0:
                at += 2
                whole = yield give(at, lax.ppermute(old_top, "prow", far))
                tops.append(whole)
            else:
                half = jnp.where(odd, old_top[nb // 2 :], old_top[: nb // 2])
                at += 3
                one = yield give(at, lax.ppermute(half, "prow", far))
                two = lax.ppermute(one, "prow", [(p, p ^ 1) for p in range(d, 2 * d)])
                tops += [one, two]
                whole = both_halves(one, two)
            old_top = jnp.where((row >> log) == 1, whole, old_top)
            log += 1
        yield give(DONE, tops)

    slot = jax.ShapeDtypeStruct((nb, cols), f32)
    half_slot = jax.ShapeDtypeStruct((nb // 2, cols), f32)

    def exchange_rider():
        table, owner = yield give(2, call(
            functools.partial(index_kernel, row_dev=row_dev),
            (jax.ShapeDtypeStruct((8, nb), jnp.int32), jax.ShapeDtypeStruct((nb, LANES), jnp.int32)),
            [SMEM, VMEM], (VMEM, VMEM),
        )(here, pivots.reshape(1, nb)))
        held = yield give(3, call(gather_kernel, slot, [SMEM, VMEM], VMEM)(table, matrix))
        at = 5
        displaced = held
        log = 0
        half = None
        while (1 << log) < n_rows:
            d = 1 << log
            far = [(p, p ^ d) for p in range(n_rows)]
            if log == 0:
                whole = yield give(at, lax.ppermute(held, "prow", far))
                arrived = [whole]
            else:
                near = [(p, p ^ 1) for p in range(n_rows)]
                one = yield give(at + 4, lax.ppermute(half, "prow", far))
                at += 5
                two = yield give(at, lax.ppermute(one, "prow", near))
                arrived = [one, two]
                whole = None if 2 << log == n_rows else both_halves(one, two)
            if 2 << log == n_rows:
                break
            held, half = call(
                functools.partial(merge_kernel, log=log, halves=log > 0),
                (slot, half_slot), [SMEM] + [VMEM] * (2 + len(arrived)), (VMEM, VMEM),
            )(here, owner, held, *arrived)
            displaced = jnp.where((row >> log) == 1, whole, displaced) if log else whole
            log += 1
        weights, top, displaced = yield give(at + 2, call(
            functools.partial(factor_kernel, log=log), (slot,) * 3,
            [SMEM] + [VMEM] * 7, (VMEM,) * 3, [pltpu.VMEM((nb, cols), f32)], vmem=24 << 20,
            flops=4 * nb * nb * cols * 3,
        )(here, owner, held, *arrived, displaced, lower_inverse, upper_inverse))
        yield give(DONE, (table, displaced, weights, top))

    chain, cross, (tops, (table, displaced, weights, top)) = spread(
        [(flat[2 * i], flat[2 * i + 1]) for i in range(parts)], col, n_cols,
        [old_top_rider(), exchange_rider()],
    )
    bufs = chain + cross

    return call(
        functools.partial(
            final_kernel, n_bufs=len(bufs), n_tops=len(tops), n_cols=n_cols, parts=parts,
            chunk=chunk,
        ),
        jax.ShapeDtypeStruct(matrix.shape, f32),
        [SMEM, SMEM, SMEM, VMEM, VMEM, VMEM, ANY] + [ANY] * (len(bufs) + len(tops)),
        ANY,
        [
            pltpu.VMEM((row_dev, cols), f32),
            pltpu.VMEM((row_dev, nb), f32),
            pltpu.VMEM((nb, nb), f32),
            pltpu.VMEM((nb, cols), jnp.bfloat16),
            pltpu.VMEM((nb, cols), jnp.bfloat16),
            pltpu.VMEM((row_dev, cols), f32),
            pltpu.SemaphoreType.DMA((2 * parts,)),
            pltpu.SemaphoreType.DMA,
            pltpu.SemaphoreType.DMA((row_dev // BLOCK,)),
            pltpu.SemaphoreType.DMA,
        ],
        vmem=30 << 20,
        flops=2 * row_dev * nb * cols * 3,
        moved=4 * row_dev * (2 * cols + nb),
    )(here, table, choice, displaced, weights, top, matrix, *bufs, *tops)


def solution(mesh):
    n_rows, n_cols = mesh.shape["prow"], mesh.shape["pcol"]
    return jax.shard_map(
        functools.partial(local, n_rows=n_rows, n_cols=n_cols, parts=6),
        mesh=mesh,
        in_specs=(P("prow", "pcol"), P(), P(), P()),
        out_specs=P("prow", "pcol"),
        check_vma=False,
    )
```

```python
import functools

import jax
import jax.numpy as jnp
from jax import lax
from jax.experimental import pallas as pl
from jax.experimental.pallas import tpu as pltpu
from jax.sharding import PartitionSpec as P

HIGHEST = lax.Precision.HIGHEST
VMEM = pl.BlockSpec(memory_space=pltpu.VMEM)
SMEM = pl.BlockSpec(memory_space=pltpu.SMEM)
ANY = pl.BlockSpec(memory_space=pl.ANY)
LANES = 128
PCOL = ("along", "side")
PICK, FROM, ROW, COUNT, TOP = 0, 1, 2, 3, 4


def call(kernel, out, ins, outs, scratch=(), vmem=16 << 20, flops=0, moved=0):
    return pl.pallas_call(
        kernel,
        out_shape=out,
        in_specs=ins,
        out_specs=outs,
        scratch_shapes=list(scratch),
        compiler_params=pltpu.CompilerParams(vmem_limit_bytes=vmem),
        cost_estimate=pl.CostEstimate(
            flops=flops, bytes_accessed=moved, transcendentals=0
        ),
    )


def index_kernel(where_ref, pivots_ref, table_ref, owner_ref, *, row_dev):
    nb = pivots_ref.shape[1]
    start = where_ref[0] * row_dev
    first = where_ref[0] == 0
    down = lax.broadcasted_iota(jnp.int32, (nb, nb), 0)
    across = lax.broadcasted_iota(jnp.int32, (nb, nb), 1)
    piv_row = jnp.broadcast_to(pivots_ref[...], (nb, nb))

    def column(full):
        return jnp.sum(jnp.where(down == across, full, 0.0), axis=1, keepdims=True)

    piv_f = piv_row.astype(jnp.float32)
    piv_col = jnp.broadcast_to(column(piv_f), (nb, nb))
    upto = (down <= across).astype(jnp.bfloat16)
    below = (piv_row >= nb).astype(jnp.float32)
    vacancy = jnp.dot(
        below[:8].astype(jnp.bfloat16), upto, preferred_element_type=jnp.float32
    )[:1]
    taken = jnp.max((piv_row == down).astype(jnp.float32), axis=1, keepdims=True)
    freed = jnp.broadcast_to(1.0 - taken, (nb, LANES))
    rank = jnp.dot(
        (across <= down).astype(jnp.bfloat16),
        freed.astype(jnp.bfloat16),
        preferred_element_type=jnp.float32,
    )[:, :1]
    down_f = down.astype(jnp.float32)
    pair = (rank == vacancy) & (freed[:, :1] > 0.5)
    source = jnp.sum(jnp.where(pair, down_f, 0.0), axis=0, keepdims=True)
    source_col = jnp.broadcast_to(column(jnp.broadcast_to(source, (nb, nb))), (nb, nb))

    own_row = (pivots_ref[...] >= start) & (pivots_ref[...] < start + row_dev)
    pick = jnp.where(own_row, pivots_ref[...] - start, source.astype(jnp.int32))
    moved_row = (own_row & (pivots_ref[...] >= nb)).astype(jnp.float32)
    start_f = start.astype(jnp.float32)
    moved_col = (
        (piv_col >= start_f) & (piv_col < start_f + row_dev) & (piv_col >= nb)
    )
    order = jnp.sum(
        jnp.where(piv_f < piv_col, jnp.broadcast_to(moved_row, (nb, nb)), 0.0),
        axis=1,
        keepdims=True,
    )
    placed = moved_col & (order == across.astype(jnp.float32))
    origin = jnp.where(first, source_col, down_f)
    listed_from = jnp.sum(jnp.where(placed, origin, 0.0), axis=0, keepdims=True)
    listed_row = jnp.sum(
        jnp.where(placed, piv_col - start_f, 0.0), axis=0, keepdims=True
    )
    listed_top = jnp.sum(jnp.where(placed, source_col, 0.0), axis=0, keepdims=True)
    count = jnp.sum(moved_row, axis=1, keepdims=True)
    table_ref[...] = jnp.zeros_like(table_ref)
    table_ref[PICK : PICK + 1, :] = pick
    table_ref[FROM : FROM + 1, :] = listed_from.astype(jnp.int32)
    table_ref[ROW : ROW + 1, :] = listed_row.astype(jnp.int32)
    table_ref[TOP : TOP + 1, :] = listed_top.astype(jnp.int32)
    table_ref[COUNT : COUNT + 1, :] = jnp.broadcast_to(
        count.astype(jnp.int32), (1, nb)
    )
    owner_ref[...] = piv_col[:, :LANES].astype(jnp.int32) // row_dev


def gather_kernel(table_ref, matrix_ref, out_ref):
    nb = out_ref.shape[0]

    @pl.loop(0, nb, step=8)
    def _(base):
        for k in range(8):
            j = base + k
            out_ref[pl.ds(j, 1), :] = matrix_ref[pl.ds(table_ref[PICK, j], 1), :]


def merge_kernel(where_ref, owner_ref, held_ref, *refs, log, halves):
    arrived, (merged_ref, half_ref) = refs[: 2 if halves else 1], refs[-2:]
    me = where_ref[0]
    mine, theirs = me >> log, (me >> log) ^ 1
    odd = me & 1
    nb, cols = held_ref.shape
    half = nb // 2

    def merge(rows, piece):
        group = owner_ref[rows, :] >> log
        take = (group == theirs) | ((theirs == 0) & (group != mine))
        for q in range(cols // LANES):
            lane = slice(q * LANES, (q + 1) * LANES)
            merged_ref[rows, lane] = jnp.where(take, piece[:, lane], held_ref[rows, lane])

    low, high = slice(0, half), slice(half, nb)
    if halves:
        @pl.when(odd == 0)
        def _():
            merge(low, arrived[0])
            merge(high, arrived[1])

        @pl.when(odd == 1)
        def _():
            merge(low, arrived[1])
            merge(high, arrived[0])
    else:
        merge(slice(0, nb), arrived[0])

    @pl.when(odd == 0)
    def _():
        half_ref[...] = merged_ref[low, :]

    @pl.when(odd == 1)
    def _():
        half_ref[...] = merged_ref[high, :]


def factor_kernel(where_ref, top_in_ref, lower_ref, upper_ref, weights_ref, top_ref):
    nb, cols = top_in_ref.shape
    u = jnp.dot(
        lower_ref[...], top_in_ref[...], precision=HIGHEST,
        preferred_element_type=jnp.float32,
    )
    top_ref[...] = u
    weights_ref[...] = jnp.dot(
        upper_ref[...], u, precision=HIGHEST, preferred_element_type=jnp.float32
    )

    @pl.when(where_ref[1] == 0)
    def _():
        top_ref[:, :nb] = top_in_ref[:, :nb]
        weights_ref[:, :nb] = -upper_ref[...]


def old_top_kernel(where_ref, matrix_ref, near_ref, far_ref, top_ref, sem):
    nb = top_ref.shape[0]
    from_matrix = pltpu.make_async_copy(
        matrix_ref.at[pl.ds(0, nb), pl.ds(0, nb)], top_ref, sem
    )

    @pl.when(where_ref[0] == 0)
    def _():
        fetch_panel(where_ref, matrix_ref, [near_ref, far_ref], top_ref, sem)
        from_matrix.wait()


def fetch_panel(where_ref, matrix_ref, bufs, out_ref, sem):
    rows, nb = out_ref.shape
    half = rows // len(bufs)
    col = where_ref[1]

    @pl.when(col == 0)
    def _():
        pltpu.make_async_copy(
            matrix_ref.at[pl.ds(0, rows), pl.ds(0, nb)], out_ref, sem
        ).start()

    for y in range(2):
        @pl.when((col > 0) & ((col & 1) == y))
        def _():
            for k, buf in enumerate(bufs):
                at = half * (k if y else k ^ 1)
                pltpu.make_async_copy(buf, out_ref.at[pl.ds(at, half), :], sem).start()


def final_kernel(
    where_ref, table_ref, displaced_ref, weights_ref, top_ref, matrix_ref,
    *refs, n_bufs, n_tops, block,
):
    bufs, tops, out_ref = refs[:n_bufs], refs[n_bufs : n_bufs + n_tops], refs[n_bufs + n_tops]
    mat, pan, low, w_hi, w_lo, result, in_sem, low_sem, mat_sem, out_sem = refs[
        n_bufs + n_tops + 1 :
    ]
    rows, cols = matrix_ref.shape
    nb = weights_ref.shape[0]
    half = nb // 2
    row = where_ref[0]
    first_row, first_col = row == 0, where_ref[1] == 0

    load = pltpu.make_async_copy(matrix_ref, mat, mat_sem)
    load.start()
    whole_panel = pltpu.make_async_copy(matrix_ref.at[:, pl.ds(0, nb)], pan, in_sem)

    fetch_panel(where_ref, matrix_ref, bufs, pan, in_sem)

    @pl.when(row == 1)
    def _():
        pltpu.make_async_copy(tops[0], low, low_sem).start()

    for log in range(1, (n_tops + 1) // 2):
        for odd in range(2):
            @pl.when(((row >> log) == 1) & ((row & 1) == odd))
            def _():
                for part, ref in enumerate(tops[2 * log - 1 : 2 * log + 1]):
                    at = half * (part ^ odd)
                    pltpu.make_async_copy(ref, low.at[pl.ds(at, half), :], low_sem).start()

    w = weights_ref[...]
    w_hi[...] = w.astype(jnp.bfloat16)
    w_lo[...] = (w - w_hi[...].astype(jnp.float32)).astype(jnp.bfloat16)

    whole_panel.wait()
    load.wait()
    count = table_ref[COUNT, 0]

    def swap(from_mat, from_pan):
        def body(k, _):
            to = table_ref[ROW, k]
            mat[pl.ds(to, 1), :] = from_mat[pl.ds(table_ref[FROM, k], 1), :]
            pan[pl.ds(to, 1), :] = from_pan[pl.ds(table_ref[TOP, k], 1), :]
            return 0

        lax.fori_loop(0, count, body, 0)

    @pl.when(first_row)
    def _():
        swap(mat, pan)

    @pl.when(jnp.logical_not(first_row))
    def _():
        pltpu.make_async_copy(tops[0], low, low_sem).wait()
        swap(displaced_ref, low)

    @pl.when(first_col)
    def _():
        mat[:, :nb] = jnp.zeros((rows, nb), jnp.float32)

    copies = []
    for b in range(rows // block):
        span = pl.ds(b * block, block)

        def update():
            p = pan[span, :]
            p_hi = p.astype(jnp.bfloat16)
            p_lo = (p - p_hi.astype(jnp.float32)).astype(jnp.bfloat16)
            dot = functools.partial(jnp.dot, preferred_element_type=jnp.float32)
            total = dot(p_lo, w_hi[...]) + dot(p_hi, w_lo[...]) + dot(p_hi, w_hi[...])
            result[span, :] = mat[span, :] - total

        if (b + 1) * block <= nb:
            pl.when(jnp.logical_not(first_row))(update)

            @pl.when(first_row)
            def _():
                result[span, :] = top_ref[span, :]
        else:
            update()
        copy = pltpu.make_async_copy(result.at[span, :], out_ref.at[span, :], out_sem)
        copy.start()
        copies.append(copy)
    for copy in copies:
        copy.wait()


def tie(*values):
    return lax.optimization_barrier(values)


def local(matrix, pivots, lower_inverse, upper_inverse, *, n_rows, n_cols, groups):
    row_dev, cols = matrix.shape
    nb = pivots.shape[0]
    f32 = jnp.float32
    row, col = lax.axis_index("prow"), lax.axis_index(PCOL)
    here = jnp.stack([row, col]).astype(jnp.int32)
    odd = row % 2 == 1
    slot = jax.ShapeDtypeStruct((nb, cols), f32)
    half_slot = jax.ShapeDtypeStruct((nb // 2, cols), f32)

    depth = n_cols // 2
    half_rows = row_dev // (2 * groups)
    piece_rows = half_rows // depth
    across = [(0, 1)] + [(p, p ^ 1) for p in range(2, n_cols)]

    def panel_rows(start, size):
        return lax.slice(matrix, (start, 0), (start + size, nb))

    def scatter(line):
        pieces = [line[z * piece_rows : (z + 1) * piece_rows] for z in range(depth)]
        mine = pieces[0]
        for z in range(1, depth):
            came = lax.ppermute(pieces[z], PCOL, [(0, 2 * z), (1, 2 * z + 1)])
            mine = jnp.where(col // 2 == z, came, mine)
        return mine

    def gather(piece):
        return lax.all_gather(piece, "along", axis=0, tiled=True)

    def exchange():
        table, owner = call(
            functools.partial(index_kernel, row_dev=row_dev),
            (jax.ShapeDtypeStruct((8, nb), jnp.int32), jax.ShapeDtypeStruct((nb, LANES), jnp.int32)),
            [SMEM, VMEM], (VMEM, VMEM),
        )(here, pivots.reshape(1, nb))
        held = call(gather_kernel, slot, [SMEM, VMEM], VMEM)(table, matrix)
        (held,) = yield (held,)
        displaced = held
        log = 0
        half = None
        while (1 << log) < n_rows:
            d = 1 << log
            far = [(p, p ^ d) for p in range(n_rows)]
            if log == 0:
                (whole,) = yield (lax.ppermute(held, "prow", far),)
                arrived = [whole]
            else:
                near = [(p, p ^ 1) for p in range(n_rows)]
                (one,) = yield (lax.ppermute(half, "prow", far),)
                (one,) = yield (one,)
                (two,) = yield (lax.ppermute(one, "prow", near),)
                arrived = [one, two]
                whole = both_halves(one, two)
            held, half = call(
                functools.partial(merge_kernel, log=log, halves=log > 0),
                (slot, half_slot), [SMEM] + [VMEM] * (2 + len(arrived)), (VMEM, VMEM),
            )(here, owner, held, *arrived)
            displaced = jnp.where((row >> log) == 1, whole, displaced)
            log += 1
        weights, top = call(
            factor_kernel, (slot, slot), [SMEM, VMEM, VMEM, VMEM], (VMEM, VMEM),
            flops=4 * nb * nb * cols * 6,
        )(here, held, lower_inverse, upper_inverse)
        return table, displaced, weights, top

    def both_halves(one, two):
        return jnp.concatenate([jnp.where(odd, two, one), jnp.where(odd, one, two)], axis=0)

    def spread_top():
        (near, far_half) = yield None
        old_top = call(
            old_top_kernel, jax.ShapeDtypeStruct((nb, nb), f32),
            [SMEM, ANY, ANY, ANY], ANY, [pltpu.SemaphoreType.DMA], vmem=4 << 20,
        )(here, matrix, near, far_half)
        tops = []
        log = 0
        while (1 << log) < n_rows:
            d = 1 << log
            far = [(p, p + d) for p in range(d)]
            if log == 0:
                (whole,) = yield (lax.ppermute(old_top, "prow", far),)
                tops.append(whole)
            else:
                half = jnp.where(odd, old_top[nb // 2 :], old_top[: nb // 2])
                (one,) = yield (lax.ppermute(half, "prow", far),)
                two = lax.ppermute(one, "prow", [(p, p ^ 1) for p in range(d, 2 * d)])
                tops += [one, two]
                whole = both_halves(one, two)
            old_top = jnp.where((row >> log) == 1, whole, old_top)
            log += 1
        return tops

    rows_side, top_side = Rider(exchange()), Rider(spread_top())
    fed = lax.ppermute(panel_rows(0, half_rows), PCOL, [(0, 1)])
    mine, along, other = None, [], []
    for g in range(groups + 2):
        if g == 3:
            top_side.value = (along[0], other[0])
        line, crossed = along[g - 2] if g > 1 else None, other[g - 3] if g > 3 else None
        bundle = (fed, mine, line, crossed, rows_side.value, top_side.value)
        fed, mine, line, crossed, rows_side.value, top_side.value = tie(*bundle)
        if g > 3:
            other[g - 3] = crossed
        if g > 1:
            other.append(lax.ppermute(line, PCOL, across))
        if 0 < g <= groups:
            along.append(gather(mine))
        if g < groups:
            run = jnp.where(
                col == 0, panel_rows((2 * g + 1) * half_rows, half_rows), fed
            )
            if g + 1 < groups:
                run, ahead = tie(run, panel_rows(2 * (g + 1) * half_rows, half_rows))
            mine = scatter(run)
            fed = lax.ppermute(ahead, PCOL, [(0, 1)]) if g + 1 < groups else None
        else:
            mine = None
        rows_side.go()
        if g >= 3:
            top_side.go()
    table, displaced, weights, top = rows_side.finish()
    tops = top_side.finish()
    bufs = [b for pair in zip(along, other) for b in pair]

    return call(
        functools.partial(final_kernel, n_bufs=len(bufs), n_tops=len(tops), block=256),
        jax.ShapeDtypeStruct(matrix.shape, f32),
        [SMEM, SMEM, VMEM, VMEM, VMEM, ANY] + [ANY] * (len(bufs) + len(tops)),
        ANY,
        [
            pltpu.VMEM((row_dev, cols), f32),
            pltpu.VMEM((row_dev, nb), f32),
            pltpu.VMEM((nb, nb), f32),
            pltpu.VMEM((nb, cols), jnp.bfloat16),
            pltpu.VMEM((nb, cols), jnp.bfloat16),
            pltpu.VMEM((row_dev, cols), f32),
        ] + [pltpu.SemaphoreType.DMA] * 4,
        vmem=30 << 20,
        flops=2 * row_dev * nb * cols * 3,
        moved=4 * row_dev * (2 * cols + nb),
    )(here, table, displaced, weights, top, matrix, *bufs, *tops)


class Rider:
    def __init__(self, stages):
        self.stages, self.result = stages, None
        self.value = next(stages)

    def go(self):
        if self.result is None:
            try:
                self.value = self.stages.send(self.value)
            except StopIteration as end:
                self.value, self.result = None, end.value

    def finish(self):
        while self.result is None:
            self.go()
        return self.result


def solution(mesh):
    n_rows, n_cols = mesh.shape["prow"], mesh.shape["pcol"]
    lines = jax.sharding.Mesh(
        mesh.devices.reshape(n_rows, n_cols // 2, 2), ("prow",) + PCOL
    )
    return jax.shard_map(
        functools.partial(local, n_rows=n_rows, n_cols=n_cols, groups=4),
        mesh=lines,
        in_specs=(P("prow", PCOL), P(), P(), P()),
        out_specs=P("prow", PCOL),
        check_vma=False,
    )
```

```python
import functools

import jax
import jax.numpy as jnp
from jax import lax
from jax.experimental import pallas as pl
from jax.experimental.pallas import tpu as pltpu
from jax.sharding import PartitionSpec as P

HIGHEST = lax.Precision.HIGHEST
VMEM = pl.BlockSpec(memory_space=pltpu.VMEM)
SMEM = pl.BlockSpec(memory_space=pltpu.SMEM)
ANY = pl.BlockSpec(memory_space=pl.ANY)
LANES = 128
PICK, FROM, ROW, COUNT, TOP = 0, 1, 2, 3, 4


def call(kernel, out, ins, outs, scratch=(), vmem=16 << 20, flops=0, moved=0):
    return pl.pallas_call(
        kernel,
        out_shape=out,
        in_specs=ins,
        out_specs=outs,
        scratch_shapes=list(scratch),
        compiler_params=pltpu.CompilerParams(vmem_limit_bytes=vmem),
        cost_estimate=pl.CostEstimate(
            flops=flops, bytes_accessed=moved, transcendentals=0
        ),
    )


def index_kernel(where_ref, pivots_ref, table_ref, owner_ref, *, row_dev):
    nb = pivots_ref.shape[1]
    start = where_ref[0] * row_dev
    first = where_ref[0] == 0
    down = lax.broadcasted_iota(jnp.int32, (nb, nb), 0)
    across = lax.broadcasted_iota(jnp.int32, (nb, nb), 1)
    piv_row = jnp.broadcast_to(pivots_ref[...], (nb, nb))

    def column(full):
        return jnp.sum(jnp.where(down == across, full, 0.0), axis=1, keepdims=True)

    piv_f = piv_row.astype(jnp.float32)
    piv_col = jnp.broadcast_to(column(piv_f), (nb, nb))
    upto = (down <= across).astype(jnp.bfloat16)
    below = (piv_row >= nb).astype(jnp.float32)
    vacancy = jnp.dot(
        below[:8].astype(jnp.bfloat16), upto, preferred_element_type=jnp.float32
    )[:1]
    taken = jnp.max((piv_row == down).astype(jnp.float32), axis=1, keepdims=True)
    freed = jnp.broadcast_to(1.0 - taken, (nb, LANES))
    rank = jnp.dot(
        (across <= down).astype(jnp.bfloat16),
        freed.astype(jnp.bfloat16),
        preferred_element_type=jnp.float32,
    )[:, :1]
    down_f = down.astype(jnp.float32)
    pair = (rank == vacancy) & (freed[:, :1] > 0.5)
    source = jnp.sum(jnp.where(pair, down_f, 0.0), axis=0, keepdims=True)
    source_col = jnp.broadcast_to(column(jnp.broadcast_to(source, (nb, nb))), (nb, nb))

    own_row = (pivots_ref[...] >= start) & (pivots_ref[...] < start + row_dev)
    pick = jnp.where(own_row, pivots_ref[...] - start, source.astype(jnp.int32))
    moved_row = (own_row & (pivots_ref[...] >= nb)).astype(jnp.float32)
    start_f = start.astype(jnp.float32)
    moved_col = (
        (piv_col >= start_f) & (piv_col < start_f + row_dev) & (piv_col >= nb)
    )
    order = jnp.sum(
        jnp.where(piv_f < piv_col, jnp.broadcast_to(moved_row, (nb, nb)), 0.0),
        axis=1,
        keepdims=True,
    )
    placed = moved_col & (order == across.astype(jnp.float32))
    origin = jnp.where(first, source_col, down_f)
    listed_from = jnp.sum(jnp.where(placed, origin, 0.0), axis=0, keepdims=True)
    listed_row = jnp.sum(
        jnp.where(placed, piv_col - start_f, 0.0), axis=0, keepdims=True
    )
    listed_top = jnp.sum(jnp.where(placed, source_col, 0.0), axis=0, keepdims=True)
    count = jnp.sum(moved_row, axis=1, keepdims=True)
    table_ref[...] = jnp.zeros_like(table_ref)
    table_ref[PICK : PICK + 1, :] = pick
    table_ref[FROM : FROM + 1, :] = listed_from.astype(jnp.int32)
    table_ref[ROW : ROW + 1, :] = listed_row.astype(jnp.int32)
    table_ref[TOP : TOP + 1, :] = listed_top.astype(jnp.int32)
    table_ref[COUNT : COUNT + 1, :] = jnp.broadcast_to(
        count.astype(jnp.int32), (1, nb)
    )
    owner_ref[...] = piv_col[:, :LANES].astype(jnp.int32) // row_dev


def gather_kernel(table_ref, matrix_ref, out_ref):
    nb = out_ref.shape[0]

    @pl.loop(0, nb, step=8)
    def _(base):
        for k in range(8):
            j = base + k
            out_ref[pl.ds(j, 1), :] = matrix_ref[pl.ds(table_ref[PICK, j], 1), :]


def merge_kernel(where_ref, owner_ref, held_ref, *refs, log, halves):
    arrived, (merged_ref, half_ref) = refs[: 2 if halves else 1], refs[-2:]
    me = where_ref[0]
    mine, theirs = me >> log, (me >> log) ^ 1
    odd = me & 1
    nb, cols = held_ref.shape
    half = nb // 2

    def merge(rows, piece):
        group = owner_ref[rows, :] >> log
        take = (group == theirs) | ((theirs == 0) & (group != mine))
        for q in range(cols // LANES):
            lane = slice(q * LANES, (q + 1) * LANES)
            merged_ref[rows, lane] = jnp.where(take, piece[:, lane], held_ref[rows, lane])

    low, high = slice(0, half), slice(half, nb)
    if halves:
        @pl.when(odd == 0)
        def _():
            merge(low, arrived[0])
            merge(high, arrived[1])

        @pl.when(odd == 1)
        def _():
            merge(low, arrived[1])
            merge(high, arrived[0])
    else:
        merge(slice(0, nb), arrived[0])

    @pl.when(odd == 0)
    def _():
        half_ref[...] = merged_ref[low, :]

    @pl.when(odd == 1)
    def _():
        half_ref[...] = merged_ref[high, :]


def split(x):
    hi = x.astype(jnp.bfloat16)
    return hi, (x - hi.astype(jnp.float32)).astype(jnp.bfloat16)


def product(a, b):
    dot = functools.partial(jnp.dot, preferred_element_type=jnp.float32)
    return dot(a[1], b[0]) + dot(a[0], b[1]) + dot(a[0], b[0])


def factor_kernel(
    where_ref, owner_ref, held_ref, one_ref, two_ref, before_ref, lower_ref, upper_ref,
    weights_ref, top_ref, displaced_ref, new_top, *, log,
):
    me = where_ref[0]
    mine, theirs = me >> log, (me >> log) ^ 1
    nb, cols = held_ref.shape
    half = nb // 2

    def merge(rows, piece):
        group = owner_ref[rows, :] >> log
        take = (group == theirs) | ((theirs == 0) & (group != mine))
        for q in range(cols // LANES):
            lane = slice(q * LANES, (q + 1) * LANES)
            new_top[rows, lane] = jnp.where(take, piece[:, lane], held_ref[rows, lane])

        @pl.when(mine == 1)
        def _():
            displaced_ref[rows, :] = piece[...]

    @pl.when(mine != 1)
    def _():
        displaced_ref[...] = before_ref[...]

    for odd, (first, second) in enumerate([(one_ref, two_ref), (two_ref, one_ref)]):
        @pl.when((me & 1) == odd)
        def _():
            merge(slice(0, half), first)
            merge(slice(half, nb), second)

    u = product(split(lower_ref[...]), split(new_top[...]))
    top_ref[...] = u
    weights_ref[...] = product(split(upper_ref[...]), split(u))

    @pl.when(where_ref[1] == 0)
    def _():
        top_ref[:, :nb] = new_top[:, :nb]
        weights_ref[:, :nb] = -upper_ref[...]


def old_top_kernel(where_ref, matrix_ref, line_ref, cross_ref, top_ref, sem):
    nb = top_ref.shape[0]
    part = nb // 2

    @pl.when(where_ref[0] == 0)
    def _():
        fetch_panel(where_ref, matrix_ref, [(0, line_ref, 0, cross_ref, 0)], part, top_ref, sem)
        pltpu.make_async_copy(
            matrix_ref.at[pl.ds(0, nb), pl.ds(0, nb)], top_ref, sem
        ).wait()


def fetch_panel(where_ref, matrix_ref, items, part, out_ref, sem):
    rows, nb = out_ref.shape
    col = where_ref[1]

    @pl.when(col == 0)
    def _():
        pltpu.make_async_copy(
            matrix_ref.at[pl.ds(0, rows), pl.ds(0, nb)], out_ref, sem
        ).start()

    for y in range(2):
        @pl.when((col > 0) & ((col & 1) == y))
        def _():
            for row, line, line_at, cross, cross_at in items:
                for k, (ref, at) in enumerate([(line, line_at), (cross, cross_at)]):
                    to = row + part * (k if y else 1 - k)
                    pltpu.make_async_copy(
                        ref.at[pl.ds(at, part), :], out_ref.at[pl.ds(to, part), :], sem
                    ).start()


def final_kernel(
    where_ref, table_ref, displaced_ref, weights_ref, top_ref, matrix_ref,
    *refs, n_bufs, n_tops, places, part, block,
):
    bufs, tops, out_ref = refs[:n_bufs], refs[n_bufs : n_bufs + n_tops], refs[n_bufs + n_tops]
    mat, pan, low, w_hi, w_lo, result, in_sem, low_sem, mat_sem, out_sem = refs[
        n_bufs + n_tops + 1 :
    ]
    rows, cols = matrix_ref.shape
    nb = weights_ref.shape[0]
    half = nb // 2
    row = where_ref[0]
    first_row, first_col = row == 0, where_ref[1] == 0

    load = pltpu.make_async_copy(matrix_ref, mat, mat_sem)
    load.start()
    whole_panel = pltpu.make_async_copy(matrix_ref.at[:, pl.ds(0, nb)], pan, in_sem)

    items = [(at, bufs[a], i, bufs[b], j) for at, a, i, b, j in places]
    fetch_panel(where_ref, matrix_ref, items, part, pan, in_sem)

    @pl.when(row == 1)
    def _():
        pltpu.make_async_copy(tops[0], low, low_sem).start()

    for log in range(1, (n_tops + 1) // 2):
        for odd in range(2):
            @pl.when(((row >> log) == 1) & ((row & 1) == odd))
            def _():
                for part, ref in enumerate(tops[2 * log - 1 : 2 * log + 1]):
                    at = half * (part ^ odd)
                    pltpu.make_async_copy(ref, low.at[pl.ds(at, half), :], low_sem).start()

    w = weights_ref[...]
    w_hi[...] = w.astype(jnp.bfloat16)
    w_lo[...] = (w - w_hi[...].astype(jnp.float32)).astype(jnp.bfloat16)

    whole_panel.wait()
    load.wait()
    count = table_ref[COUNT, 0]

    def swap(from_mat, from_pan):
        def body(k, _):
            to = table_ref[ROW, k]
            mat[pl.ds(to, 1), :] = from_mat[pl.ds(table_ref[FROM, k], 1), :]
            pan[pl.ds(to, 1), :] = from_pan[pl.ds(table_ref[TOP, k], 1), :]
            return 0

        lax.fori_loop(0, count, body, 0)

    @pl.when(first_row)
    def _():
        swap(mat, pan)

    @pl.when(jnp.logical_not(first_row))
    def _():
        pltpu.make_async_copy(tops[0], low, low_sem).wait()
        swap(displaced_ref, low)

    @pl.when(first_col)
    def _():
        mat[:, :nb] = jnp.zeros((rows, nb), jnp.float32)

    copies = []
    for b in range(rows // block):
        span = pl.ds(b * block, block)

        def update():
            p = pan[span, :]
            p_hi = p.astype(jnp.bfloat16)
            p_lo = (p - p_hi.astype(jnp.float32)).astype(jnp.bfloat16)
            dot = functools.partial(jnp.dot, preferred_element_type=jnp.float32)
            total = dot(p_lo, w_hi[...]) + dot(p_hi, w_lo[...]) + dot(p_hi, w_hi[...])
            result[span, :] = mat[span, :] - total

        if (b + 1) * block <= nb:
            pl.when(jnp.logical_not(first_row))(update)

            @pl.when(first_row)
            def _():
                result[span, :] = top_ref[span, :]
        else:
            update()
        copy = pltpu.make_async_copy(result.at[span, :], out_ref.at[span, :], out_sem)
        copy.start()
        copies.append(copy)
    for copy in copies:
        copy.wait()


def tie(*values):
    return lax.optimization_barrier(values)


def local(matrix, pivots, lower_inverse, upper_inverse, *, n_rows, n_cols):
    row_dev, cols = matrix.shape
    nb = pivots.shape[0]
    f32 = jnp.float32
    row, col = lax.axis_index("prow"), lax.axis_index("pcol")
    here = jnp.stack([row, col]).astype(jnp.int32)
    odd = row % 2 == 1
    slot = jax.ShapeDtypeStruct((nb, cols), f32)
    half_slot = jax.ShapeDtypeStruct((nb // 2, cols), f32)

    groups = row_dev // (2 * nb)
    depth = n_cols // 2
    part = nb // 2
    piece = 2 * part // depth
    lanes = [[z * 2 + y for z in range(depth)] for y in range(2)]
    across = [(0, 1)] + [(p, p ^ 1) for p in range(2, n_cols)]

    def panel(g, s, y):
        start = 2 * nb * g + nb * s + part * (1 - y)
        return lax.slice(matrix, (start, 0), (start + part, nb))

    def feed(rows):
        return lax.ppermute(rows, "pcol", [(0, 1)])

    def scatter(run, s):
        mine = None
        for k in reversed(range(depth // 2)):
            z = k + s * (depth // 2)
            came = run[k * piece : (k + 1) * piece]
            if z:
                came = lax.ppermute(came, "pcol", [(0, 2 * z), (1, 2 * z + 1)])
            mine = came if mine is None else jnp.where(col // 2 == z, came, mine)
        return mine

    def gather(piece):
        return lax.all_gather(piece, "pcol", axis=0, tiled=True, axis_index_groups=lanes)

    def cross(line, g):
        parts = [line] if g else [line[:part], line[part:]]
        return [lax.ppermute(rows, "pcol", across) for rows in parts]

    def exchange():
        table, owner = call(
            functools.partial(index_kernel, row_dev=row_dev),
            (jax.ShapeDtypeStruct((8, nb), jnp.int32), jax.ShapeDtypeStruct((nb, LANES), jnp.int32)),
            [SMEM, VMEM], (VMEM, VMEM),
        )(here, pivots.reshape(1, nb))
        held = call(gather_kernel, slot, [SMEM, VMEM], VMEM)(table, matrix)
        (held,) = yield (held,)
        displaced = held
        log = 0
        half = None
        while (1 << log) < n_rows:
            d = 1 << log
            far = [(p, p ^ d) for p in range(n_rows)]
            if log == 0:
                (whole,) = yield (lax.ppermute(held, "prow", far),)
                arrived = [whole]
            else:
                near = [(p, p ^ 1) for p in range(n_rows)]
                (one,) = yield (lax.ppermute(half, "prow", far),)
                (two,) = yield (lax.ppermute(one, "prow", near),)
                arrived = [one, two]
                whole = None if 2 << log == n_rows else both_halves(one, two)
            if 2 << log == n_rows:
                break
            held, half = call(
                functools.partial(merge_kernel, log=log, halves=log > 0),
                (slot, half_slot), [SMEM] + [VMEM] * (2 + len(arrived)), (VMEM, VMEM),
            )(here, owner, held, *arrived)
            displaced = jnp.where((row >> log) == 1, whole, displaced) if log else whole
            log += 1
        held, arrived = yield held, arrived
        weights, top, displaced = call(
            functools.partial(factor_kernel, log=log), (slot,) * 3,
            [SMEM] + [VMEM] * 7, (VMEM,) * 3, [pltpu.VMEM((nb, cols), f32)], vmem=24 << 20,
            flops=4 * nb * nb * cols * 3,
        )(here, owner, held, *arrived, displaced, lower_inverse, upper_inverse)
        return table, displaced, weights, top

    def both_halves(one, two):
        return jnp.concatenate([jnp.where(odd, two, one), jnp.where(odd, one, two)], axis=0)

    def spread_top():
        (near, far_half) = yield None
        old_top = call(
            old_top_kernel, jax.ShapeDtypeStruct((nb, nb), f32),
            [SMEM, ANY, ANY, ANY], ANY, [pltpu.SemaphoreType.DMA], vmem=4 << 20,
        )(here, matrix, near, far_half)
        tops = []
        log = 0
        while (1 << log) < n_rows:
            d = 1 << log
            far = [(p, p + d) for p in range(d)]
            if log == 0:
                (whole,) = yield (lax.ppermute(old_top, "prow", far),)
                tops.append(whole)
            else:
                half = jnp.where(odd, old_top[nb // 2 :], old_top[: nb // 2])
                (one,) = yield (lax.ppermute(half, "prow", far),)
                two = lax.ppermute(one, "prow", [(p, p ^ 1) for p in range(d, 2 * d)])
                tops += [one, two]
                whole = both_halves(one, two)
            old_top = jnp.where((row >> log) == 1, whole, old_top)
            log += 1
        return tops

    rows_side, top_side = Rider(exchange()), Rider(spread_top())
    turns = [(g, s) for g in range(groups) for s in (1, 0)]
    fed = feed(panel(0, 1, 1))
    far_piece = near_piece = None
    along, other = [], []
    for t, (g, s) in enumerate(turns):
        if s and g:
            fed, far_piece, near_piece = tie(fed, far_piece, near_piece)
        elif g:
            fed, along[g - 1], rows_side.value = tie(fed, along[g - 1], rows_side.value)
        else:
            fed, rows_side.value = tie(fed, rows_side.value)
        run = jnp.where(col == 0, panel(g, s, 0), fed)
        if t + 1 < len(turns):
            run, ahead = tie(run, panel(*turns[t + 1], 1))
            fed = feed(ahead)
        if s and g:
            along.append(gather(jnp.where(col // 2 < depth // 2, near_piece, far_piece)))
        elif g:
            other.append(cross(along[g - 1], g - 1))
        if s:
            far_piece = scatter(run, s)
        else:
            near_piece = scatter(run, s)
        if g == 0 or s == 0:
            rows_side.go()
    far_piece, near_piece, rows_side.value = tie(far_piece, near_piece, rows_side.value)
    along.append(gather(jnp.where(col // 2 < depth // 2, near_piece, far_piece)))
    rows_side.go()
    along[-1], other[0], rows_side.value = tie(along[-1], other[0], rows_side.value)
    other.append(cross(along[-1], groups - 1))
    top_side.value = (along[0], other[0][0])
    top_side.go()
    table, displaced, weights, top = rows_side.finish()
    tops = top_side.finish()
    bufs = along + [ref for refs in other for ref in refs]
    places = [
        (
            2 * nb * g + nb * s, g, s * part,
            groups + sum(map(len, other[:g])) + (s if len(other[g]) > 1 else 0),
            0 if len(other[g]) > 1 else s * part,
        )
        for g in range(groups) for s in range(2)
    ]

    return call(
        functools.partial(
            final_kernel, n_bufs=len(bufs), n_tops=len(tops), places=places, part=part,
            block=256,
        ),
        jax.ShapeDtypeStruct(matrix.shape, f32),
        [SMEM, SMEM, VMEM, VMEM, VMEM, ANY] + [ANY] * (len(bufs) + len(tops)),
        ANY,
        [
            pltpu.VMEM((row_dev, cols), f32),
            pltpu.VMEM((row_dev, nb), f32),
            pltpu.VMEM((nb, nb), f32),
            pltpu.VMEM((nb, cols), jnp.bfloat16),
            pltpu.VMEM((nb, cols), jnp.bfloat16),
            pltpu.VMEM((row_dev, cols), f32),
        ] + [pltpu.SemaphoreType.DMA] * 4,
        vmem=30 << 20,
        flops=2 * row_dev * nb * cols * 3,
        moved=4 * row_dev * (2 * cols + nb),
    )(here, table, displaced, weights, top, matrix, *bufs, *tops)


class Rider:
    def __init__(self, stages):
        self.stages, self.result = stages, None
        self.value = next(stages)

    def go(self):
        if self.result is None:
            try:
                self.value = self.stages.send(self.value)
            except StopIteration as end:
                self.value, self.result = None, end.value

    def finish(self):
        while self.result is None:
            self.go()
        return self.result


def solution(mesh):
    n_rows, n_cols = mesh.shape["prow"], mesh.shape["pcol"]
    return jax.shard_map(
        functools.partial(local, n_rows=n_rows, n_cols=n_cols),
        mesh=mesh,
        in_specs=(P("prow", "pcol"), P(), P(), P()),
        out_specs=P("prow", "pcol"),
        check_vma=False,
    )
```

```python
import functools

import jax
import jax.numpy as jnp
from jax import lax
from jax.experimental import pallas as pl
from jax.experimental.pallas import tpu as pltpu
from jax.sharding import PartitionSpec as P

HIGHEST = lax.Precision.HIGHEST
VMEM = pl.BlockSpec(memory_space=pltpu.VMEM)
SMEM = pl.BlockSpec(memory_space=pltpu.SMEM)
ANY = pl.BlockSpec(memory_space=pl.ANY)
LANES = 128
PICK, FROM, ROW, COUNT, TOP = 0, 1, 2, 3, 4


def call(kernel, out, ins, outs, scratch=(), vmem=16 << 20, flops=0, moved=0):
    return pl.pallas_call(
        kernel,
        out_shape=out,
        in_specs=ins,
        out_specs=outs,
        scratch_shapes=list(scratch),
        compiler_params=pltpu.CompilerParams(vmem_limit_bytes=vmem),
        cost_estimate=pl.CostEstimate(
            flops=flops, bytes_accessed=moved, transcendentals=0
        ),
    )


def index_kernel(where_ref, pivots_ref, table_ref, owner_ref, *, row_dev):
    nb = pivots_ref.shape[1]
    start = where_ref[0] * row_dev
    first = where_ref[0] == 0
    down = lax.broadcasted_iota(jnp.int32, (nb, nb), 0)
    across = lax.broadcasted_iota(jnp.int32, (nb, nb), 1)
    piv_row = jnp.broadcast_to(pivots_ref[...], (nb, nb))

    def column(full):
        return jnp.sum(jnp.where(down == across, full, 0.0), axis=1, keepdims=True)

    piv_f = piv_row.astype(jnp.float32)
    piv_col = jnp.broadcast_to(column(piv_f), (nb, nb))
    upto = (down <= across).astype(jnp.bfloat16)
    below = (piv_row >= nb).astype(jnp.float32)
    vacancy = jnp.dot(
        below[:8].astype(jnp.bfloat16), upto, preferred_element_type=jnp.float32
    )[:1]
    taken = jnp.max((piv_row == down).astype(jnp.float32), axis=1, keepdims=True)
    freed = jnp.broadcast_to(1.0 - taken, (nb, LANES))
    rank = jnp.dot(
        (across <= down).astype(jnp.bfloat16),
        freed.astype(jnp.bfloat16),
        preferred_element_type=jnp.float32,
    )[:, :1]
    down_f = down.astype(jnp.float32)
    pair = (rank == vacancy) & (freed[:, :1] > 0.5)
    source = jnp.sum(jnp.where(pair, down_f, 0.0), axis=0, keepdims=True)
    source_col = jnp.broadcast_to(column(jnp.broadcast_to(source, (nb, nb))), (nb, nb))

    own_row = (pivots_ref[...] >= start) & (pivots_ref[...] < start + row_dev)
    pick = jnp.where(own_row, pivots_ref[...] - start, source.astype(jnp.int32))
    moved_row = (own_row & (pivots_ref[...] >= nb)).astype(jnp.float32)
    start_f = start.astype(jnp.float32)
    moved_col = (
        (piv_col >= start_f) & (piv_col < start_f + row_dev) & (piv_col >= nb)
    )
    order = jnp.sum(
        jnp.where(piv_f < piv_col, jnp.broadcast_to(moved_row, (nb, nb)), 0.0),
        axis=1,
        keepdims=True,
    )
    placed = moved_col & (order == across.astype(jnp.float32))
    origin = jnp.where(first, source_col, down_f)
    listed_from = jnp.sum(jnp.where(placed, origin, 0.0), axis=0, keepdims=True)
    listed_row = jnp.sum(
        jnp.where(placed, piv_col - start_f, 0.0), axis=0, keepdims=True
    )
    listed_top = jnp.sum(jnp.where(placed, source_col, 0.0), axis=0, keepdims=True)
    count = jnp.sum(moved_row, axis=1, keepdims=True)
    table_ref[...] = jnp.zeros_like(table_ref)
    table_ref[PICK : PICK + 1, :] = pick
    table_ref[FROM : FROM + 1, :] = listed_from.astype(jnp.int32)
    table_ref[ROW : ROW + 1, :] = listed_row.astype(jnp.int32)
    table_ref[TOP : TOP + 1, :] = listed_top.astype(jnp.int32)
    table_ref[COUNT : COUNT + 1, :] = jnp.broadcast_to(
        count.astype(jnp.int32), (1, nb)
    )
    owner_ref[...] = piv_col[:, :LANES].astype(jnp.int32) // row_dev


def gather_kernel(table_ref, matrix_ref, out_ref):
    nb = out_ref.shape[0]

    @pl.loop(0, nb, step=8)
    def _(base):
        for k in range(8):
            j = base + k
            out_ref[pl.ds(j, 1), :] = matrix_ref[pl.ds(table_ref[PICK, j], 1), :]


def merge_kernel(where_ref, owner_ref, held_ref, *refs, log, halves):
    arrived, (merged_ref, half_ref) = refs[: 2 if halves else 1], refs[-2:]
    me = where_ref[0]
    mine, theirs = me >> log, (me >> log) ^ 1
    odd = me & 1
    nb, cols = held_ref.shape
    half = nb // 2

    def merge(rows, piece):
        group = owner_ref[rows, :] >> log
        take = (group == theirs) | ((theirs == 0) & (group != mine))
        for q in range(cols // LANES):
            lane = slice(q * LANES, (q + 1) * LANES)
            merged_ref[rows, lane] = jnp.where(take, piece[:, lane], held_ref[rows, lane])

    low, high = slice(0, half), slice(half, nb)
    if halves:
        @pl.when(odd == 0)
        def _():
            merge(low, arrived[0])
            merge(high, arrived[1])

        @pl.when(odd == 1)
        def _():
            merge(low, arrived[1])
            merge(high, arrived[0])
    else:
        merge(slice(0, nb), arrived[0])

    @pl.when(odd == 0)
    def _():
        half_ref[...] = merged_ref[low, :]

    @pl.when(odd == 1)
    def _():
        half_ref[...] = merged_ref[high, :]


def split(x):
    hi = x.astype(jnp.bfloat16)
    return hi, (x - hi.astype(jnp.float32)).astype(jnp.bfloat16)


def product(a, b):
    dot = functools.partial(jnp.dot, preferred_element_type=jnp.float32)
    return dot(a[1], b[0]) + dot(a[0], b[1]) + dot(a[0], b[0])


def factor_kernel(
    where_ref, owner_ref, held_ref, one_ref, two_ref, before_ref, lower_ref, upper_ref,
    weights_ref, top_ref, displaced_ref, new_top, *, log,
):
    me = where_ref[0]
    mine, theirs = me >> log, (me >> log) ^ 1
    nb, cols = held_ref.shape
    half = nb // 2

    def merge(rows, piece):
        group = owner_ref[rows, :] >> log
        take = (group == theirs) | ((theirs == 0) & (group != mine))
        for q in range(cols // LANES):
            lane = slice(q * LANES, (q + 1) * LANES)
            new_top[rows, lane] = jnp.where(take, piece[:, lane], held_ref[rows, lane])

        @pl.when(mine == 1)
        def _():
            displaced_ref[rows, :] = piece[...]

    @pl.when(mine != 1)
    def _():
        displaced_ref[...] = before_ref[...]

    for odd, (first, second) in enumerate([(one_ref, two_ref), (two_ref, one_ref)]):
        @pl.when((me & 1) == odd)
        def _():
            merge(slice(0, half), first)
            merge(slice(half, nb), second)

    u = product(split(lower_ref[...]), split(new_top[...]))
    top_ref[...] = u
    weights_ref[...] = product(split(upper_ref[...]), split(u))

    @pl.when(where_ref[1] == 0)
    def _():
        top_ref[:, :nb] = new_top[:, :nb]
        weights_ref[:, :nb] = -upper_ref[...]


def line_kernel(choice_ref, *refs, first, used, options):
    bufs, out_ref = dict(zip(used, refs)), refs[-1]
    chunk = bufs[used[0]].shape[0]
    for k, names in enumerate(options):
        for b in names:
            @pl.when(choice_ref[first + k] == b)
            def _():
                out_ref[k * chunk : (k + 1) * chunk, :] = bufs[b][...]


def final_kernel(
    where_ref, table_ref, displaced_ref, weights_ref, top_ref, matrix_ref,
    *refs, n_bufs, n_tops, parts, block,
):
    bufs, tops, out_ref = refs[:n_bufs], refs[n_bufs : n_bufs + n_tops], refs[n_bufs + n_tops]
    mat, pan, low, w_hi, w_lo, result, in_sem, low_sem, mat_sem, out_sem = refs[
        n_bufs + n_tops + 1 :
    ]
    rows, cols = matrix_ref.shape
    nb = weights_ref.shape[0]
    half = nb // 2
    chunk = rows // (2 * parts)
    row = where_ref[0]
    first_row, first_col = row == 0, where_ref[1] == 0

    load = pltpu.make_async_copy(matrix_ref, mat, mat_sem)
    load.start()
    whole_panel = pltpu.make_async_copy(matrix_ref.at[:, pl.ds(0, nb)], pan, in_sem)

    at = 0
    for buf in bufs:
        count = buf.shape[0] // (2 * chunk)
        for h in range(2):
            for k in range(count):
                to = (2 * (at + k) + 1 - h) * chunk
                pltpu.make_async_copy(
                    buf.at[pl.ds((h * count + k) * chunk, chunk), :],
                    pan.at[pl.ds(to, chunk), :], in_sem,
                ).start()
        at += count

    @pl.when(row == 1)
    def _():
        pltpu.make_async_copy(tops[0], low, low_sem).start()

    for log in range(1, (n_tops + 1) // 2):
        for odd in range(2):
            @pl.when(((row >> log) == 1) & ((row & 1) == odd))
            def _():
                for part, ref in enumerate(tops[2 * log - 1 : 2 * log + 1]):
                    at = half * (part ^ odd)
                    pltpu.make_async_copy(ref, low.at[pl.ds(at, half), :], low_sem).start()

    w = weights_ref[...]
    w_hi[...] = w.astype(jnp.bfloat16)
    w_lo[...] = (w - w_hi[...].astype(jnp.float32)).astype(jnp.bfloat16)

    whole_panel.wait()
    load.wait()
    count = table_ref[COUNT, 0]

    def swap(from_mat, from_pan):
        def body(k, _):
            to = table_ref[ROW, k]
            mat[pl.ds(to, 1), :] = from_mat[pl.ds(table_ref[FROM, k], 1), :]
            pan[pl.ds(to, 1), :] = from_pan[pl.ds(table_ref[TOP, k], 1), :]
            return 0

        lax.fori_loop(0, count, body, 0)

    @pl.when(first_row)
    def _():
        swap(mat, pan)

    @pl.when(jnp.logical_not(first_row))
    def _():
        pltpu.make_async_copy(tops[0], low, low_sem).wait()
        swap(displaced_ref, low)

    @pl.when(first_col)
    def _():
        mat[:, :nb] = jnp.zeros((rows, nb), jnp.float32)

    copies = []
    for b in range(rows // block):
        span = pl.ds(b * block, block)

        def update():
            p = pan[span, :]
            p_hi = p.astype(jnp.bfloat16)
            p_lo = (p - p_hi.astype(jnp.float32)).astype(jnp.bfloat16)
            dot = functools.partial(jnp.dot, preferred_element_type=jnp.float32)
            total = dot(p_lo, w_hi[...]) + dot(p_hi, w_lo[...]) + dot(p_hi, w_hi[...])
            result[span, :] = mat[span, :] - total

        if (b + 1) * block <= nb:
            pl.when(jnp.logical_not(first_row))(update)

            @pl.when(first_row)
            def _():
                result[span, :] = top_ref[span, :]
        else:
            update()
        copy = pltpu.make_async_copy(result.at[span, :], out_ref.at[span, :], out_sem)
        copy.start()
        copies.append(copy)
    for copy in copies:
        copy.wait()


LAG = 2


def came_in(p, i, parts):
    z, y = divmod(p, 2)
    if z == 0:
        return i + y * parts
    return 2 * parts + i + LAG * (z - 1 + y)


def spread(pieces, col, n_cols, riders):
    parts = len(pieces)
    n_chain = parts + LAG * (n_cols // 2 - 1)
    onward = [(p, p + 2) for p in range(n_cols - 2)]
    feed, chain = [], []
    waiting = [(rider, next(rider)(feed, chain)) for rider in riders]
    for s in range(n_chain):
        ahead = pieces[min(s, parts - 1)][1]
        if s >= LAG:
            due = [k for k, (_, (at, _)) in enumerate(waiting) if at == s]
            tied = [waiting[k][1][1] for k in due]
            fed = feed[min(s - LAG, parts - 1)]
            (came, fed), tied = lax.optimization_barrier(((chain[s - LAG], fed), tied))
            here = jnp.where(col == 1, fed, came)
            ahead = jnp.where(col == 0, ahead, here) if s < parts else here
        chain.append(lax.ppermute(ahead, "pcol", onward))
        if s < parts:
            feed.append(lax.ppermute(pieces[s][0], "pcol", [(0, 1)]))
        if s >= LAG:
            for k, values in zip(due, tied):
                rider = waiting[k][0]
                waiting[k] = (rider, resume(rider, values, feed, chain))
    results = []
    for rider, (at, values) in waiting:
        while at != DONE:
            at, values = resume(rider, values, feed, chain)
        results.append(values)
    return results


DONE = -1


def resume(rider, values, feed, chain):
    return rider.send(values)(feed, chain)


def give(at, values):
    return lambda feed, chain: (at, values)


def local(matrix, pivots, lower_inverse, upper_inverse, *, n_rows, n_cols, parts):
    row_dev, cols = matrix.shape
    nb = pivots.shape[0]
    f32 = jnp.float32
    row, col = lax.axis_index("prow"), lax.axis_index("pcol")
    here = jnp.stack([row, col]).astype(jnp.int32)
    odd = row % 2 == 1

    chunk = row_dev // (2 * parts)
    flat = [
        lax.slice(matrix, (k * chunk, 0), ((k + 1) * chunk, nb)) for k in range(2 * parts)
    ]
    flat = flat[:2] + list(lax.optimization_barrier(tuple(flat[2:])))
    pairs = [(flat[2 * i], flat[2 * i + 1]) for i in range(parts)]
    choice = jnp.asarray(
        [[came_in(p, i, parts) for i in range(parts)] for p in range(n_cols)], jnp.int32
    )[col]
    count = parts // 2
    sides = [[p, p + 1] for p in range(0, n_cols, 2)]

    def line(first, feed, chain):
        every = [piece for _, piece in pairs] + feed + [None] * (parts - len(feed)) + chain
        options = [
            sorted({came_in(p, i, parts) for p in range(n_cols)})
            for i in range(first, first + count)
        ]
        used = sorted(set().union(*options))
        return call(
            functools.partial(line_kernel, first=first, used=used, options=options),
            jax.ShapeDtypeStruct((count * chunk, nb), f32),
            [SMEM] + [VMEM] * len(used), VMEM, vmem=20 << 20,
        )(choice, *[every[b] for b in used])

    def gather(rows):
        return lax.all_gather(rows, "pcol", axis=0, tiled=True, axis_index_groups=sides)

    def line_rider():
        at = came_in(n_cols - 1, count - 1, parts) - 2 * parts + LAG
        early = yield give(at, ())
        early = yield lambda feed, chain: (at + 1, line(0, feed, chain))
        yield give(DONE, gather(early))

    def late_rider():
        yield lambda feed, chain: (DONE - 1, ())
        yield lambda feed, chain: (DONE, line(parts - count, feed, chain))

    def both_halves(one, two):
        return jnp.concatenate([jnp.where(odd, two, one), jnp.where(odd, one, two)], axis=0)

    def spread_top(panel):
        own = [
            panel[(h * count + i) * chunk : (h * count + i + 1) * chunk]
            for i in range(nb // (2 * chunk)) for h in (1, 0)
        ]
        old_top = jnp.concatenate(own, axis=0)
        tops = []
        log = 0
        while (1 << log) < n_rows:
            d = 1 << log
            far = [(p, p + d) for p in range(d)]
            if log == 0:
                whole = lax.ppermute(old_top, "prow", far)
                tops.append(whole)
            else:
                half = jnp.where(odd, old_top[nb // 2 :], old_top[: nb // 2])
                one = lax.ppermute(half, "prow", far)
                two = lax.ppermute(one, "prow", [(p, p ^ 1) for p in range(d, 2 * d)])
                tops += [one, two]
                whole = both_halves(one, two)
            old_top = jnp.where((row >> log) == 1, whole, old_top)
            log += 1
        return tops

    slot = jax.ShapeDtypeStruct((nb, cols), f32)
    half_slot = jax.ShapeDtypeStruct((nb // 2, cols), f32)

    def exchange_rider():
        table, owner = yield give(2, call(
            functools.partial(index_kernel, row_dev=row_dev),
            (jax.ShapeDtypeStruct((8, nb), jnp.int32), jax.ShapeDtypeStruct((nb, LANES), jnp.int32)),
            [SMEM, VMEM], (VMEM, VMEM),
        )(here, pivots.reshape(1, nb)))
        held = yield give(3, call(gather_kernel, slot, [SMEM, VMEM], VMEM)(table, matrix))
        at = 5
        displaced = held
        log = 0
        half = None
        while (1 << log) < n_rows:
            d = 1 << log
            far = [(p, p ^ d) for p in range(n_rows)]
            if log == 0:
                whole = yield give(at, lax.ppermute(held, "prow", far))
                arrived = [whole]
            else:
                near = [(p, p ^ 1) for p in range(n_rows)]
                one = yield give(at + 4, lax.ppermute(half, "prow", far))
                at += 5
                two = yield give(at, lax.ppermute(one, "prow", near))
                arrived = [one, two]
                whole = None if 2 << log == n_rows else both_halves(one, two)
            if 2 << log == n_rows:
                break
            held, half = call(
                functools.partial(merge_kernel, log=log, halves=log > 0),
                (slot, half_slot), [SMEM] + [VMEM] * (2 + len(arrived)), (VMEM, VMEM),
            )(here, owner, held, *arrived)
            displaced = jnp.where((row >> log) == 1, whole, displaced) if log else whole
            log += 1
        yield give(DONE, (table, owner, log, displaced, held, arrived))

    early, late, (table, owner, log, displaced, held, arrived) = spread(
        pairs, col, n_cols, [line_rider(), late_rider(), exchange_rider()]
    )
    bufs = [early, gather(late)]
    _, held, arrived, early = lax.optimization_barrier((late, held, arrived, early))
    tops = spread_top(early)
    weights, top, displaced = call(
        functools.partial(factor_kernel, log=log), (slot,) * 3,
        [SMEM] + [VMEM] * 7, (VMEM,) * 3, [pltpu.VMEM((nb, cols), f32)], vmem=20 << 20,
        flops=4 * nb * nb * cols * 3,
    )(here, owner, held, *arrived, displaced, lower_inverse, upper_inverse)

    return call(
        functools.partial(
            final_kernel, n_bufs=len(bufs), n_tops=len(tops), parts=parts,
            block=256,
        ),
        jax.ShapeDtypeStruct(matrix.shape, f32),
        [SMEM, SMEM, VMEM, VMEM, VMEM, ANY] + [ANY] * (len(bufs) + len(tops)),
        ANY,
        [
            pltpu.VMEM((row_dev, cols), f32),
            pltpu.VMEM((row_dev, nb), f32),
            pltpu.VMEM((nb, nb), f32),
            pltpu.VMEM((nb, cols), jnp.bfloat16),
            pltpu.VMEM((nb, cols), jnp.bfloat16),
            pltpu.VMEM((row_dev, cols), f32),
        ] + [pltpu.SemaphoreType.DMA] * 4,
        vmem=30 << 20,
        flops=2 * row_dev * nb * cols * 3,
        moved=4 * row_dev * (2 * cols + nb),
    )(here, table, displaced, weights, top, matrix, *bufs, *tops)


def solution(mesh):
    n_rows, n_cols = mesh.shape["prow"], mesh.shape["pcol"]
    return jax.shard_map(
        functools.partial(local, n_rows=n_rows, n_cols=n_cols, parts=8),
        mesh=mesh,
        in_specs=(P("prow", "pcol"), P(), P(), P()),
        out_specs=P("prow", "pcol"),
        check_vma=False,
    )
```

```python
import functools

import jax
import jax.numpy as jnp
from jax import lax
from jax.experimental import pallas as pl
from jax.experimental.pallas import tpu as pltpu
from jax.sharding import PartitionSpec as P

HIGHEST = lax.Precision.HIGHEST
VMEM = pl.BlockSpec(memory_space=pltpu.VMEM)
SMEM = pl.BlockSpec(memory_space=pltpu.SMEM)
ANY = pl.BlockSpec(memory_space=pl.ANY)
LANES = 128
PICK, FROM, ROW, COUNT, TOP = 0, 1, 2, 3, 4


def call(kernel, out, ins, outs, scratch=(), vmem=16 << 20, flops=0, moved=0):
    return pl.pallas_call(
        kernel,
        out_shape=out,
        in_specs=ins,
        out_specs=outs,
        scratch_shapes=list(scratch),
        compiler_params=pltpu.CompilerParams(vmem_limit_bytes=vmem),
        cost_estimate=pl.CostEstimate(
            flops=flops, bytes_accessed=moved, transcendentals=0
        ),
    )


def index_kernel(where_ref, pivots_ref, table_ref, owner_ref, *, row_dev):
    nb = pivots_ref.shape[1]
    start = where_ref[0] * row_dev
    first = where_ref[0] == 0
    down = lax.broadcasted_iota(jnp.int32, (nb, nb), 0)
    across = lax.broadcasted_iota(jnp.int32, (nb, nb), 1)
    piv_row = jnp.broadcast_to(pivots_ref[...], (nb, nb))

    def column(full):
        return jnp.sum(jnp.where(down == across, full, 0.0), axis=1, keepdims=True)

    piv_f = piv_row.astype(jnp.float32)
    piv_col = jnp.broadcast_to(column(piv_f), (nb, nb))
    upto = (down <= across).astype(jnp.bfloat16)
    below = (piv_row >= nb).astype(jnp.float32)
    vacancy = jnp.dot(
        below[:8].astype(jnp.bfloat16), upto, preferred_element_type=jnp.float32
    )[:1]
    taken = jnp.max((piv_row == down).astype(jnp.float32), axis=1, keepdims=True)
    freed = jnp.broadcast_to(1.0 - taken, (nb, LANES))
    rank = jnp.dot(
        (across <= down).astype(jnp.bfloat16),
        freed.astype(jnp.bfloat16),
        preferred_element_type=jnp.float32,
    )[:, :1]
    down_f = down.astype(jnp.float32)
    pair = (rank == vacancy) & (freed[:, :1] > 0.5)
    source = jnp.sum(jnp.where(pair, down_f, 0.0), axis=0, keepdims=True)
    source_col = jnp.broadcast_to(column(jnp.broadcast_to(source, (nb, nb))), (nb, nb))

    own_row = (pivots_ref[...] >= start) & (pivots_ref[...] < start + row_dev)
    pick = jnp.where(own_row, pivots_ref[...] - start, source.astype(jnp.int32))
    moved_row = (own_row & (pivots_ref[...] >= nb)).astype(jnp.float32)
    start_f = start.astype(jnp.float32)
    moved_col = (
        (piv_col >= start_f) & (piv_col < start_f + row_dev) & (piv_col >= nb)
    )
    order = jnp.sum(
        jnp.where(piv_f < piv_col, jnp.broadcast_to(moved_row, (nb, nb)), 0.0),
        axis=1,
        keepdims=True,
    )
    placed = moved_col & (order == across.astype(jnp.float32))
    origin = jnp.where(first, source_col, down_f)
    listed_from = jnp.sum(jnp.where(placed, origin, 0.0), axis=0, keepdims=True)
    listed_row = jnp.sum(
        jnp.where(placed, piv_col - start_f, 0.0), axis=0, keepdims=True
    )
    listed_top = jnp.sum(jnp.where(placed, source_col, 0.0), axis=0, keepdims=True)
    count = jnp.sum(moved_row, axis=1, keepdims=True)
    table_ref[...] = jnp.zeros_like(table_ref)
    table_ref[PICK : PICK + 1, :] = pick
    table_ref[FROM : FROM + 1, :] = listed_from.astype(jnp.int32)
    table_ref[ROW : ROW + 1, :] = listed_row.astype(jnp.int32)
    table_ref[TOP : TOP + 1, :] = listed_top.astype(jnp.int32)
    table_ref[COUNT : COUNT + 1, :] = jnp.broadcast_to(
        count.astype(jnp.int32), (1, nb)
    )
    owner_ref[...] = piv_col[:, :LANES].astype(jnp.int32) // row_dev


def gather_kernel(table_ref, matrix_ref, out_ref):
    nb = out_ref.shape[0]

    @pl.loop(0, nb, step=8)
    def _(base):
        for k in range(8):
            j = base + k
            out_ref[pl.ds(j, 1), :] = matrix_ref[pl.ds(table_ref[PICK, j], 1), :]


def merge_kernel(where_ref, owner_ref, held_ref, *refs, log, halves):
    arrived, (merged_ref, half_ref) = refs[: 2 if halves else 1], refs[-2:]
    me = where_ref[0]
    mine, theirs = me >> log, (me >> log) ^ 1
    odd = me & 1
    nb, cols = held_ref.shape
    half = nb // 2

    def merge(rows, piece):
        group = owner_ref[rows, :] >> log
        take = (group == theirs) | ((theirs == 0) & (group != mine))
        for q in range(cols // LANES):
            lane = slice(q * LANES, (q + 1) * LANES)
            merged_ref[rows, lane] = jnp.where(take, piece[:, lane], held_ref[rows, lane])

    low, high = slice(0, half), slice(half, nb)
    if halves:
        @pl.when(odd == 0)
        def _():
            merge(low, arrived[0])
            merge(high, arrived[1])

        @pl.when(odd == 1)
        def _():
            merge(low, arrived[1])
            merge(high, arrived[0])
    else:
        merge(slice(0, nb), arrived[0])

    @pl.when(odd == 0)
    def _():
        half_ref[...] = merged_ref[low, :]

    @pl.when(odd == 1)
    def _():
        half_ref[...] = merged_ref[high, :]


def factor_kernel(where_ref, top_in_ref, lower_ref, upper_ref, weights_ref, top_ref):
    nb, cols = top_in_ref.shape
    u = jnp.dot(
        lower_ref[...], top_in_ref[...], precision=HIGHEST,
        preferred_element_type=jnp.float32,
    )
    top_ref[...] = u
    weights_ref[...] = jnp.dot(
        upper_ref[...], u, precision=HIGHEST, preferred_element_type=jnp.float32
    )

    @pl.when(where_ref[1] == 0)
    def _():
        top_ref[:, :nb] = top_in_ref[:, :nb]
        weights_ref[:, :nb] = -upper_ref[...]


def fetch(choice_ref, bufs, place, sem, n_cols, parts, pairs):
    for i in range(pairs):
        for h in range(2):
            for b in sorted({arrival(p, i, h, n_cols, parts) for p in range(1, n_cols)}):
                @pl.when(choice_ref[2 * i + h] == b)
                def _():
                    pltpu.make_async_copy(bufs[b], place(i, h), sem).start()


def old_top_kernel(where_ref, choice_ref, matrix_ref, *refs, used, n_cols, parts, pairs):
    bufs, top_ref, sem = dict(zip(used, refs)), refs[-2], refs[-1]
    nb = top_ref.shape[0]
    chunk = nb // (2 * pairs)
    from_matrix = pltpu.make_async_copy(
        matrix_ref.at[pl.ds(0, nb), pl.ds(0, nb)], top_ref, sem
    )

    @pl.when(where_ref[0] == 0)
    def _():
        @pl.when(where_ref[1] == 0)
        def _():
            from_matrix.start()

        @pl.when(where_ref[1] > 0)
        def _():
            fetch(
                choice_ref, bufs,
                lambda i, h: top_ref.at[pl.ds((2 * i + h) * chunk, chunk), :],
                sem, n_cols, parts, pairs,
            )

        from_matrix.wait()


def final_kernel(
    where_ref, table_ref, choice_ref, displaced_ref, weights_ref, top_ref, matrix_ref,
    *refs, n_bufs, n_tops, n_cols, parts, block,
):
    bufs, tops, out_ref = refs[:n_bufs], refs[n_bufs : n_bufs + n_tops], refs[n_bufs + n_tops]
    mat, pan, low, w_hi, w_lo, result, in_sem, low_sem, mat_sem, out_sem = refs[
        n_bufs + n_tops + 1 :
    ]
    rows, cols = matrix_ref.shape
    nb = weights_ref.shape[0]
    half = nb // 2
    chunk = rows // (2 * parts)
    row = where_ref[0]
    first_row, first_col = row == 0, where_ref[1] == 0

    load = pltpu.make_async_copy(matrix_ref, mat, mat_sem)
    load.start()
    whole_panel = pltpu.make_async_copy(matrix_ref.at[:, pl.ds(0, nb)], pan, in_sem)

    @pl.when(first_col)
    def _():
        whole_panel.start()

    @pl.when(jnp.logical_not(first_col))
    def _():
        fetch(
            choice_ref, bufs, lambda i, h: pan.at[pl.ds((2 * i + h) * chunk, chunk), :],
            in_sem, n_cols, parts, parts,
        )

    @pl.when(row == 1)
    def _():
        pltpu.make_async_copy(tops[0], low, low_sem).start()

    for log in range(1, (n_tops + 1) // 2):
        for odd in range(2):
            @pl.when(((row >> log) == 1) & ((row & 1) == odd))
            def _():
                for part, ref in enumerate(tops[2 * log - 1 : 2 * log + 1]):
                    at = half * (part ^ odd)
                    pltpu.make_async_copy(ref, low.at[pl.ds(at, half), :], low_sem).start()

    w = weights_ref[...]
    w_hi[...] = w.astype(jnp.bfloat16)
    w_lo[...] = (w - w_hi[...].astype(jnp.float32)).astype(jnp.bfloat16)

    whole_panel.wait()
    load.wait()
    count = table_ref[COUNT, 0]

    def swap(from_mat, from_pan):
        def body(k, _):
            to = table_ref[ROW, k]
            mat[pl.ds(to, 1), :] = from_mat[pl.ds(table_ref[FROM, k], 1), :]
            pan[pl.ds(to, 1), :] = from_pan[pl.ds(table_ref[TOP, k], 1), :]
            return 0

        lax.fori_loop(0, count, body, 0)

    @pl.when(first_row)
    def _():
        swap(mat, pan)

    @pl.when(jnp.logical_not(first_row))
    def _():
        pltpu.make_async_copy(tops[0], low, low_sem).wait()
        swap(displaced_ref, low)

    @pl.when(first_col)
    def _():
        mat[:, :nb] = jnp.zeros((rows, nb), jnp.float32)

    copies = []
    for b in range(rows // block):
        span = pl.ds(b * block, block)

        def update():
            p = pan[span, :]
            p_hi = p.astype(jnp.bfloat16)
            p_lo = (p - p_hi.astype(jnp.float32)).astype(jnp.bfloat16)
            dot = functools.partial(jnp.dot, preferred_element_type=jnp.float32)
            total = dot(p_lo, w_hi[...]) + dot(p_hi, w_lo[...]) + dot(p_hi, w_hi[...])
            result[span, :] = mat[span, :] - total

        if (b + 1) * block <= nb:
            pl.when(jnp.logical_not(first_row))(update)

            @pl.when(first_row)
            def _():
                result[span, :] = top_ref[span, :]
        else:
            update()
        copy = pltpu.make_async_copy(result.at[span, :], out_ref.at[span, :], out_sem)
        copy.start()
        copies.append(copy)
    for copy in copies:
        copy.wait()


LAG = 1


def steps(n_cols, parts):
    depth = n_cols // 2
    return parts + LAG * (depth - 1), max(2 * parts, parts + LAG * depth)


def arrival(p, i, h, n_cols, parts):
    z, y = divmod(p, 2)
    cross = steps(n_cols, parts)[0]
    if z == 0:
        return cross + i + h * parts
    if y == 0:
        return cross + i + LAG * (z + 1) if h == 0 else i + LAG * (z - 1)
    return i + LAG * z if h == 0 else cross + i + LAG * z


def spread(pieces, col, n_cols, riders):
    parts = len(pieces)
    n_chain, n_cross = steps(n_cols, parts)
    along = [(p, p + 2) for p in range(n_cols - 2)]
    across = [(0, 1)] + [(p, p ^ 1) for p in range(2, n_cols)]
    chain, cross = [], []
    waiting = [(rider, next(rider)(chain, cross)) for rider in riders]
    for s in range(n_cross):
        ahead = pieces[min(s, parts - 1)][1]
        aside = pieces[s][0] if s < parts else pieces[min(s - parts, parts - 1)][1]
        if s >= LAG:
            came = chain[s - LAG] if s - LAG < n_chain else chain[-1]
            due = [k for k, (_, (at, _)) in enumerate(waiting) if at == s]
            tied = [waiting[k][1][1] for k in due]
            (came, fed), tied = lax.optimization_barrier(((came, cross[s - LAG]), tied))
            ahead = jnp.where(col == 0, ahead, jnp.where(col == 1, fed, came))
            aside = jnp.where(col == 0, aside, came)
        if s < n_chain:
            chain.append(lax.ppermute(ahead, "pcol", along))
        cross.append(lax.ppermute(aside, "pcol", across))
        if s >= LAG:
            for k, values in zip(due, tied):
                rider = waiting[k][0]
                waiting[k] = (rider, resume(rider, values, chain, cross))
    results = []
    for rider, (at, values) in waiting:
        while at != DONE:
            at, values = resume(rider, values, chain, cross)
        results.append(values)
    return chain, cross, results


DONE = -1


def resume(rider, values, chain, cross):
    return rider.send(values)(chain, cross)


def give(at, values):
    return lambda chain, cross: (at, values)


def local(matrix, pivots, lower_inverse, upper_inverse, *, n_rows, n_cols, parts):
    row_dev, cols = matrix.shape
    nb = pivots.shape[0]
    f32 = jnp.float32
    row, col = lax.axis_index("prow"), lax.axis_index("pcol")
    here = jnp.stack([row, col]).astype(jnp.int32)
    odd = row % 2 == 1

    chunk = row_dev // (2 * parts)
    flat = [
        lax.slice(matrix, (k * chunk, 0), ((k + 1) * chunk, nb)) for k in range(2 * parts)
    ]
    flat = flat[:2] + list(lax.optimization_barrier(tuple(flat[2:])))
    choice = jnp.asarray(
        [
            [0] * (2 * parts) if p == 0 else
            [arrival(p, i, h, n_cols, parts) for i in range(parts) for h in range(2)]
            for p in range(n_cols)
        ],
        jnp.int32,
    )[col]

    pairs = nb // (2 * chunk)
    used = sorted({
        arrival(p, i, h, n_cols, parts)
        for p in range(1, n_cols) for i in range(pairs) for h in range(2)
    })
    n_chain = steps(n_cols, parts)[0]
    last = max(b - n_chain if b >= n_chain else b for b in used)

    def both_halves(one, two):
        return jnp.concatenate([jnp.where(odd, two, one), jnp.where(odd, one, two)], axis=0)

    def old_top_rider():
        at = last + LAG

        def start(chain, cross):
            return at, [chain[b] if b < n_chain else cross[b - n_chain] for b in used]

        arrived = yield give(at - 1, ())
        arrived = yield start
        old_top = call(
            functools.partial(
                old_top_kernel, used=used, n_cols=n_cols, parts=parts, pairs=pairs
            ),
            jax.ShapeDtypeStruct((nb, nb), f32),
            [SMEM, SMEM, ANY] + [ANY] * len(used), ANY, [pltpu.SemaphoreType.DMA],
            vmem=4 << 20,
        )(here, choice, matrix, *arrived)
        tops = []
        log = 0
        while (1 << log) < n_rows:
            d = 1 << log
            far = [(p, p + d) for p in range(d)]
            if log == 0:
                at += 1
                whole = yield give(at, lax.ppermute(old_top, "prow", far))
                tops.append(whole)
            else:
                half = jnp.where(odd, old_top[nb // 2 :], old_top[: nb // 2])
                at += 1
                one = yield give(at, lax.ppermute(half, "prow", far))
                two = lax.ppermute(one, "prow", [(p, p ^ 1) for p in range(d, 2 * d)])
                tops += [one, two]
                whole = both_halves(one, two)
            old_top = jnp.where((row >> log) == 1, whole, old_top)
            log += 1
        yield give(DONE, tops)

    slot = jax.ShapeDtypeStruct((nb, cols), f32)
    half_slot = jax.ShapeDtypeStruct((nb // 2, cols), f32)

    def exchange_rider():
        table, owner = yield give(1, call(
            functools.partial(index_kernel, row_dev=row_dev),
            (jax.ShapeDtypeStruct((8, nb), jnp.int32), jax.ShapeDtypeStruct((nb, LANES), jnp.int32)),
            [SMEM, VMEM], (VMEM, VMEM),
        )(here, pivots.reshape(1, nb)))
        held = yield give(2, call(gather_kernel, slot, [SMEM, VMEM], VMEM)(table, matrix))
        at = 3
        displaced = held
        log = 0
        half = None
        while (1 << log) < n_rows:
            d = 1 << log
            far = [(p, p ^ d) for p in range(n_rows)]
            if log == 0:
                whole = yield give(at, lax.ppermute(held, "prow", far))
                arrived = [whole]
            else:
                near = [(p, p ^ 1) for p in range(n_rows)]
                one = yield give(at + 2, lax.ppermute(half, "prow", far))
                at += 3
                two = yield give(at, lax.ppermute(one, "prow", near))
                arrived = [one, two]
                whole = both_halves(one, two)
            held, half = call(
                functools.partial(merge_kernel, log=log, halves=log > 0),
                (slot, half_slot), [SMEM] + [VMEM] * (2 + len(arrived)), (VMEM, VMEM),
            )(here, owner, held, *arrived)
            displaced = jnp.where((row >> log) == 1, whole, displaced)
            log += 1
        held, displaced = yield give(at + 1, (held, displaced))
        weights, top = yield give(at + 2, call(
            factor_kernel, (slot, slot), [SMEM, VMEM, VMEM, VMEM], (VMEM, VMEM),
            flops=4 * nb * nb * cols * 6,
        )(here, held, lower_inverse, upper_inverse))
        yield give(DONE, (table, displaced, weights, top))

    chain, cross, (tops, (table, displaced, weights, top)) = spread(
        [(flat[2 * i], flat[2 * i + 1]) for i in range(parts)], col, n_cols,
        [old_top_rider(), exchange_rider()],
    )
    bufs = chain + cross

    return call(
        functools.partial(
            final_kernel, n_bufs=len(bufs), n_tops=len(tops), n_cols=n_cols, parts=parts,
            block=256,
        ),
        jax.ShapeDtypeStruct(matrix.shape, f32),
        [SMEM, SMEM, SMEM, VMEM, VMEM, VMEM, ANY] + [ANY] * (len(bufs) + len(tops)),
        ANY,
        [
            pltpu.VMEM((row_dev, cols), f32),
            pltpu.VMEM((row_dev, nb), f32),
            pltpu.VMEM((nb, nb), f32),
            pltpu.VMEM((nb, cols), jnp.bfloat16),
            pltpu.VMEM((nb, cols), jnp.bfloat16),
            pltpu.VMEM((row_dev, cols), f32),
        ] + [pltpu.SemaphoreType.DMA] * 4,
        vmem=30 << 20,
        flops=2 * row_dev * nb * cols * 3,
        moved=4 * row_dev * (2 * cols + nb),
    )(here, table, choice, displaced, weights, top, matrix, *bufs, *tops)


def solution(mesh):
    n_rows, n_cols = mesh.shape["prow"], mesh.shape["pcol"]
    return jax.shard_map(
        functools.partial(local, n_rows=n_rows, n_cols=n_cols, parts=4),
        mesh=mesh,
        in_specs=(P("prow", "pcol"), P(), P(), P()),
        out_specs=P("prow", "pcol"),
        check_vma=False,
    )
```

```python
import functools

import jax
import jax.numpy as jnp
from jax import lax
from jax.experimental import pallas as pl
from jax.experimental.pallas import tpu as pltpu
from jax.sharding import PartitionSpec as P

VMEM = pl.BlockSpec(memory_space=pltpu.VMEM)
SMEM = pl.BlockSpec(memory_space=pltpu.SMEM)
ANY = pl.BlockSpec(memory_space=pl.ANY)
LANES = 128
PICK, FROM, ROW, COUNT, TOP = 0, 1, 2, 3, 4


def call(kernel, out, ins, outs, scratch=(), vmem=16 << 20, flops=0, moved=0):
    return pl.pallas_call(
        kernel,
        out_shape=out,
        in_specs=ins,
        out_specs=outs,
        scratch_shapes=list(scratch),
        compiler_params=pltpu.CompilerParams(vmem_limit_bytes=vmem),
        cost_estimate=pl.CostEstimate(
            flops=flops, bytes_accessed=moved, transcendentals=0
        ),
    )


def index_kernel(where_ref, pivots_ref, table_ref, owner_ref, *, row_dev):
    nb = pivots_ref.shape[1]
    start = where_ref[0] * row_dev
    first = where_ref[0] == 0
    down = lax.broadcasted_iota(jnp.int32, (nb, nb), 0)
    across = lax.broadcasted_iota(jnp.int32, (nb, nb), 1)
    piv_row = jnp.broadcast_to(pivots_ref[...], (nb, nb))

    def column(full):
        return jnp.sum(jnp.where(down == across, full, 0.0), axis=1, keepdims=True)

    piv_f = piv_row.astype(jnp.float32)
    piv_col = jnp.broadcast_to(column(piv_f), (nb, nb))
    upto = (down <= across).astype(jnp.bfloat16)
    below = (piv_row >= nb).astype(jnp.float32)
    vacancy = jnp.dot(
        below[:8].astype(jnp.bfloat16), upto, preferred_element_type=jnp.float32
    )[:1]
    taken = jnp.max((piv_row == down).astype(jnp.float32), axis=1, keepdims=True)
    freed = jnp.broadcast_to(1.0 - taken, (nb, LANES))
    rank = jnp.dot(
        (across <= down).astype(jnp.bfloat16),
        freed.astype(jnp.bfloat16),
        preferred_element_type=jnp.float32,
    )[:, :1]
    down_f = down.astype(jnp.float32)
    pair = (rank == vacancy) & (freed[:, :1] > 0.5)
    source = jnp.sum(jnp.where(pair, down_f, 0.0), axis=0, keepdims=True)
    source_col = jnp.broadcast_to(column(jnp.broadcast_to(source, (nb, nb))), (nb, nb))

    own_row = (pivots_ref[...] >= start) & (pivots_ref[...] < start + row_dev)
    pick = jnp.where(own_row, pivots_ref[...] - start, source.astype(jnp.int32))
    moved_row = (own_row & (pivots_ref[...] >= nb)).astype(jnp.float32)
    start_f = start.astype(jnp.float32)
    moved_col = (
        (piv_col >= start_f) & (piv_col < start_f + row_dev) & (piv_col >= nb)
    )
    order = jnp.sum(
        jnp.where(piv_f < piv_col, jnp.broadcast_to(moved_row, (nb, nb)), 0.0),
        axis=1,
        keepdims=True,
    )
    placed = moved_col & (order == across.astype(jnp.float32))
    origin = jnp.where(first, source_col, down_f)
    listed_from = jnp.sum(jnp.where(placed, origin, 0.0), axis=0, keepdims=True)
    listed_row = jnp.sum(
        jnp.where(placed, piv_col - start_f, 0.0), axis=0, keepdims=True
    )
    listed_top = jnp.sum(jnp.where(placed, source_col, 0.0), axis=0, keepdims=True)
    count = jnp.sum(moved_row, axis=1, keepdims=True)
    table_ref[...] = jnp.zeros_like(table_ref)
    table_ref[PICK : PICK + 1, :] = pick
    table_ref[FROM : FROM + 1, :] = listed_from.astype(jnp.int32)
    table_ref[ROW : ROW + 1, :] = listed_row.astype(jnp.int32)
    table_ref[TOP : TOP + 1, :] = listed_top.astype(jnp.int32)
    table_ref[COUNT : COUNT + 1, :] = jnp.broadcast_to(
        count.astype(jnp.int32), (1, nb)
    )
    owner_ref[...] = piv_col[:, :LANES].astype(jnp.int32) // row_dev


def gather_kernel(table_ref, matrix_ref, out_ref):
    nb = out_ref.shape[0]

    @pl.loop(0, nb, step=8)
    def _(base):
        for k in range(8):
            j = base + k
            out_ref[pl.ds(j, 1), :] = matrix_ref[pl.ds(table_ref[PICK, j], 1), :]


def merge(where_ref, owner_ref, held_ref, came_ref, merged_ref, log):
    mine, theirs = where_ref[0] >> log, (where_ref[0] >> log) ^ 1
    group = owner_ref[...] >> log
    take = (group == theirs) | ((theirs == 0) & (group != mine))
    for q in range(held_ref.shape[1] // LANES):
        lane = slice(q * LANES, (q + 1) * LANES)
        merged_ref[:, lane] = jnp.where(take, came_ref[:, lane], held_ref[:, lane])


def merge_kernel(where_ref, owner_ref, held_ref, came_ref, merged_ref, *, log):
    merge(where_ref, owner_ref, held_ref, came_ref, merged_ref, log)


def split(x):
    hi = x.astype(jnp.bfloat16)
    return hi, (x - hi.astype(jnp.float32)).astype(jnp.bfloat16)


def product(a, b):
    dot = functools.partial(jnp.dot, preferred_element_type=jnp.float32)
    return dot(a[1], b[0]) + dot(a[0], b[1]) + dot(a[0], b[0])


def factor_kernel(
    where_ref, owner_ref, held_ref, came_ref, lower_ref, upper_ref, weights_ref, top_ref,
    new_top, *, log,
):
    nb = held_ref.shape[0]
    merge(where_ref, owner_ref, held_ref, came_ref, new_top, log)
    u = product(split(lower_ref[...]), split(new_top[...]))
    top_ref[...] = u
    weights_ref[...] = product(split(upper_ref[...]), split(u))

    @pl.when(where_ref[1] == 0)
    def _():
        top_ref[:, :nb] = new_top[:, :nb]
        weights_ref[:, :nb] = -upper_ref[...]


def fetch(choice_ref, bufs, place, sem, n_cols, parts, pairs):
    for i in range(pairs):
        for h in range(2):
            for b in sorted({arrival(p, i, h, n_cols, parts) for p in range(1, n_cols)}):
                @pl.when(choice_ref[2 * i + h] == b)
                def _():
                    pltpu.make_async_copy(bufs[b], place(i, h), sem).start()


def old_top_kernel(
    where_ref, choice_ref, *refs, used, n_cols, parts, pairs
):
    own, bufs, top_ref = refs[: 2 * pairs], dict(zip(used, refs[2 * pairs :])), refs[-1]
    chunk = own[0].shape[0]
    for k in range(2 * pairs):
        span = slice(k * chunk, (k + 1) * chunk)

        @pl.when(where_ref[1] == 0)
        def _():
            top_ref[span, :] = own[k][...]

        for b in sorted({arrival(p, k // 2, k % 2, n_cols, parts) for p in range(1, n_cols)}):
            @pl.when((where_ref[1] > 0) & (choice_ref[k] == b))
            def _():
                top_ref[span, :] = bufs[b][...]


def final_kernel(
    where_ref, table_ref, choice_ref, weights_ref, top_ref, matrix_ref,
    *refs, n_bufs, n_tops, n_cols, parts, block,
):
    bufs, refs = refs[:n_bufs], refs[n_bufs:]
    tops, slots, refs = refs[:n_tops], refs[n_tops : 2 * n_tops], refs[2 * n_tops :]
    out_ref, mat, pan, low, displaced, w_hi, w_lo, result, in_sem, low_sem, mat_sem, out_sem = refs
    rows, cols = matrix_ref.shape
    nb = weights_ref.shape[0]
    chunk = rows // (2 * parts)
    row = where_ref[0]
    first_row, first_col = row == 0, where_ref[1] == 0

    load = pltpu.make_async_copy(matrix_ref, mat, mat_sem)
    load.start()
    whole_panel = pltpu.make_async_copy(matrix_ref.at[:, pl.ds(0, nb)], pan, in_sem)

    @pl.when(first_col)
    def _():
        whole_panel.start()

    @pl.when(jnp.logical_not(first_col))
    def _():
        fetch(
            choice_ref, bufs, lambda i, h: pan.at[pl.ds((2 * i + h) * chunk, chunk), :],
            in_sem, n_cols, parts, parts,
        )

    for log in range(n_tops):
        @pl.when((row & ((2 << log) - 1)) == (1 << log))
        def _():
            pltpu.make_async_copy(tops[log], low, low_sem).start()

        @pl.when((row >> log) == 1)
        def _():
            pltpu.make_async_copy(slots[log], displaced, low_sem).start()

    w = weights_ref[...]
    w_hi[...] = w.astype(jnp.bfloat16)
    w_lo[...] = (w - w_hi[...].astype(jnp.float32)).astype(jnp.bfloat16)

    whole_panel.wait()
    load.wait()
    count = table_ref[COUNT, 0]

    def swap(from_mat, from_pan):
        def body(k, _):
            to = table_ref[ROW, k]
            mat[pl.ds(to, 1), :] = from_mat[pl.ds(table_ref[FROM, k], 1), :]
            pan[pl.ds(to, 1), :] = from_pan[pl.ds(table_ref[TOP, k], 1), :]
            return 0

        lax.fori_loop(0, count, body, 0)

    @pl.when(first_row)
    def _():
        swap(mat, pan)

    @pl.when(jnp.logical_not(first_row))
    def _():
        pltpu.make_async_copy(tops[0], low, low_sem).wait()
        pltpu.make_async_copy(slots[0], displaced, low_sem).wait()
        swap(displaced, low)

    @pl.when(first_col)
    def _():
        mat[:, :nb] = jnp.zeros((rows, nb), jnp.float32)

    copies = []
    for b in range(rows // block):
        span = pl.ds(b * block, block)

        def update():
            p = pan[span, :]
            p_hi = p.astype(jnp.bfloat16)
            p_lo = (p - p_hi.astype(jnp.float32)).astype(jnp.bfloat16)
            dot = functools.partial(jnp.dot, preferred_element_type=jnp.float32)
            total = dot(p_lo, w_hi[...]) + dot(p_hi, w_lo[...]) + dot(p_hi, w_hi[...])
            result[span, :] = mat[span, :] - total

        if (b + 1) * block <= nb:
            pl.when(jnp.logical_not(first_row))(update)

            @pl.when(first_row)
            def _():
                result[span, :] = top_ref[span, :]
        else:
            update()
        copy = pltpu.make_async_copy(result.at[span, :], out_ref.at[span, :], out_sem)
        copy.start()
        copies.append(copy)
    for copy in copies:
        copy.wait()


LAG = 2


def steps(n_cols, parts):
    depth = n_cols // 2
    return parts + LAG * (depth - 1), max(2 * parts, parts + LAG * depth)


def arrival(p, i, h, n_cols, parts):
    z, y = divmod(p, 2)
    cross = steps(n_cols, parts)[0]
    if z == 0:
        return cross + i + h * parts
    if y == 0:
        return cross + i + LAG * (z + 1) if h == 0 else i + LAG * (z - 1)
    return i + LAG * z if h == 0 else cross + i + LAG * z


def spread(pieces, col, n_cols, riders):
    parts = len(pieces)
    n_chain, n_cross = steps(n_cols, parts)
    along = [(p, p + 2) for p in range(n_cols - 2)]
    across = [(0, 1)] + [(p, p ^ 1) for p in range(2, n_cols)]
    chain, cross = [], []
    waiting = [(rider, next(rider)(chain, cross)) for rider in riders]
    for s in range(n_cross):
        ahead = pieces[min(s, parts - 1)][1]
        aside = pieces[s][0] if s < parts else pieces[min(s - parts, parts - 1)][1]
        if s >= LAG:
            came = chain[s - LAG] if s - LAG < n_chain else chain[-1]
            due = [k for k, (_, (at, _)) in enumerate(waiting) if at == s]
            tied = [waiting[k][1][1] for k in due]
            (came, fed), tied = lax.optimization_barrier(((came, cross[s - LAG]), tied))
            ahead = jnp.where(col == 0, ahead, jnp.where(col == 1, fed, came))
            aside = jnp.where(col == 0, aside, came)
        if s < n_chain:
            chain.append(lax.ppermute(ahead, "pcol", along))
        cross.append(lax.ppermute(aside, "pcol", across))
        if s >= LAG:
            for k, values in zip(due, tied):
                rider = waiting[k][0]
                waiting[k] = (rider, resume(rider, values, chain, cross))
    results = []
    for rider, (at, values) in waiting:
        while at != DONE:
            at, values = resume(rider, values, chain, cross)
        results.append(values)
    return chain, cross, results


DONE = -1


def resume(rider, values, chain, cross):
    return rider.send(values)(chain, cross)


def give(at, values):
    return lambda chain, cross: (at, values)


def local(matrix, pivots, lower_inverse, upper_inverse, *, n_rows, n_cols, parts):
    row_dev, cols = matrix.shape
    nb = pivots.shape[0]
    f32 = jnp.float32
    row, col = lax.axis_index("prow"), lax.axis_index("pcol")
    here = jnp.stack([row, col]).astype(jnp.int32)

    chunk = row_dev // (2 * parts)
    flat = [
        lax.slice(matrix, (k * chunk, 0), ((k + 1) * chunk, nb)) for k in range(2 * parts)
    ]
    flat = flat[:2] + list(lax.optimization_barrier(tuple(flat[2:])))
    choice = jnp.asarray(
        [
            [0] * (2 * parts) if p == 0 else
            [arrival(p, i, h, n_cols, parts) for i in range(parts) for h in range(2)]
            for p in range(n_cols)
        ],
        jnp.int32,
    )[col]

    pairs = nb // (2 * chunk)
    used = sorted({
        arrival(p, i, h, n_cols, parts)
        for p in range(1, n_cols) for i in range(pairs) for h in range(2)
    })
    n_chain = steps(n_cols, parts)[0]
    last = max(b - n_chain if b >= n_chain else b for b in used)

    def old_top_rider():
        at = last + LAG

        def start(chain, cross):
            return at, [chain[b] if b < n_chain else cross[b - n_chain] for b in used]

        arrived = yield give(at - 1, ())
        arrived = yield start
        old_top = call(
            functools.partial(
                old_top_kernel, used=used, n_cols=n_cols, parts=parts, pairs=pairs
            ),
            jax.ShapeDtypeStruct((nb, nb), f32),
            [SMEM, SMEM] + [VMEM] * (2 * pairs + len(used)), VMEM,
        )(here, choice, *flat[: 2 * pairs], *arrived)
        tops = []
        d = n_rows // 2
        while d:
            came = lax.ppermute(old_top, "prow", [(p, p + d) for p in range(0, n_rows, 2 * d)])
            if d > 1:
                at += 2
                came = yield give(at, came)
                old_top = jnp.where(row % (2 * d) == d, came, old_top)
            tops.insert(0, came)
            d //= 2
        yield give(DONE, tops)

    slot = jax.ShapeDtypeStruct((nb, cols), f32)

    def exchange_rider():
        table, owner = yield give(2, call(
            functools.partial(index_kernel, row_dev=row_dev),
            (jax.ShapeDtypeStruct((8, nb), jnp.int32), jax.ShapeDtypeStruct((nb, LANES), jnp.int32)),
            [SMEM, VMEM], (VMEM, VMEM),
        )(here, pivots.reshape(1, nb)))
        held = yield give(3, call(gather_kernel, slot, [SMEM, VMEM], VMEM)(table, matrix))
        at = 5
        slots = []
        for log in range(n_rows.bit_length() - 1):
            d = 1 << log
            came = lax.ppermute(held, "prow", [(p, p ^ d) for p in range(n_rows)])
            came = yield give(at, came)
            slots.append(came)
            if 2 * d < n_rows:
                held = call(
                    functools.partial(merge_kernel, log=log), slot, [SMEM] + [VMEM] * 3, VMEM
                )(here, owner, held, came)
                held = yield give(at + 1, held)
                at += 5
        weights, top = yield give(at + 2, call(
            functools.partial(factor_kernel, log=log), (slot,) * 2,
            [SMEM] + [VMEM] * 5, (VMEM,) * 2, [pltpu.VMEM((nb, cols), f32)],
            flops=4 * nb * nb * cols * 3,
        )(here, owner, held, came, lower_inverse, upper_inverse))
        yield give(DONE, (table, slots, weights, top))

    chain, cross, (tops, (table, slots, weights, top)) = spread(
        [(flat[2 * i], flat[2 * i + 1]) for i in range(parts)], col, n_cols,
        [old_top_rider(), exchange_rider()],
    )
    bufs = chain + cross

    return call(
        functools.partial(
            final_kernel, n_bufs=len(bufs), n_tops=len(tops), n_cols=n_cols, parts=parts,
            block=256,
        ),
        jax.ShapeDtypeStruct(matrix.shape, f32),
        [SMEM, SMEM, SMEM, VMEM, VMEM, ANY] + [ANY] * (len(bufs) + 2 * len(tops)),
        ANY,
        [
            pltpu.VMEM((row_dev, cols), f32),
            pltpu.VMEM((row_dev, nb), f32),
            pltpu.VMEM((nb, nb), f32),
            pltpu.VMEM((nb, cols), f32),
            pltpu.VMEM((nb, cols), jnp.bfloat16),
            pltpu.VMEM((nb, cols), jnp.bfloat16),
            pltpu.VMEM((row_dev, cols), f32),
        ] + [pltpu.SemaphoreType.DMA] * 4,
        vmem=30 << 20,
        flops=2 * row_dev * nb * cols * 3,
        moved=4 * row_dev * (2 * cols + nb),
    )(here, table, choice, weights, top, matrix, *bufs, *tops, *slots)


def solution(mesh):
    n_rows, n_cols = mesh.shape["prow"], mesh.shape["pcol"]
    return jax.shard_map(
        functools.partial(local, n_rows=n_rows, n_cols=n_cols, parts=8),
        mesh=mesh,
        in_specs=(P("prow", "pcol"), P(), P(), P()),
        out_specs=P("prow", "pcol"),
        check_vma=False,
    )
```

```python
import functools

import jax
import jax.numpy as jnp
from jax import lax
from jax.experimental import pallas as pl
from jax.experimental.pallas import tpu as pltpu
from jax.sharding import PartitionSpec as P

VMEM = pl.BlockSpec(memory_space=pltpu.VMEM)
SMEM = pl.BlockSpec(memory_space=pltpu.SMEM)
ANY = pl.BlockSpec(memory_space=pl.ANY)
LANES = 128
PICK, FROM, ROW, COUNT, TOP = 0, 1, 2, 3, 4


def call(kernel, out, ins, outs, scratch=(), vmem=10 << 20, flops=0, moved=0):
    return pl.pallas_call(
        kernel,
        out_shape=out,
        in_specs=ins,
        out_specs=outs,
        scratch_shapes=list(scratch),
        compiler_params=pltpu.CompilerParams(vmem_limit_bytes=vmem),
        cost_estimate=pl.CostEstimate(
            flops=flops, bytes_accessed=moved, transcendentals=0
        ),
    )


def index_kernel(where_ref, pivots_ref, table_ref, owner_ref, *, row_dev):
    nb = pivots_ref.shape[1]
    start = where_ref[0] * row_dev
    first = where_ref[0] == 0
    down = lax.broadcasted_iota(jnp.int32, (nb, nb), 0)
    across = lax.broadcasted_iota(jnp.int32, (nb, nb), 1)
    piv_row = jnp.broadcast_to(pivots_ref[...], (nb, nb))

    def column(full):
        return jnp.sum(jnp.where(down == across, full, 0.0), axis=1, keepdims=True)

    piv_f = piv_row.astype(jnp.float32)
    piv_col = jnp.broadcast_to(column(piv_f), (nb, nb))
    upto = (down <= across).astype(jnp.bfloat16)
    below = (piv_row >= nb).astype(jnp.float32)
    vacancy = jnp.dot(
        below[:8].astype(jnp.bfloat16), upto, preferred_element_type=jnp.float32
    )[:1]
    taken = jnp.max((piv_row == down).astype(jnp.float32), axis=1, keepdims=True)
    freed = jnp.broadcast_to(1.0 - taken, (nb, LANES))
    rank = jnp.dot(
        (across <= down).astype(jnp.bfloat16),
        freed.astype(jnp.bfloat16),
        preferred_element_type=jnp.float32,
    )[:, :1]
    down_f = down.astype(jnp.float32)
    pair = (rank == vacancy) & (freed[:, :1] > 0.5)
    source = jnp.sum(jnp.where(pair, down_f, 0.0), axis=0, keepdims=True)
    source_col = jnp.broadcast_to(column(jnp.broadcast_to(source, (nb, nb))), (nb, nb))

    own_row = (pivots_ref[...] >= start) & (pivots_ref[...] < start + row_dev)
    pick = jnp.where(own_row, pivots_ref[...] - start, source.astype(jnp.int32))
    moved_row = (own_row & (pivots_ref[...] >= nb)).astype(jnp.float32)
    start_f = start.astype(jnp.float32)
    moved_col = (
        (piv_col >= start_f) & (piv_col < start_f + row_dev) & (piv_col >= nb)
    )
    order = jnp.sum(
        jnp.where(piv_f < piv_col, jnp.broadcast_to(moved_row, (nb, nb)), 0.0),
        axis=1,
        keepdims=True,
    )
    placed = moved_col & (order == across.astype(jnp.float32))
    origin = jnp.where(first, source_col, down_f)
    listed_from = jnp.sum(jnp.where(placed, origin, 0.0), axis=0, keepdims=True)
    listed_row = jnp.sum(
        jnp.where(placed, piv_col - start_f, 0.0), axis=0, keepdims=True
    )
    listed_top = jnp.sum(jnp.where(placed, source_col, 0.0), axis=0, keepdims=True)
    count = jnp.sum(moved_row, axis=1, keepdims=True)
    table_ref[...] = jnp.zeros_like(table_ref)
    table_ref[PICK : PICK + 1, :] = pick
    table_ref[FROM : FROM + 1, :] = listed_from.astype(jnp.int32)
    table_ref[ROW : ROW + 1, :] = listed_row.astype(jnp.int32)
    table_ref[TOP : TOP + 1, :] = listed_top.astype(jnp.int32)
    table_ref[COUNT : COUNT + 1, :] = jnp.broadcast_to(
        count.astype(jnp.int32), (1, nb)
    )
    owner_ref[...] = piv_col[:, :LANES].astype(jnp.int32) // row_dev


def gather_kernel(table_ref, matrix_ref, out_ref):
    nb = out_ref.shape[0]

    @pl.loop(0, nb, step=8)
    def _(base):
        for k in range(8):
            j = base + k
            out_ref[pl.ds(j, 1), :] = matrix_ref[pl.ds(table_ref[PICK, j], 1), :]


def merge(where_ref, owner_ref, held_ref, came_ref, merged_ref, log):
    mine, theirs = where_ref[0] >> log, (where_ref[0] >> log) ^ 1
    group = owner_ref[...] >> log
    take = (group == theirs) | ((theirs == 0) & (group != mine))
    for q in range(held_ref.shape[1] // LANES):
        lane = slice(q * LANES, (q + 1) * LANES)
        merged_ref[:, lane] = jnp.where(take, came_ref[:, lane], held_ref[:, lane])


def merge_kernel(where_ref, owner_ref, held_ref, came_ref, merged_ref, *, log):
    merge(where_ref, owner_ref, held_ref, came_ref, merged_ref, log)


def split(x):
    hi = x.astype(jnp.bfloat16)
    return hi, (x - hi.astype(jnp.float32)).astype(jnp.bfloat16)


def product(a, b):
    dot = functools.partial(jnp.dot, preferred_element_type=jnp.float32)
    return dot(a[1], b[0]) + dot(a[0], b[1]) + dot(a[0], b[0])


def factor_kernel(
    where_ref, owner_ref, held_ref, came_ref, lower_ref, upper_ref, weights_ref, top_ref,
    new_top, *, log,
):
    nb = held_ref.shape[0]
    merge(where_ref, owner_ref, held_ref, came_ref, new_top, log)
    u = product(split(lower_ref[...]), split(new_top[...]))
    top_ref[...] = u
    weights_ref[...] = product(split(upper_ref[...]), split(u))

    @pl.when(where_ref[1] == 0)
    def _():
        top_ref[:, :nb] = new_top[:, :nb]
        weights_ref[:, :nb] = -upper_ref[...]


def fetch(choice_ref, bufs, place, sem, n_cols, parts, pairs):
    for i in range(pairs):
        for h in range(2):
            for b in sorted({arrival(p, i, h, n_cols, parts) for p in range(1, n_cols)}):
                @pl.when(choice_ref[2 * i + h] == b)
                def _():
                    pltpu.make_async_copy(bufs[b], place(i, h), sem).start()


def old_top_kernel(where_ref, choice_ref, matrix_ref, *refs, used, n_cols, parts, pairs):
    bufs, top_ref, sem = dict(zip(used, refs)), refs[-2], refs[-1]
    nb = top_ref.shape[0]
    chunk = nb // (2 * pairs)
    from_matrix = pltpu.make_async_copy(
        matrix_ref.at[pl.ds(0, nb), pl.ds(0, nb)], top_ref, sem
    )

    @pl.when(where_ref[0] == 0)
    def _():
        @pl.when(where_ref[1] == 0)
        def _():
            from_matrix.start()

        @pl.when(where_ref[1] > 0)
        def _():
            fetch(
                choice_ref, bufs,
                lambda i, h: top_ref.at[pl.ds((2 * i + h) * chunk, chunk), :],
                sem, n_cols, parts, pairs,
            )

        from_matrix.wait()


def final_kernel(
    where_ref, table_ref, choice_ref, weights_ref, top_ref, matrix_ref,
    *refs, n_bufs, n_tops, n_cols, parts, block,
):
    bufs, refs = refs[:n_bufs], refs[n_bufs:]
    tops, slots, refs = refs[:n_tops], refs[n_tops : 2 * n_tops], refs[2 * n_tops :]
    out_ref, mat, pan, low, displaced, w_hi, w_lo, result, in_sem, low_sem, mat_sem, out_sem = refs
    rows, cols = matrix_ref.shape
    nb = weights_ref.shape[0]
    chunk = rows // (2 * parts)
    row = where_ref[0]
    first_row, first_col = row == 0, where_ref[1] == 0

    load = pltpu.make_async_copy(matrix_ref, mat, mat_sem)
    load.start()
    whole_panel = pltpu.make_async_copy(matrix_ref.at[:, pl.ds(0, nb)], pan, in_sem)

    @pl.when(first_col)
    def _():
        whole_panel.start()

    @pl.when(jnp.logical_not(first_col))
    def _():
        fetch(
            choice_ref, bufs, lambda i, h: pan.at[pl.ds((2 * i + h) * chunk, chunk), :],
            in_sem, n_cols, parts, parts,
        )

    for log in range(n_tops):
        @pl.when((row & ((2 << log) - 1)) == (1 << log))
        def _():
            pltpu.make_async_copy(tops[log], low, low_sem).start()

        @pl.when((row >> log) == 1)
        def _():
            pltpu.make_async_copy(slots[log], displaced, low_sem).start()

    w = weights_ref[...]
    w_hi[...] = w.astype(jnp.bfloat16)
    w_lo[...] = (w - w_hi[...].astype(jnp.float32)).astype(jnp.bfloat16)

    whole_panel.wait()
    load.wait()
    count = table_ref[COUNT, 0]

    def swap(from_mat, from_pan):
        def body(k, _):
            to = table_ref[ROW, k]
            mat[pl.ds(to, 1), :] = from_mat[pl.ds(table_ref[FROM, k], 1), :]
            pan[pl.ds(to, 1), :] = from_pan[pl.ds(table_ref[TOP, k], 1), :]
            return 0

        lax.fori_loop(0, count, body, 0)

    @pl.when(first_row)
    def _():
        swap(mat, pan)

    @pl.when(jnp.logical_not(first_row))
    def _():
        pltpu.make_async_copy(tops[0], low, low_sem).wait()
        pltpu.make_async_copy(slots[0], displaced, low_sem).wait()
        swap(displaced, low)

    @pl.when(first_col)
    def _():
        mat[:, :nb] = jnp.zeros((rows, nb), jnp.float32)

    copies = []
    for b in range(rows // block):
        span = pl.ds(b * block, block)

        def update():
            p = pan[span, :]
            p_hi = p.astype(jnp.bfloat16)
            p_lo = (p - p_hi.astype(jnp.float32)).astype(jnp.bfloat16)
            dot = functools.partial(jnp.dot, preferred_element_type=jnp.float32)
            total = dot(p_lo, w_hi[...]) + dot(p_hi, w_lo[...]) + dot(p_hi, w_hi[...])
            result[span, :] = mat[span, :] - total

        if (b + 1) * block <= nb:
            pl.when(jnp.logical_not(first_row))(update)

            @pl.when(first_row)
            def _():
                result[span, :] = top_ref[span, :]
        else:
            update()
        copy = pltpu.make_async_copy(result.at[span, :], out_ref.at[span, :], out_sem)
        copy.start()
        copies.append(copy)
    for copy in copies:
        copy.wait()


LAG = 2


def steps(n_cols, parts):
    depth = n_cols // 2
    return parts + LAG * (depth - 1), max(2 * parts, parts + LAG * depth)


def arrival(p, i, h, n_cols, parts):
    z, y = divmod(p, 2)
    cross = steps(n_cols, parts)[0]
    if z == 0:
        return cross + i + h * parts
    if y == 0:
        return cross + i + LAG * (z + 1) if h == 0 else i + LAG * (z - 1)
    return i + LAG * z if h == 0 else cross + i + LAG * z


def spread(pieces, col, n_cols, riders):
    parts = len(pieces)
    n_chain, n_cross = steps(n_cols, parts)
    along = [(p, p + 2) for p in range(n_cols - 2)]
    across = [(0, 1)] + [(p, p ^ 1) for p in range(2, n_cols)]
    chain, cross = [], []
    waiting = [(rider, next(rider)(chain, cross)) for rider in riders]
    for s in range(n_cross):
        ahead = pieces[min(s, parts - 1)][1]
        aside = pieces[s][0] if s < parts else pieces[min(s - parts, parts - 1)][1]
        if s >= LAG:
            came = chain[s - LAG] if s - LAG < n_chain else chain[-1]
            due = [k for k, (_, (at, _)) in enumerate(waiting) if at == s]
            tied = [waiting[k][1][1] for k in due]
            (came, fed), tied = lax.optimization_barrier(((came, cross[s - LAG]), tied))
            ahead = jnp.where(col == 0, ahead, jnp.where(col == 1, fed, came))
            aside = jnp.where(col == 0, aside, came)
        if s < n_chain:
            chain.append(lax.ppermute(ahead, "pcol", along))
        cross.append(lax.ppermute(aside, "pcol", across))
        if s >= LAG:
            for k, values in zip(due, tied):
                rider = waiting[k][0]
                waiting[k] = (rider, resume(rider, values, chain, cross))
    results = []
    for rider, (at, values) in waiting:
        while at != DONE:
            at, values = resume(rider, values, chain, cross)
        results.append(values)
    return chain, cross, results


DONE = -1


def resume(rider, values, chain, cross):
    return rider.send(values)(chain, cross)


def give(at, values):
    return lambda chain, cross: (at, values)


def local(matrix, pivots, lower_inverse, upper_inverse, *, n_rows, n_cols, parts):
    row_dev, cols = matrix.shape
    nb = pivots.shape[0]
    f32 = jnp.float32
    row, col = lax.axis_index("prow"), lax.axis_index("pcol")
    here = jnp.stack([row, col]).astype(jnp.int32)

    chunk = row_dev // (2 * parts)
    flat = [
        lax.slice(matrix, (k * chunk, 0), ((k + 1) * chunk, nb)) for k in range(2 * parts)
    ]
    flat = flat[:2] + list(lax.optimization_barrier(tuple(flat[2:])))
    choice = jnp.asarray(
        [
            [0] * (2 * parts) if p == 0 else
            [arrival(p, i, h, n_cols, parts) for i in range(parts) for h in range(2)]
            for p in range(n_cols)
        ],
        jnp.int32,
    )[col]

    pairs = nb // (2 * chunk)
    used = sorted({
        arrival(p, i, h, n_cols, parts)
        for p in range(1, n_cols) for i in range(pairs) for h in range(2)
    })
    n_chain = steps(n_cols, parts)[0]
    last = max(b - n_chain if b >= n_chain else b for b in used)

    def old_top_rider():
        at = last + LAG

        def start(chain, cross):
            return at, [chain[b] if b < n_chain else cross[b - n_chain] for b in used]

        arrived = yield give(at - 1, ())
        arrived = yield start
        old_top = call(
            functools.partial(
                old_top_kernel, used=used, n_cols=n_cols, parts=parts, pairs=pairs
            ),
            jax.ShapeDtypeStruct((nb, nb), f32),
            [SMEM, SMEM, ANY] + [ANY] * len(used), ANY, [pltpu.SemaphoreType.DMA],
            vmem=4 << 20,
        )(here, choice, matrix, *arrived)
        tops = []
        d = n_rows // 2
        while d:
            came = lax.ppermute(old_top, "prow", [(p, p + d) for p in range(0, n_rows, 2 * d)])
            if d > 1:
                at += 2
                came = yield give(at, came)
                old_top = jnp.where(row % (2 * d) == d, came, old_top)
            tops.insert(0, came)
            d //= 2
        yield give(DONE, tops)

    slot = jax.ShapeDtypeStruct((nb, cols), f32)

    def exchange_rider():
        table, owner = yield give(2, call(
            functools.partial(index_kernel, row_dev=row_dev),
            (jax.ShapeDtypeStruct((8, nb), jnp.int32), jax.ShapeDtypeStruct((nb, LANES), jnp.int32)),
            [SMEM, VMEM], (VMEM, VMEM),
        )(here, pivots.reshape(1, nb)))
        held = yield give(3, call(gather_kernel, slot, [SMEM, VMEM], VMEM)(table, matrix))
        at = 5
        slots = []
        for log in range(n_rows.bit_length() - 1):
            d = 1 << log
            came = lax.ppermute(held, "prow", [(p, p ^ d) for p in range(n_rows)])
            came = yield give(at, came)
            slots.append(came)
            if 2 * d < n_rows:
                held = call(
                    functools.partial(merge_kernel, log=log), slot, [SMEM] + [VMEM] * 3, VMEM
                )(here, owner, held, came)
                held = yield give(at + 1, held)
                at += 5
        weights, top = yield give(at + 2, call(
            functools.partial(factor_kernel, log=log), (slot,) * 2,
            [SMEM] + [VMEM] * 5, (VMEM,) * 2, [pltpu.VMEM((nb, cols), f32)],
            vmem=16 << 20, flops=4 * nb * nb * cols * 3,
        )(here, owner, held, came, lower_inverse, upper_inverse))
        yield give(DONE, (table, slots, weights, top))

    chain, cross, (tops, (table, slots, weights, top)) = spread(
        [(flat[2 * i], flat[2 * i + 1]) for i in range(parts)], col, n_cols,
        [old_top_rider(), exchange_rider()],
    )
    bufs = chain + cross

    return call(
        functools.partial(
            final_kernel, n_bufs=len(bufs), n_tops=len(tops), n_cols=n_cols, parts=parts,
            block=256,
        ),
        jax.ShapeDtypeStruct(matrix.shape, f32),
        [SMEM, SMEM, SMEM, VMEM, VMEM, ANY] + [ANY] * (len(bufs) + 2 * len(tops)),
        ANY,
        [
            pltpu.VMEM((row_dev, cols), f32),
            pltpu.VMEM((row_dev, nb), f32),
            pltpu.VMEM((nb, nb), f32),
            pltpu.VMEM((nb, cols), f32),
            pltpu.VMEM((nb, cols), jnp.bfloat16),
            pltpu.VMEM((nb, cols), jnp.bfloat16),
            pltpu.VMEM((row_dev, cols), f32),
        ] + [pltpu.SemaphoreType.DMA] * 4,
        vmem=30 << 20,
        flops=2 * row_dev * nb * cols * 3,
        moved=4 * row_dev * (2 * cols + nb),
    )(here, table, choice, weights, top, matrix, *bufs, *tops, *slots)


def solution(mesh):
    n_rows, n_cols = mesh.shape["prow"], mesh.shape["pcol"]
    return jax.shard_map(
        functools.partial(local, n_rows=n_rows, n_cols=n_cols, parts=8),
        mesh=mesh,
        in_specs=(P("prow", "pcol"), P(), P(), P()),
        out_specs=P("prow", "pcol"),
        check_vma=False,
    )
```

```python
import functools

import jax
import jax.numpy as jnp
from jax import lax
from jax.experimental import pallas as pl
from jax.experimental.pallas import tpu as pltpu
from jax.sharding import PartitionSpec as P

VMEM = pl.BlockSpec(memory_space=pltpu.VMEM)
SMEM = pl.BlockSpec(memory_space=pltpu.SMEM)
ANY = pl.BlockSpec(memory_space=pl.ANY)
LANES = 128
PICK, FROM, ROW, COUNT, TOP = 0, 1, 2, 3, 4


def call(kernel, out, ins, outs, scratch=(), vmem=16 << 20, flops=0, moved=0):
    return pl.pallas_call(
        kernel,
        out_shape=out,
        in_specs=ins,
        out_specs=outs,
        scratch_shapes=list(scratch),
        compiler_params=pltpu.CompilerParams(vmem_limit_bytes=vmem),
        cost_estimate=pl.CostEstimate(
            flops=flops, bytes_accessed=moved, transcendentals=0
        ),
    )


def index_kernel(where_ref, pivots_ref, table_ref, owner_ref, *, row_dev):
    nb = pivots_ref.shape[1]
    start = where_ref[0] * row_dev
    first = where_ref[0] == 0
    down = lax.broadcasted_iota(jnp.int32, (nb, nb), 0)
    across = lax.broadcasted_iota(jnp.int32, (nb, nb), 1)
    piv_row = jnp.broadcast_to(pivots_ref[...], (nb, nb))

    def column(full):
        return jnp.sum(jnp.where(down == across, full, 0.0), axis=1, keepdims=True)

    piv_f = piv_row.astype(jnp.float32)
    piv_col = jnp.broadcast_to(column(piv_f), (nb, nb))
    upto = (down <= across).astype(jnp.bfloat16)
    below = (piv_row >= nb).astype(jnp.float32)
    vacancy = jnp.dot(
        below[:8].astype(jnp.bfloat16), upto, preferred_element_type=jnp.float32
    )[:1]
    taken = jnp.max((piv_row == down).astype(jnp.float32), axis=1, keepdims=True)
    freed = jnp.broadcast_to(1.0 - taken, (nb, LANES))
    rank = jnp.dot(
        (across <= down).astype(jnp.bfloat16),
        freed.astype(jnp.bfloat16),
        preferred_element_type=jnp.float32,
    )[:, :1]
    down_f = down.astype(jnp.float32)
    pair = (rank == vacancy) & (freed[:, :1] > 0.5)
    source = jnp.sum(jnp.where(pair, down_f, 0.0), axis=0, keepdims=True)
    source_col = jnp.broadcast_to(column(jnp.broadcast_to(source, (nb, nb))), (nb, nb))

    own_row = (pivots_ref[...] >= start) & (pivots_ref[...] < start + row_dev)
    pick = jnp.where(own_row, pivots_ref[...] - start, source.astype(jnp.int32))
    moved_row = (own_row & (pivots_ref[...] >= nb)).astype(jnp.float32)
    start_f = start.astype(jnp.float32)
    moved_col = (
        (piv_col >= start_f) & (piv_col < start_f + row_dev) & (piv_col >= nb)
    )
    order = jnp.sum(
        jnp.where(piv_f < piv_col, jnp.broadcast_to(moved_row, (nb, nb)), 0.0),
        axis=1,
        keepdims=True,
    )
    placed = moved_col & (order == across.astype(jnp.float32))
    origin = jnp.where(first, source_col, down_f)
    listed_from = jnp.sum(jnp.where(placed, origin, 0.0), axis=0, keepdims=True)
    listed_row = jnp.sum(
        jnp.where(placed, piv_col - start_f, 0.0), axis=0, keepdims=True
    )
    listed_top = jnp.sum(jnp.where(placed, source_col, 0.0), axis=0, keepdims=True)
    count = jnp.sum(moved_row, axis=1, keepdims=True)
    table_ref[...] = jnp.zeros_like(table_ref)
    table_ref[PICK : PICK + 1, :] = pick
    table_ref[FROM : FROM + 1, :] = listed_from.astype(jnp.int32)
    table_ref[ROW : ROW + 1, :] = listed_row.astype(jnp.int32)
    table_ref[TOP : TOP + 1, :] = listed_top.astype(jnp.int32)
    table_ref[COUNT : COUNT + 1, :] = jnp.broadcast_to(
        count.astype(jnp.int32), (1, nb)
    )
    owner_ref[...] = piv_col[:, :LANES].astype(jnp.int32) // row_dev


def gather_kernel(table_ref, matrix_ref, out_ref):
    nb = out_ref.shape[0]

    @pl.loop(0, nb, step=8)
    def _(base):
        for k in range(8):
            j = base + k
            out_ref[pl.ds(j, 1), :] = matrix_ref[pl.ds(table_ref[PICK, j], 1), :]


def merge_kernel(where_ref, owner_ref, held_ref, *refs, log, halves):
    arrived, (merged_ref, half_ref) = refs[: 2 if halves else 1], refs[-2:]
    me = where_ref[0]
    mine, theirs = me >> log, (me >> log) ^ 1
    odd = me & 1
    nb, cols = held_ref.shape
    half = nb // 2

    def merge(rows, piece):
        group = owner_ref[rows, :] >> log
        take = (group == theirs) | ((theirs == 0) & (group != mine))
        for q in range(cols // LANES):
            lane = slice(q * LANES, (q + 1) * LANES)
            merged_ref[rows, lane] = jnp.where(take, piece[:, lane], held_ref[rows, lane])

    low, high = slice(0, half), slice(half, nb)
    if halves:
        @pl.when(odd == 0)
        def _():
            merge(low, arrived[0])
            merge(high, arrived[1])

        @pl.when(odd == 1)
        def _():
            merge(low, arrived[1])
            merge(high, arrived[0])
    else:
        merge(slice(0, nb), arrived[0])

    @pl.when(odd == 0)
    def _():
        half_ref[...] = merged_ref[low, :]

    @pl.when(odd == 1)
    def _():
        half_ref[...] = merged_ref[high, :]


def split(x):
    hi = x.astype(jnp.bfloat16)
    return hi, (x - hi.astype(jnp.float32)).astype(jnp.bfloat16)


def product(a, b):
    dot = functools.partial(jnp.dot, preferred_element_type=jnp.float32)
    return dot(a[1], b[0]) + dot(a[0], b[1]) + dot(a[0], b[0])


def factor_kernel(
    where_ref, owner_ref, held_ref, one_ref, two_ref, before_ref, lower_ref, upper_ref,
    weights_ref, top_ref, displaced_ref, new_top, *, log,
):
    me = where_ref[0]
    mine, theirs = me >> log, (me >> log) ^ 1
    nb, cols = held_ref.shape
    half = nb // 2

    def merge(rows, piece):
        group = owner_ref[rows, :] >> log
        take = (group == theirs) | ((theirs == 0) & (group != mine))
        for q in range(cols // LANES):
            lane = slice(q * LANES, (q + 1) * LANES)
            new_top[rows, lane] = jnp.where(take, piece[:, lane], held_ref[rows, lane])

        @pl.when(mine == 1)
        def _():
            displaced_ref[rows, :] = piece[...]

    @pl.when(mine != 1)
    def _():
        displaced_ref[...] = before_ref[...]

    for odd, (first, second) in enumerate([(one_ref, two_ref), (two_ref, one_ref)]):
        @pl.when((me & 1) == odd)
        def _():
            merge(slice(0, half), first)
            merge(slice(half, nb), second)

    u = product(split(lower_ref[...]), split(new_top[...]))
    top_ref[...] = u
    weights_ref[...] = product(split(upper_ref[...]), split(u))

    @pl.when(where_ref[1] == 0)
    def _():
        top_ref[:, :nb] = new_top[:, :nb]
        weights_ref[:, :nb] = -upper_ref[...]


def fetch(choice_ref, bufs, place, sem, n_cols, parts, pairs):
    for i in range(pairs):
        for h in range(2):
            for b in sorted({arrival(p, i, h, n_cols, parts) for p in range(1, n_cols)}):
                @pl.when(choice_ref[2 * i + h] == b)
                def _():
                    pltpu.make_async_copy(bufs[b], place(i, h), sem).start()


def old_top_kernel(where_ref, choice_ref, matrix_ref, *refs, used, n_cols, parts, pairs):
    bufs, top_ref, sem = dict(zip(used, refs)), refs[-2], refs[-1]
    nb = top_ref.shape[0]
    chunk = nb // (2 * pairs)
    from_matrix = pltpu.make_async_copy(
        matrix_ref.at[pl.ds(0, nb), pl.ds(0, nb)], top_ref, sem
    )

    @pl.when(where_ref[0] == 0)
    def _():
        @pl.when(where_ref[1] == 0)
        def _():
            from_matrix.start()

        @pl.when(where_ref[1] > 0)
        def _():
            fetch(
                choice_ref, bufs,
                lambda i, h: top_ref.at[pl.ds((2 * i + h) * chunk, chunk), :],
                sem, n_cols, parts, pairs,
            )

        from_matrix.wait()


def final_kernel(
    where_ref, table_ref, choice_ref, displaced_ref, weights_ref, top_ref, matrix_ref,
    *refs, n_bufs, n_tops, n_cols, parts, block,
):
    bufs, tops, out_ref = refs[:n_bufs], refs[n_bufs : n_bufs + n_tops], refs[n_bufs + n_tops]
    mat, pan, low, w_hi, w_lo, result, in_sem, low_sem, mat_sem, out_sem = refs[
        n_bufs + n_tops + 1 :
    ]
    rows, cols = matrix_ref.shape
    nb = weights_ref.shape[0]
    chunk = rows // (2 * parts)
    row = where_ref[0]
    first_row, first_col = row == 0, where_ref[1] == 0

    load = pltpu.make_async_copy(matrix_ref, mat, mat_sem)
    load.start()
    whole_panel = pltpu.make_async_copy(matrix_ref.at[:, pl.ds(0, nb)], pan, in_sem)

    @pl.when(first_col)
    def _():
        whole_panel.start()

    @pl.when(jnp.logical_not(first_col))
    def _():
        fetch(
            choice_ref, bufs, lambda i, h: pan.at[pl.ds((2 * i + h) * chunk, chunk), :],
            in_sem, n_cols, parts, parts,
        )

    for log in range(n_tops):
        @pl.when((row & ((2 << log) - 1)) == (1 << log))
        def _():
            pltpu.make_async_copy(tops[log], low, low_sem).start()

    w = weights_ref[...]
    w_hi[...] = w.astype(jnp.bfloat16)
    w_lo[...] = (w - w_hi[...].astype(jnp.float32)).astype(jnp.bfloat16)

    whole_panel.wait()
    load.wait()
    count = table_ref[COUNT, 0]

    def swap(from_mat, from_pan):
        def body(k, _):
            to = table_ref[ROW, k]
            mat[pl.ds(to, 1), :] = from_mat[pl.ds(table_ref[FROM, k], 1), :]
            pan[pl.ds(to, 1), :] = from_pan[pl.ds(table_ref[TOP, k], 1), :]
            return 0

        lax.fori_loop(0, count, body, 0)

    @pl.when(first_row)
    def _():
        swap(mat, pan)

    @pl.when(jnp.logical_not(first_row))
    def _():
        pltpu.make_async_copy(tops[0], low, low_sem).wait()
        swap(displaced_ref, low)

    @pl.when(first_col)
    def _():
        mat[:, :nb] = jnp.zeros((rows, nb), jnp.float32)

    copies = []
    for b in range(rows // block):
        span = pl.ds(b * block, block)

        def update():
            p = pan[span, :]
            p_hi = p.astype(jnp.bfloat16)
            p_lo = (p - p_hi.astype(jnp.float32)).astype(jnp.bfloat16)
            dot = functools.partial(jnp.dot, preferred_element_type=jnp.float32)
            total = dot(p_lo, w_hi[...]) + dot(p_hi, w_lo[...]) + dot(p_hi, w_hi[...])
            result[span, :] = mat[span, :] - total

        if (b + 1) * block <= nb:
            pl.when(jnp.logical_not(first_row))(update)

            @pl.when(first_row)
            def _():
                result[span, :] = top_ref[span, :]
        else:
            update()
        copy = pltpu.make_async_copy(result.at[span, :], out_ref.at[span, :], out_sem)
        copy.start()
        copies.append(copy)
    for copy in copies:
        copy.wait()


LAG = 2


def steps(n_cols, parts):
    depth = n_cols // 2
    return parts + LAG * (depth - 1), max(2 * parts, parts + LAG * depth)


def arrival(p, i, h, n_cols, parts):
    z, y = divmod(p, 2)
    cross = steps(n_cols, parts)[0]
    if z == 0:
        return cross + i + h * parts
    if y == 0:
        return cross + i + LAG * (z + 1) if h == 0 else i + LAG * (z - 1)
    return i + LAG * z if h == 0 else cross + i + LAG * z


def spread(pieces, col, n_cols, riders):
    parts = len(pieces)
    n_chain, n_cross = steps(n_cols, parts)
    along = [(p, p + 2) for p in range(n_cols - 2)]
    across = [(0, 1)] + [(p, p ^ 1) for p in range(2, n_cols)]
    chain, cross = [], []
    waiting = [(rider, next(rider)(chain, cross)) for rider in riders]
    for s in range(n_cross):
        ahead = pieces[min(s, parts - 1)][1]
        aside = pieces[s][0] if s < parts else pieces[min(s - parts, parts - 1)][1]
        if s >= LAG:
            came = chain[s - LAG] if s - LAG < n_chain else chain[-1]
            due = [k for k, (_, (at, _)) in enumerate(waiting) if at == s]
            tied = [waiting[k][1][1] for k in due]
            (came, fed), tied = lax.optimization_barrier(((came, cross[s - LAG]), tied))
            ahead = jnp.where(col == 0, ahead, jnp.where(col == 1, fed, came))
            aside = jnp.where(col == 0, aside, came)
        if s < n_chain:
            chain.append(lax.ppermute(ahead, "pcol", along))
        cross.append(lax.ppermute(aside, "pcol", across))
        if s >= LAG:
            for k, values in zip(due, tied):
                rider = waiting[k][0]
                waiting[k] = (rider, resume(rider, values, chain, cross))
    results = []
    for rider, (at, values) in waiting:
        while at != DONE:
            at, values = resume(rider, values, chain, cross)
        results.append(values)
    return chain, cross, results


DONE = -1


def resume(rider, values, chain, cross):
    return rider.send(values)(chain, cross)


def give(at, values):
    return lambda chain, cross: (at, values)


def local(matrix, pivots, lower_inverse, upper_inverse, *, n_rows, n_cols, parts):
    row_dev, cols = matrix.shape
    nb = pivots.shape[0]
    f32 = jnp.float32
    row, col = lax.axis_index("prow"), lax.axis_index("pcol")
    here = jnp.stack([row, col]).astype(jnp.int32)
    odd = row % 2 == 1

    chunk = row_dev // (2 * parts)
    flat = [
        lax.slice(matrix, (k * chunk, 0), ((k + 1) * chunk, nb)) for k in range(2 * parts)
    ]
    flat = flat[:2] + list(lax.optimization_barrier(tuple(flat[2:])))
    choice = jnp.asarray(
        [
            [0] * (2 * parts) if p == 0 else
            [arrival(p, i, h, n_cols, parts) for i in range(parts) for h in range(2)]
            for p in range(n_cols)
        ],
        jnp.int32,
    )[col]

    pairs = nb // (2 * chunk)
    used = sorted({
        arrival(p, i, h, n_cols, parts)
        for p in range(1, n_cols) for i in range(pairs) for h in range(2)
    })
    n_chain = steps(n_cols, parts)[0]
    last = max(b - n_chain if b >= n_chain else b for b in used)

    def both_halves(one, two):
        return jnp.concatenate([jnp.where(odd, two, one), jnp.where(odd, one, two)], axis=0)

    def old_top_rider():
        at = last + LAG

        def start(chain, cross):
            return at, [chain[b] if b < n_chain else cross[b - n_chain] for b in used]

        arrived = yield give(at - 1, ())
        arrived = yield start
        old_top = call(
            functools.partial(
                old_top_kernel, used=used, n_cols=n_cols, parts=parts, pairs=pairs
            ),
            jax.ShapeDtypeStruct((nb, nb), f32),
            [SMEM, SMEM, ANY] + [ANY] * len(used), ANY, [pltpu.SemaphoreType.DMA],
            vmem=4 << 20,
        )(here, choice, matrix, *arrived)
        tops = []
        d = n_rows // 2
        while d:
            came = lax.ppermute(old_top, "prow", [(p, p + d) for p in range(0, n_rows, 2 * d)])
            if d > 1:
                at += 2
                came = yield give(at, came)
                old_top = jnp.where(row % (2 * d) == d, came, old_top)
            tops.insert(0, came)
            d //= 2
        yield give(DONE, tops)

    slot = jax.ShapeDtypeStruct((nb, cols), f32)
    half_slot = jax.ShapeDtypeStruct((nb // 2, cols), f32)

    def exchange_rider():
        table, owner = yield give(2, call(
            functools.partial(index_kernel, row_dev=row_dev),
            (jax.ShapeDtypeStruct((8, nb), jnp.int32), jax.ShapeDtypeStruct((nb, LANES), jnp.int32)),
            [SMEM, VMEM], (VMEM, VMEM),
        )(here, pivots.reshape(1, nb)))
        held = yield give(3, call(gather_kernel, slot, [SMEM, VMEM], VMEM)(table, matrix))
        at = 5
        displaced = held
        log = 0
        half = None
        while (1 << log) < n_rows:
            d = 1 << log
            far = [(p, p ^ d) for p in range(n_rows)]
            if log == 0:
                whole = yield give(at, lax.ppermute(held, "prow", far))
                arrived = [whole]
            else:
                near = [(p, p ^ 1) for p in range(n_rows)]
                one = yield give(at + 4, lax.ppermute(half, "prow", far))
                at += 5
                two = yield give(at, lax.ppermute(one, "prow", near))
                arrived = [one, two]
                whole = None if 2 << log == n_rows else both_halves(one, two)
            if 2 << log == n_rows:
                break
            held, half = call(
                functools.partial(merge_kernel, log=log, halves=log > 0),
                (slot, half_slot), [SMEM] + [VMEM] * (2 + len(arrived)), (VMEM, VMEM),
            )(here, owner, held, *arrived)
            displaced = jnp.where((row >> log) == 1, whole, displaced) if log else whole
            log += 1
        weights, top, displaced = yield give(at + 2, call(
            functools.partial(factor_kernel, log=log), (slot,) * 3,
            [SMEM] + [VMEM] * 7, (VMEM,) * 3, [pltpu.VMEM((nb, cols), f32)],
            flops=4 * nb * nb * cols * 3,
        )(here, owner, held, *arrived, displaced, lower_inverse, upper_inverse))
        yield give(DONE, (table, displaced, weights, top))

    chain, cross, (tops, (table, displaced, weights, top)) = spread(
        [(flat[2 * i], flat[2 * i + 1]) for i in range(parts)], col, n_cols,
        [old_top_rider(), exchange_rider()],
    )
    bufs = chain + cross

    return call(
        functools.partial(
            final_kernel, n_bufs=len(bufs), n_tops=len(tops), n_cols=n_cols, parts=parts,
            block=256,
        ),
        jax.ShapeDtypeStruct(matrix.shape, f32),
        [SMEM, SMEM, SMEM, VMEM, VMEM, VMEM, ANY] + [ANY] * (len(bufs) + len(tops)),
        ANY,
        [
            pltpu.VMEM((row_dev, cols), f32),
            pltpu.VMEM((row_dev, nb), f32),
            pltpu.VMEM((nb, nb), f32),
            pltpu.VMEM((nb, cols), jnp.bfloat16),
            pltpu.VMEM((nb, cols), jnp.bfloat16),
            pltpu.VMEM((row_dev, cols), f32),
        ] + [pltpu.SemaphoreType.DMA] * 4,
        vmem=30 << 20,
        flops=2 * row_dev * nb * cols * 3,
        moved=4 * row_dev * (2 * cols + nb),
    )(here, table, choice, displaced, weights, top, matrix, *bufs, *tops)


def solution(mesh):
    n_rows, n_cols = mesh.shape["prow"], mesh.shape["pcol"]
    return jax.shard_map(
        functools.partial(local, n_rows=n_rows, n_cols=n_cols, parts=8),
        mesh=mesh,
        in_specs=(P("prow", "pcol"), P(), P(), P()),
        out_specs=P("prow", "pcol"),
        check_vma=False,
    )
```

```python
import functools

import jax
import jax.numpy as jnp
from jax import lax
from jax.experimental import pallas as pl
from jax.experimental.pallas import tpu as pltpu
from jax.sharding import PartitionSpec as P

HIGHEST = lax.Precision.HIGHEST
VMEM = pl.BlockSpec(memory_space=pltpu.VMEM)
SMEM = pl.BlockSpec(memory_space=pltpu.SMEM)
ANY = pl.BlockSpec(memory_space=pl.ANY)
LANES = 128
PICK, FROM, ROW, COUNT, TOP = 0, 1, 2, 3, 4


def call(kernel, out, ins, outs, scratch=(), vmem=16 << 20, flops=0, moved=0):
    return pl.pallas_call(
        kernel,
        out_shape=out,
        in_specs=ins,
        out_specs=outs,
        scratch_shapes=list(scratch),
        compiler_params=pltpu.CompilerParams(vmem_limit_bytes=vmem),
        cost_estimate=pl.CostEstimate(
            flops=flops, bytes_accessed=moved, transcendentals=0
        ),
    )


def index_kernel(where_ref, pivots_ref, table_ref, owner_ref, *, row_dev):
    nb = pivots_ref.shape[1]
    start = where_ref[0] * row_dev
    first = where_ref[0] == 0
    down = lax.broadcasted_iota(jnp.int32, (nb, nb), 0)
    across = lax.broadcasted_iota(jnp.int32, (nb, nb), 1)
    piv_row = jnp.broadcast_to(pivots_ref[...], (nb, nb))

    def column(full):
        return jnp.sum(jnp.where(down == across, full, 0.0), axis=1, keepdims=True)

    piv_f = piv_row.astype(jnp.float32)
    piv_col = jnp.broadcast_to(column(piv_f), (nb, nb))
    upto = (down <= across).astype(jnp.bfloat16)
    below = (piv_row >= nb).astype(jnp.float32)
    vacancy = jnp.dot(
        below[:8].astype(jnp.bfloat16), upto, preferred_element_type=jnp.float32
    )[:1]
    taken = jnp.max((piv_row == down).astype(jnp.float32), axis=1, keepdims=True)
    freed = jnp.broadcast_to(1.0 - taken, (nb, LANES))
    rank = jnp.dot(
        (across <= down).astype(jnp.bfloat16),
        freed.astype(jnp.bfloat16),
        preferred_element_type=jnp.float32,
    )[:, :1]
    down_f = down.astype(jnp.float32)
    pair = (rank == vacancy) & (freed[:, :1] > 0.5)
    source = jnp.sum(jnp.where(pair, down_f, 0.0), axis=0, keepdims=True)
    source_col = jnp.broadcast_to(column(jnp.broadcast_to(source, (nb, nb))), (nb, nb))

    own_row = (pivots_ref[...] >= start) & (pivots_ref[...] < start + row_dev)
    pick = jnp.where(own_row, pivots_ref[...] - start, source.astype(jnp.int32))
    moved_row = (own_row & (pivots_ref[...] >= nb)).astype(jnp.float32)
    start_f = start.astype(jnp.float32)
    moved_col = (
        (piv_col >= start_f) & (piv_col < start_f + row_dev) & (piv_col >= nb)
    )
    order = jnp.sum(
        jnp.where(piv_f < piv_col, jnp.broadcast_to(moved_row, (nb, nb)), 0.0),
        axis=1,
        keepdims=True,
    )
    placed = moved_col & (order == across.astype(jnp.float32))
    origin = jnp.where(first, source_col, down_f)
    listed_from = jnp.sum(jnp.where(placed, origin, 0.0), axis=0, keepdims=True)
    listed_row = jnp.sum(
        jnp.where(placed, piv_col - start_f, 0.0), axis=0, keepdims=True
    )
    listed_top = jnp.sum(jnp.where(placed, source_col, 0.0), axis=0, keepdims=True)
    count = jnp.sum(moved_row, axis=1, keepdims=True)
    table_ref[...] = jnp.zeros_like(table_ref)
    table_ref[PICK : PICK + 1, :] = pick
    table_ref[FROM : FROM + 1, :] = listed_from.astype(jnp.int32)
    table_ref[ROW : ROW + 1, :] = listed_row.astype(jnp.int32)
    table_ref[TOP : TOP + 1, :] = listed_top.astype(jnp.int32)
    table_ref[COUNT : COUNT + 1, :] = jnp.broadcast_to(
        count.astype(jnp.int32), (1, nb)
    )
    owner_ref[...] = piv_col[:, :LANES].astype(jnp.int32) // row_dev


def gather_kernel(table_ref, matrix_ref, out_ref):
    nb = out_ref.shape[0]

    @pl.loop(0, nb, step=8)
    def _(base):
        for k in range(8):
            j = base + k
            out_ref[pl.ds(j, 1), :] = matrix_ref[pl.ds(table_ref[PICK, j], 1), :]


def merge_kernel(where_ref, owner_ref, held_ref, *refs, log, halves):
    arrived, (merged_ref, half_ref) = refs[: 2 if halves else 1], refs[-2:]
    me = where_ref[0]
    mine, theirs = me >> log, (me >> log) ^ 1
    odd = me & 1
    nb, cols = held_ref.shape
    half = nb // 2

    def merge(rows, piece):
        group = owner_ref[rows, :] >> log
        take = (group == theirs) | ((theirs == 0) & (group != mine))
        for q in range(cols // LANES):
            lane = slice(q * LANES, (q + 1) * LANES)
            merged_ref[rows, lane] = jnp.where(take, piece[:, lane], held_ref[rows, lane])

    low, high = slice(0, half), slice(half, nb)
    if halves:
        @pl.when(odd == 0)
        def _():
            merge(low, arrived[0])
            merge(high, arrived[1])

        @pl.when(odd == 1)
        def _():
            merge(low, arrived[1])
            merge(high, arrived[0])
    else:
        merge(slice(0, nb), arrived[0])

    @pl.when(odd == 0)
    def _():
        half_ref[...] = merged_ref[low, :]

    @pl.when(odd == 1)
    def _():
        half_ref[...] = merged_ref[high, :]


def factor_kernel(where_ref, top_in_ref, lower_ref, upper_ref, weights_ref, top_ref):
    nb, cols = top_in_ref.shape
    u = jnp.dot(
        lower_ref[...], top_in_ref[...], precision=HIGHEST,
        preferred_element_type=jnp.float32,
    )
    top_ref[...] = u
    weights_ref[...] = jnp.dot(
        upper_ref[...], u, precision=HIGHEST, preferred_element_type=jnp.float32
    )

    @pl.when(where_ref[1] == 0)
    def _():
        top_ref[:, :nb] = top_in_ref[:, :nb]
        weights_ref[:, :nb] = -upper_ref[...]


def fetch(choice_ref, bufs, place, sem, n_cols, parts, pairs):
    for i in range(pairs):
        for h in range(2):
            for b in sorted({arrival(p, i, h, n_cols, parts) for p in range(1, n_cols)}):
                @pl.when(choice_ref[2 * i + h] == b)
                def _():
                    pltpu.make_async_copy(bufs[b], place(i, h), sem).start()


def old_top_kernel(where_ref, choice_ref, matrix_ref, *refs, used, n_cols, parts, pairs):
    bufs, top_ref, sem = dict(zip(used, refs)), refs[-2], refs[-1]
    nb = top_ref.shape[0]
    chunk = nb // (2 * pairs)
    from_matrix = pltpu.make_async_copy(
        matrix_ref.at[pl.ds(0, nb), pl.ds(0, nb)], top_ref, sem
    )

    @pl.when(where_ref[0] == 0)
    def _():
        @pl.when(where_ref[1] == 0)
        def _():
            from_matrix.start()

        @pl.when(where_ref[1] > 0)
        def _():
            fetch(
                choice_ref, bufs,
                lambda i, h: top_ref.at[pl.ds((2 * i + h) * chunk, chunk), :],
                sem, n_cols, parts, pairs,
            )

        from_matrix.wait()


def final_kernel(
    where_ref, table_ref, choice_ref, displaced_ref, weights_ref, top_ref, matrix_ref,
    *refs, n_bufs, n_tops, n_cols, parts, block,
):
    bufs, tops, out_ref = refs[:n_bufs], refs[n_bufs : n_bufs + n_tops], refs[n_bufs + n_tops]
    mat, pan, low, w_hi, w_lo, result, in_sem, low_sem, mat_sem, out_sem = refs[
        n_bufs + n_tops + 1 :
    ]
    rows, cols = matrix_ref.shape
    nb = weights_ref.shape[0]
    chunk = rows // (2 * parts)
    row = where_ref[0]
    first_row, first_col = row == 0, where_ref[1] == 0

    load = pltpu.make_async_copy(matrix_ref, mat, mat_sem)
    load.start()
    whole_panel = pltpu.make_async_copy(matrix_ref.at[:, pl.ds(0, nb)], pan, in_sem)

    @pl.when(first_col)
    def _():
        whole_panel.start()

    @pl.when(jnp.logical_not(first_col))
    def _():
        fetch(
            choice_ref, bufs, lambda i, h: pan.at[pl.ds((2 * i + h) * chunk, chunk), :],
            in_sem, n_cols, parts, parts,
        )

    for log in range(n_tops):
        @pl.when((row & ((2 << log) - 1)) == (1 << log))
        def _():
            pltpu.make_async_copy(tops[log], low, low_sem).start()

    w = weights_ref[...]
    w_hi[...] = w.astype(jnp.bfloat16)
    w_lo[...] = (w - w_hi[...].astype(jnp.float32)).astype(jnp.bfloat16)

    whole_panel.wait()
    load.wait()
    count = table_ref[COUNT, 0]

    def swap(from_mat, from_pan):
        def body(k, _):
            to = table_ref[ROW, k]
            mat[pl.ds(to, 1), :] = from_mat[pl.ds(table_ref[FROM, k], 1), :]
            pan[pl.ds(to, 1), :] = from_pan[pl.ds(table_ref[TOP, k], 1), :]
            return 0

        lax.fori_loop(0, count, body, 0)

    @pl.when(first_row)
    def _():
        swap(mat, pan)

    @pl.when(jnp.logical_not(first_row))
    def _():
        pltpu.make_async_copy(tops[0], low, low_sem).wait()
        swap(displaced_ref, low)

    @pl.when(first_col)
    def _():
        mat[:, :nb] = jnp.zeros((rows, nb), jnp.float32)

    copies = []
    for b in range(rows // block):
        span = pl.ds(b * block, block)

        def update():
            p = pan[span, :]
            p_hi = p.astype(jnp.bfloat16)
            p_lo = (p - p_hi.astype(jnp.float32)).astype(jnp.bfloat16)
            dot = functools.partial(jnp.dot, preferred_element_type=jnp.float32)
            total = dot(p_lo, w_hi[...]) + dot(p_hi, w_lo[...]) + dot(p_hi, w_hi[...])
            result[span, :] = mat[span, :] - total

        if (b + 1) * block <= nb:
            pl.when(jnp.logical_not(first_row))(update)

            @pl.when(first_row)
            def _():
                result[span, :] = top_ref[span, :]
        else:
            update()
        copy = pltpu.make_async_copy(result.at[span, :], out_ref.at[span, :], out_sem)
        copy.start()
        copies.append(copy)
    for copy in copies:
        copy.wait()


LAG = 2


def steps(n_cols, parts):
    depth = n_cols // 2
    return parts + LAG * (depth - 1), max(2 * parts, parts + LAG * depth)


def arrival(p, i, h, n_cols, parts):
    z, y = divmod(p, 2)
    cross = steps(n_cols, parts)[0]
    if z == 0:
        return cross + i + h * parts
    if y == 0:
        return cross + i + LAG * (z + 1) if h == 0 else i + LAG * (z - 1)
    return i + LAG * z if h == 0 else cross + i + LAG * z


def spread(pieces, col, n_cols, riders):
    parts = len(pieces)
    n_chain, n_cross = steps(n_cols, parts)
    along = [(p, p + 2) for p in range(n_cols - 2)]
    across = [(0, 1)] + [(p, p ^ 1) for p in range(2, n_cols)]
    chain, cross = [], []
    waiting = [(rider, next(rider)(chain, cross)) for rider in riders]
    for s in range(n_cross):
        ahead = pieces[min(s, parts - 1)][1]
        aside = pieces[s][0] if s < parts else pieces[min(s - parts, parts - 1)][1]
        if s >= LAG:
            came = chain[s - LAG] if s - LAG < n_chain else chain[-1]
            due = [k for k, (_, (at, _)) in enumerate(waiting) if at == s]
            tied = [waiting[k][1][1] for k in due]
            (came, fed), tied = lax.optimization_barrier(((came, cross[s - LAG]), tied))
            ahead = jnp.where(col == 0, ahead, jnp.where(col == 1, fed, came))
            aside = jnp.where(col == 0, aside, came)
        if s < n_chain:
            chain.append(lax.ppermute(ahead, "pcol", along))
        cross.append(lax.ppermute(aside, "pcol", across))
        if s >= LAG:
            for k, values in zip(due, tied):
                rider = waiting[k][0]
                waiting[k] = (rider, resume(rider, values, chain, cross))
    results = []
    for rider, (at, values) in waiting:
        while at != DONE:
            at, values = resume(rider, values, chain, cross)
        results.append(values)
    return chain, cross, results


DONE = -1


def resume(rider, values, chain, cross):
    return rider.send(values)(chain, cross)


def give(at, values):
    return lambda chain, cross: (at, values)


def local(matrix, pivots, lower_inverse, upper_inverse, *, n_rows, n_cols, parts):
    row_dev, cols = matrix.shape
    nb = pivots.shape[0]
    f32 = jnp.float32
    row, col = lax.axis_index("prow"), lax.axis_index("pcol")
    here = jnp.stack([row, col]).astype(jnp.int32)
    odd = row % 2 == 1

    chunk = row_dev // (2 * parts)
    flat = [
        lax.slice(matrix, (k * chunk, 0), ((k + 1) * chunk, nb)) for k in range(2 * parts)
    ]
    flat = flat[:2] + list(lax.optimization_barrier(tuple(flat[2:])))
    choice = jnp.asarray(
        [
            [0] * (2 * parts) if p == 0 else
            [arrival(p, i, h, n_cols, parts) for i in range(parts) for h in range(2)]
            for p in range(n_cols)
        ],
        jnp.int32,
    )[col]

    pairs = nb // (2 * chunk)
    used = sorted({
        arrival(p, i, h, n_cols, parts)
        for p in range(1, n_cols) for i in range(pairs) for h in range(2)
    })
    n_chain = steps(n_cols, parts)[0]
    last = max(b - n_chain if b >= n_chain else b for b in used)

    def both_halves(one, two):
        return jnp.concatenate([jnp.where(odd, two, one), jnp.where(odd, one, two)], axis=0)

    def old_top_rider():
        at = last + LAG

        def start(chain, cross):
            return at, [chain[b] if b < n_chain else cross[b - n_chain] for b in used]

        arrived = yield give(at - 1, ())
        arrived = yield start
        old_top = call(
            functools.partial(
                old_top_kernel, used=used, n_cols=n_cols, parts=parts, pairs=pairs
            ),
            jax.ShapeDtypeStruct((nb, nb), f32),
            [SMEM, SMEM, ANY] + [ANY] * len(used), ANY, [pltpu.SemaphoreType.DMA],
            vmem=4 << 20,
        )(here, choice, matrix, *arrived)
        tops = []
        d = n_rows // 2
        while d:
            came = lax.ppermute(old_top, "prow", [(p, p + d) for p in range(0, n_rows, 2 * d)])
            if d > 1:
                at += 3
                came = yield give(at, came)
                old_top = jnp.where(row % (2 * d) == d, came, old_top)
            tops.insert(0, came)
            d //= 2
        yield give(DONE, tops)

    slot = jax.ShapeDtypeStruct((nb, cols), f32)
    half_slot = jax.ShapeDtypeStruct((nb // 2, cols), f32)

    def exchange_rider():
        table, owner = yield give(2, call(
            functools.partial(index_kernel, row_dev=row_dev),
            (jax.ShapeDtypeStruct((8, nb), jnp.int32), jax.ShapeDtypeStruct((nb, LANES), jnp.int32)),
            [SMEM, VMEM], (VMEM, VMEM),
        )(here, pivots.reshape(1, nb)))
        held = yield give(3, call(gather_kernel, slot, [SMEM, VMEM], VMEM)(table, matrix))
        at = 5
        displaced = held
        log = 0
        half = None
        while (1 << log) < n_rows:
            d = 1 << log
            far = [(p, p ^ d) for p in range(n_rows)]
            if log == 0:
                whole = yield give(at, lax.ppermute(held, "prow", far))
                arrived = [whole]
            else:
                near = [(p, p ^ 1) for p in range(n_rows)]
                one = yield give(at + 4, lax.ppermute(half, "prow", far))
                at += 5
                two = yield give(at, lax.ppermute(one, "prow", near))
                arrived = [one, two]
                whole = both_halves(one, two)
            held, half = call(
                functools.partial(merge_kernel, log=log, halves=log > 0),
                (slot, half_slot), [SMEM] + [VMEM] * (2 + len(arrived)), (VMEM, VMEM),
            )(here, owner, held, *arrived)
            displaced = jnp.where((row >> log) == 1, whole, displaced)
            log += 1
        held, displaced = yield give(at + 1, (held, displaced))
        weights, top = yield give(at + 2, call(
            factor_kernel, (slot, slot), [SMEM, VMEM, VMEM, VMEM], (VMEM, VMEM),
            flops=4 * nb * nb * cols * 6,
        )(here, held, lower_inverse, upper_inverse))
        yield give(DONE, (table, displaced, weights, top))

    chain, cross, (tops, (table, displaced, weights, top)) = spread(
        [(flat[2 * i], flat[2 * i + 1]) for i in range(parts)], col, n_cols,
        [old_top_rider(), exchange_rider()],
    )
    bufs = chain + cross

    return call(
        functools.partial(
            final_kernel, n_bufs=len(bufs), n_tops=len(tops), n_cols=n_cols, parts=parts,
            block=256,
        ),
        jax.ShapeDtypeStruct(matrix.shape, f32),
        [SMEM, SMEM, SMEM, VMEM, VMEM, VMEM, ANY] + [ANY] * (len(bufs) + len(tops)),
        ANY,
        [
            pltpu.VMEM((row_dev, cols), f32),
            pltpu.VMEM((row_dev, nb), f32),
            pltpu.VMEM((nb, nb), f32),
            pltpu.VMEM((nb, cols), jnp.bfloat16),
            pltpu.VMEM((nb, cols), jnp.bfloat16),
            pltpu.VMEM((row_dev, cols), f32),
        ] + [pltpu.SemaphoreType.DMA] * 4,
        vmem=30 << 20,
        flops=2 * row_dev * nb * cols * 3,
        moved=4 * row_dev * (2 * cols + nb),
    )(here, table, choice, displaced, weights, top, matrix, *bufs, *tops)


def solution(mesh):
    n_rows, n_cols = mesh.shape["prow"], mesh.shape["pcol"]
    return jax.shard_map(
        functools.partial(local, n_rows=n_rows, n_cols=n_cols, parts=8),
        mesh=mesh,
        in_specs=(P("prow", "pcol"), P(), P(), P()),
        out_specs=P("prow", "pcol"),
        check_vma=False,
    )
```

```python
import functools

import jax
import jax.numpy as jnp
from jax import lax
from jax.experimental import pallas as pl
from jax.experimental.pallas import tpu as pltpu
from jax.sharding import PartitionSpec as P

VMEM = pl.BlockSpec(memory_space=pltpu.VMEM)
SMEM = pl.BlockSpec(memory_space=pltpu.SMEM)
ANY = pl.BlockSpec(memory_space=pl.ANY)
LANES = 128
PICK, FROM, ROW, COUNT, TOP = 0, 1, 2, 3, 4


def call(kernel, out, ins, outs, scratch=(), vmem=16 << 20, flops=0, moved=0):
    return pl.pallas_call(
        kernel,
        out_shape=out,
        in_specs=ins,
        out_specs=outs,
        scratch_shapes=list(scratch),
        compiler_params=pltpu.CompilerParams(vmem_limit_bytes=vmem),
        cost_estimate=pl.CostEstimate(
            flops=flops, bytes_accessed=moved, transcendentals=0
        ),
    )


def index_kernel(where_ref, pivots_ref, table_ref, owner_ref, *, row_dev):
    nb = pivots_ref.shape[1]
    start = where_ref[0] * row_dev
    first = where_ref[0] == 0
    down = lax.broadcasted_iota(jnp.int32, (nb, nb), 0)
    across = lax.broadcasted_iota(jnp.int32, (nb, nb), 1)
    piv_row = jnp.broadcast_to(pivots_ref[...], (nb, nb))

    def column(full):
        return jnp.sum(jnp.where(down == across, full, 0.0), axis=1, keepdims=True)

    piv_f = piv_row.astype(jnp.float32)
    piv_col = jnp.broadcast_to(column(piv_f), (nb, nb))
    upto = (down <= across).astype(jnp.bfloat16)
    below = (piv_row >= nb).astype(jnp.float32)
    vacancy = jnp.dot(
        below[:8].astype(jnp.bfloat16), upto, preferred_element_type=jnp.float32
    )[:1]
    taken = jnp.max((piv_row == down).astype(jnp.float32), axis=1, keepdims=True)
    freed = jnp.broadcast_to(1.0 - taken, (nb, LANES))
    rank = jnp.dot(
        (across <= down).astype(jnp.bfloat16),
        freed.astype(jnp.bfloat16),
        preferred_element_type=jnp.float32,
    )[:, :1]
    down_f = down.astype(jnp.float32)
    pair = (rank == vacancy) & (freed[:, :1] > 0.5)
    source = jnp.sum(jnp.where(pair, down_f, 0.0), axis=0, keepdims=True)
    source_col = jnp.broadcast_to(column(jnp.broadcast_to(source, (nb, nb))), (nb, nb))

    own_row = (pivots_ref[...] >= start) & (pivots_ref[...] < start + row_dev)
    pick = jnp.where(own_row, pivots_ref[...] - start, source.astype(jnp.int32))
    moved_row = (own_row & (pivots_ref[...] >= nb)).astype(jnp.float32)
    start_f = start.astype(jnp.float32)
    moved_col = (
        (piv_col >= start_f) & (piv_col < start_f + row_dev) & (piv_col >= nb)
    )
    order = jnp.sum(
        jnp.where(piv_f < piv_col, jnp.broadcast_to(moved_row, (nb, nb)), 0.0),
        axis=1,
        keepdims=True,
    )
    placed = moved_col & (order == across.astype(jnp.float32))
    origin = jnp.where(first, source_col, down_f)
    listed_from = jnp.sum(jnp.where(placed, origin, 0.0), axis=0, keepdims=True)
    listed_row = jnp.sum(
        jnp.where(placed, piv_col - start_f, 0.0), axis=0, keepdims=True
    )
    listed_top = jnp.sum(jnp.where(placed, source_col, 0.0), axis=0, keepdims=True)
    count = jnp.sum(moved_row, axis=1, keepdims=True)
    table_ref[...] = jnp.zeros_like(table_ref)
    table_ref[PICK : PICK + 1, :] = pick
    table_ref[FROM : FROM + 1, :] = listed_from.astype(jnp.int32)
    table_ref[ROW : ROW + 1, :] = listed_row.astype(jnp.int32)
    table_ref[TOP : TOP + 1, :] = listed_top.astype(jnp.int32)
    table_ref[COUNT : COUNT + 1, :] = jnp.broadcast_to(
        count.astype(jnp.int32), (1, nb)
    )
    owner_ref[...] = piv_col[:, :LANES].astype(jnp.int32) // row_dev


def gather_kernel(table_ref, matrix_ref, out_ref):
    nb = out_ref.shape[0]

    @pl.loop(0, nb, step=8)
    def _(base):
        for k in range(8):
            j = base + k
            out_ref[pl.ds(j, 1), :] = matrix_ref[pl.ds(table_ref[PICK, j], 1), :]


def merge_kernel(where_ref, owner_ref, held_ref, *refs, log, halves):
    arrived, (merged_ref, half_ref) = refs[: 2 if halves else 1], refs[-2:]
    me = where_ref[0]
    mine, theirs = me >> log, (me >> log) ^ 1
    odd = me & 1
    nb, cols = held_ref.shape
    half = nb // 2

    def merge(rows, piece):
        group = owner_ref[rows, :] >> log
        take = (group == theirs) | ((theirs == 0) & (group != mine))
        for q in range(cols // LANES):
            lane = slice(q * LANES, (q + 1) * LANES)
            merged_ref[rows, lane] = jnp.where(take, piece[:, lane], held_ref[rows, lane])

    low, high = slice(0, half), slice(half, nb)
    if halves:
        @pl.when(odd == 0)
        def _():
            merge(low, arrived[0])
            merge(high, arrived[1])

        @pl.when(odd == 1)
        def _():
            merge(low, arrived[1])
            merge(high, arrived[0])
    else:
        merge(slice(0, nb), arrived[0])

    @pl.when(odd == 0)
    def _():
        half_ref[...] = merged_ref[low, :]

    @pl.when(odd == 1)
    def _():
        half_ref[...] = merged_ref[high, :]


def split(x):
    hi = x.astype(jnp.bfloat16)
    return hi, (x - hi.astype(jnp.float32)).astype(jnp.bfloat16)


def product(a, b):
    dot = functools.partial(jnp.dot, preferred_element_type=jnp.float32)
    return dot(a[1], b[0]) + dot(a[0], b[1]) + dot(a[0], b[0])


def factor_kernel(where_ref, top_in_ref, lower_ref, upper_ref, weights_ref, top_ref):
    nb = top_in_ref.shape[0]
    u = product(split(lower_ref[...]), split(top_in_ref[...]))
    top_ref[...] = u
    weights_ref[...] = product(split(upper_ref[...]), split(u))

    @pl.when(where_ref[1] == 0)
    def _():
        top_ref[:, :nb] = top_in_ref[:, :nb]
        weights_ref[:, :nb] = -upper_ref[...]


def fetch(choice_ref, bufs, place, sem, n_cols, parts, pairs):
    for i in range(pairs):
        for h in range(2):
            for b in sorted({arrival(p, i, h, n_cols, parts) for p in range(1, n_cols)}):
                @pl.when(choice_ref[2 * i + h] == b)
                def _():
                    pltpu.make_async_copy(bufs[b], place(i, h), sem).start()


def old_top_kernel(where_ref, choice_ref, matrix_ref, *refs, used, n_cols, parts, pairs):
    bufs, top_ref, sem = dict(zip(used, refs)), refs[-2], refs[-1]
    nb = top_ref.shape[0]
    chunk = nb // (2 * pairs)
    from_matrix = pltpu.make_async_copy(
        matrix_ref.at[pl.ds(0, nb), pl.ds(0, nb)], top_ref, sem
    )

    @pl.when(where_ref[0] == 0)
    def _():
        @pl.when(where_ref[1] == 0)
        def _():
            from_matrix.start()

        @pl.when(where_ref[1] > 0)
        def _():
            fetch(
                choice_ref, bufs,
                lambda i, h: top_ref.at[pl.ds((2 * i + h) * chunk, chunk), :],
                sem, n_cols, parts, pairs,
            )

        from_matrix.wait()


def final_kernel(
    where_ref, table_ref, choice_ref, displaced_ref, weights_ref, top_ref, matrix_ref,
    *refs, n_bufs, n_tops, n_cols, parts, block,
):
    bufs, tops, out_ref = refs[:n_bufs], refs[n_bufs : n_bufs + n_tops], refs[n_bufs + n_tops]
    mat, pan, low, w_hi, w_lo, result, in_sem, low_sem, mat_sem, out_sem = refs[
        n_bufs + n_tops + 1 :
    ]
    rows, cols = matrix_ref.shape
    nb = weights_ref.shape[0]
    half = nb // 2
    chunk = rows // (2 * parts)
    row = where_ref[0]
    first_row, first_col = row == 0, where_ref[1] == 0

    load = pltpu.make_async_copy(matrix_ref, mat, mat_sem)
    load.start()
    whole_panel = pltpu.make_async_copy(matrix_ref.at[:, pl.ds(0, nb)], pan, in_sem)

    @pl.when(first_col)
    def _():
        whole_panel.start()

    @pl.when(jnp.logical_not(first_col))
    def _():
        fetch(
            choice_ref, bufs, lambda i, h: pan.at[pl.ds((2 * i + h) * chunk, chunk), :],
            in_sem, n_cols, parts, parts,
        )

    @pl.when(row == 1)
    def _():
        pltpu.make_async_copy(tops[0], low, low_sem).start()

    for log in range(1, (n_tops + 1) // 2):
        for odd in range(2):
            @pl.when(((row >> log) == 1) & ((row & 1) == odd))
            def _():
                for part, ref in enumerate(tops[2 * log - 1 : 2 * log + 1]):
                    at = half * (part ^ odd)
                    pltpu.make_async_copy(ref, low.at[pl.ds(at, half), :], low_sem).start()

    w = weights_ref[...]
    w_hi[...] = w.astype(jnp.bfloat16)
    w_lo[...] = (w - w_hi[...].astype(jnp.float32)).astype(jnp.bfloat16)

    whole_panel.wait()
    load.wait()
    count = table_ref[COUNT, 0]

    def swap(from_mat, from_pan):
        def body(turn, _):
            at = [jnp.minimum(4 * turn + k, count - 1) for k in range(4)]
            mats = [from_mat[pl.ds(table_ref[FROM, k], 1), :] for k in at]
            pans = [from_pan[pl.ds(table_ref[TOP, k], 1), :] for k in at]
            for k, row_mat, row_pan in zip(at, mats, pans):
                mat[pl.ds(table_ref[ROW, k], 1), :] = row_mat
                pan[pl.ds(table_ref[ROW, k], 1), :] = row_pan
            return 0

        lax.fori_loop(0, (count + 3) // 4, body, 0)

    @pl.when(first_row)
    def _():
        swap(mat, pan)

    @pl.when(jnp.logical_not(first_row))
    def _():
        pltpu.make_async_copy(tops[0], low, low_sem).wait()
        swap(displaced_ref, low)

    @pl.when(first_col)
    def _():
        mat[:, :nb] = jnp.zeros((rows, nb), jnp.float32)

    copies = []
    for b in range(rows // block):
        span = pl.ds(b * block, block)

        def update():
            p = pan[span, :]
            p_hi = p.astype(jnp.bfloat16)
            p_lo = (p - p_hi.astype(jnp.float32)).astype(jnp.bfloat16)
            dot = functools.partial(jnp.dot, preferred_element_type=jnp.float32)
            total = dot(p_lo, w_hi[...]) + dot(p_hi, w_lo[...]) + dot(p_hi, w_hi[...])
            result[span, :] = mat[span, :] - total

        if (b + 1) * block <= nb:
            pl.when(jnp.logical_not(first_row))(update)

            @pl.when(first_row)
            def _():
                result[span, :] = top_ref[span, :]
        else:
            update()
        copy = pltpu.make_async_copy(result.at[span, :], out_ref.at[span, :], out_sem)
        copy.start()
        copies.append(copy)
    for copy in copies:
        copy.wait()


LAG = 2


def steps(n_cols, parts):
    depth = n_cols // 2
    return parts + LAG * (depth - 1), max(2 * parts, parts + LAG * depth)


def arrival(p, i, h, n_cols, parts):
    z, y = divmod(p, 2)
    cross = steps(n_cols, parts)[0]
    if z == 0:
        return cross + i + h * parts
    if y == 0:
        return cross + i + LAG * (z + 1) if h == 0 else i + LAG * (z - 1)
    return i + LAG * z if h == 0 else cross + i + LAG * z


def spread(pieces, col, n_cols, riders):
    parts = len(pieces)
    n_chain, n_cross = steps(n_cols, parts)
    along = [(p, p + 2) for p in range(n_cols - 2)]
    across = [(0, 1)] + [(p, p ^ 1) for p in range(2, n_cols)]
    chain, cross = [], []
    waiting = [(rider, next(rider)(chain, cross)) for rider in riders]
    for s in range(n_cross):
        ahead = pieces[min(s, parts - 1)][1]
        aside = pieces[s][0] if s < parts else pieces[min(s - parts, parts - 1)][1]
        if s >= LAG:
            came = chain[s - LAG] if s - LAG < n_chain else chain[-1]
            due = [k for k, (_, (at, _)) in enumerate(waiting) if at == s]
            tied = [waiting[k][1][1] for k in due]
            (came, fed), tied = lax.optimization_barrier(((came, cross[s - LAG]), tied))
            ahead = jnp.where(col == 0, ahead, jnp.where(col == 1, fed, came))
            aside = jnp.where(col == 0, aside, came)
        if s < n_chain:
            chain.append(lax.ppermute(ahead, "pcol", along))
        cross.append(lax.ppermute(aside, "pcol", across))
        if s >= LAG:
            for k, values in zip(due, tied):
                rider = waiting[k][0]
                waiting[k] = (rider, resume(rider, values, chain, cross))
    results = []
    for rider, (at, values) in waiting:
        while at != DONE:
            at, values = resume(rider, values, chain, cross)
        results.append(values)
    return chain, cross, results


DONE = -1


def resume(rider, values, chain, cross):
    return rider.send(values)(chain, cross)


def give(at, values):
    return lambda chain, cross: (at, values)


def local(matrix, pivots, lower_inverse, upper_inverse, *, n_rows, n_cols, parts):
    row_dev, cols = matrix.shape
    nb = pivots.shape[0]
    f32 = jnp.float32
    row, col = lax.axis_index("prow"), lax.axis_index("pcol")
    here = jnp.stack([row, col]).astype(jnp.int32)
    odd = row % 2 == 1

    chunk = row_dev // (2 * parts)
    flat = [
        lax.slice(matrix, (k * chunk, 0), ((k + 1) * chunk, nb)) for k in range(2 * parts)
    ]
    flat = flat[:2] + list(lax.optimization_barrier(tuple(flat[2:])))
    choice = jnp.asarray(
        [
            [0] * (2 * parts) if p == 0 else
            [arrival(p, i, h, n_cols, parts) for i in range(parts) for h in range(2)]
            for p in range(n_cols)
        ],
        jnp.int32,
    )[col]

    pairs = nb // (2 * chunk)
    used = sorted({
        arrival(p, i, h, n_cols, parts)
        for p in range(1, n_cols) for i in range(pairs) for h in range(2)
    })
    n_chain = steps(n_cols, parts)[0]
    last = max(b - n_chain if b >= n_chain else b for b in used)

    def both_halves(one, two):
        return jnp.concatenate([jnp.where(odd, two, one), jnp.where(odd, one, two)], axis=0)

    def old_top_rider():
        at = last + LAG

        def start(chain, cross):
            return at, [chain[b] if b < n_chain else cross[b - n_chain] for b in used]

        arrived = yield give(at - 1, ())
        arrived = yield start
        old_top = call(
            functools.partial(
                old_top_kernel, used=used, n_cols=n_cols, parts=parts, pairs=pairs
            ),
            jax.ShapeDtypeStruct((nb, nb), f32),
            [SMEM, SMEM, ANY] + [ANY] * len(used), ANY, [pltpu.SemaphoreType.DMA],
            vmem=4 << 20,
        )(here, choice, matrix, *arrived)
        tops = []
        log = 0
        while (1 << log) < n_rows:
            d = 1 << log
            far = [(p, p + d) for p in range(d)]
            if log == 0:
                at += 2
                whole = yield give(at, lax.ppermute(old_top, "prow", far))
                tops.append(whole)
            else:
                half = jnp.where(odd, old_top[nb // 2 :], old_top[: nb // 2])
                at += 3
                one = yield give(at, lax.ppermute(half, "prow", far))
                two = lax.ppermute(one, "prow", [(p, p ^ 1) for p in range(d, 2 * d)])
                tops += [one, two]
                whole = both_halves(one, two)
            old_top = jnp.where((row >> log) == 1, whole, old_top)
            log += 1
        yield give(DONE, tops)

    slot = jax.ShapeDtypeStruct((nb, cols), f32)
    half_slot = jax.ShapeDtypeStruct((nb // 2, cols), f32)

    def exchange_rider():
        table, owner = yield give(2, call(
            functools.partial(index_kernel, row_dev=row_dev),
            (jax.ShapeDtypeStruct((8, nb), jnp.int32), jax.ShapeDtypeStruct((nb, LANES), jnp.int32)),
            [SMEM, VMEM], (VMEM, VMEM),
        )(here, pivots.reshape(1, nb)))
        held = yield give(3, call(gather_kernel, slot, [SMEM, VMEM], VMEM)(table, matrix))
        at = 5
        displaced = held
        log = 0
        half = None
        while (1 << log) < n_rows:
            d = 1 << log
            far = [(p, p ^ d) for p in range(n_rows)]
            if log == 0:
                whole = yield give(at, lax.ppermute(held, "prow", far))
                arrived = [whole]
            else:
                near = [(p, p ^ 1) for p in range(n_rows)]
                one = yield give(at + 4, lax.ppermute(half, "prow", far))
                at += 5
                two = yield give(at, lax.ppermute(one, "prow", near))
                arrived = [one, two]
                whole = both_halves(one, two)
            held, half = call(
                functools.partial(merge_kernel, log=log, halves=log > 0),
                (slot, half_slot), [SMEM] + [VMEM] * (2 + len(arrived)), (VMEM, VMEM),
            )(here, owner, held, *arrived)
            displaced = jnp.where((row >> log) == 1, whole, displaced)
            log += 1
        held, displaced = yield give(at + 1, (held, displaced))
        weights, top = yield give(at + 2, call(
            factor_kernel, (slot, slot), [SMEM, VMEM, VMEM, VMEM], (VMEM, VMEM),
            flops=4 * nb * nb * cols * 6,
        )(here, held, lower_inverse, upper_inverse))
        yield give(DONE, (table, displaced, weights, top))

    chain, cross, (tops, (table, displaced, weights, top)) = spread(
        [(flat[2 * i], flat[2 * i + 1]) for i in range(parts)], col, n_cols,
        [old_top_rider(), exchange_rider()],
    )
    bufs = chain + cross

    return call(
        functools.partial(
            final_kernel, n_bufs=len(bufs), n_tops=len(tops), n_cols=n_cols, parts=parts,
            block=256,
        ),
        jax.ShapeDtypeStruct(matrix.shape, f32),
        [SMEM, SMEM, SMEM, VMEM, VMEM, VMEM, ANY] + [ANY] * (len(bufs) + len(tops)),
        ANY,
        [
            pltpu.VMEM((row_dev, cols), f32),
            pltpu.VMEM((row_dev, nb), f32),
            pltpu.VMEM((nb, nb), f32),
            pltpu.VMEM((nb, cols), jnp.bfloat16),
            pltpu.VMEM((nb, cols), jnp.bfloat16),
            pltpu.VMEM((row_dev, cols), f32),
        ] + [pltpu.SemaphoreType.DMA] * 4,
        vmem=30 << 20,
        flops=2 * row_dev * nb * cols * 3,
        moved=4 * row_dev * (2 * cols + nb),
    )(here, table, choice, displaced, weights, top, matrix, *bufs, *tops)


def solution(mesh):
    n_rows, n_cols = mesh.shape["prow"], mesh.shape["pcol"]
    return jax.shard_map(
        functools.partial(local, n_rows=n_rows, n_cols=n_cols, parts=8),
        mesh=mesh,
        in_specs=(P("prow", "pcol"), P(), P(), P()),
        out_specs=P("prow", "pcol"),
        check_vma=False,
    )
```

```python
import functools

import jax
import jax.numpy as jnp
from jax import lax
from jax.experimental import pallas as pl
from jax.experimental.pallas import tpu as pltpu
from jax.sharding import PartitionSpec as P

VMEM = pl.BlockSpec(memory_space=pltpu.VMEM)
SMEM = pl.BlockSpec(memory_space=pltpu.SMEM)
ANY = pl.BlockSpec(memory_space=pl.ANY)
LANES = 128
PICK, FROM, ROW, COUNT, TOP, EARLY = 0, 1, 2, 3, 4, 5


def call(kernel, out, ins, outs, scratch=(), vmem=16 << 20, flops=0, moved=0):
    return pl.pallas_call(
        kernel,
        out_shape=out,
        in_specs=ins,
        out_specs=outs,
        scratch_shapes=list(scratch),
        compiler_params=pltpu.CompilerParams(vmem_limit_bytes=vmem),
        cost_estimate=pl.CostEstimate(
            flops=flops, bytes_accessed=moved, transcendentals=0
        ),
    )


def index_kernel(where_ref, pivots_ref, table_ref, owner_ref, *, row_dev):
    nb = pivots_ref.shape[1]
    start = where_ref[0] * row_dev
    first = where_ref[0] == 0
    down = lax.broadcasted_iota(jnp.int32, (nb, nb), 0)
    across = lax.broadcasted_iota(jnp.int32, (nb, nb), 1)
    piv_row = jnp.broadcast_to(pivots_ref[...], (nb, nb))

    def column(full):
        return jnp.sum(jnp.where(down == across, full, 0.0), axis=1, keepdims=True)

    piv_f = piv_row.astype(jnp.float32)
    piv_col = jnp.broadcast_to(column(piv_f), (nb, nb))
    upto = (down <= across).astype(jnp.bfloat16)
    below = (piv_row >= nb).astype(jnp.float32)
    vacancy = jnp.dot(
        below[:8].astype(jnp.bfloat16), upto, preferred_element_type=jnp.float32
    )[:1]
    taken = jnp.max((piv_row == down).astype(jnp.float32), axis=1, keepdims=True)
    freed = jnp.broadcast_to(1.0 - taken, (nb, LANES))
    rank = jnp.dot(
        (across <= down).astype(jnp.bfloat16),
        freed.astype(jnp.bfloat16),
        preferred_element_type=jnp.float32,
    )[:, :1]
    down_f = down.astype(jnp.float32)
    pair = (rank == vacancy) & (freed[:, :1] > 0.5)
    source = jnp.sum(jnp.where(pair, down_f, 0.0), axis=0, keepdims=True)
    source_col = jnp.broadcast_to(column(jnp.broadcast_to(source, (nb, nb))), (nb, nb))

    own_row = (pivots_ref[...] >= start) & (pivots_ref[...] < start + row_dev)
    pick = jnp.where(own_row, pivots_ref[...] - start, source.astype(jnp.int32))
    moved_row = (own_row & (pivots_ref[...] >= nb)).astype(jnp.float32)
    start_f = start.astype(jnp.float32)
    moved_col = (
        (piv_col >= start_f) & (piv_col < start_f + row_dev) & (piv_col >= nb)
    )
    order = jnp.sum(
        jnp.where(piv_f < piv_col, jnp.broadcast_to(moved_row, (nb, nb)), 0.0),
        axis=1,
        keepdims=True,
    )
    placed = moved_col & (order == across.astype(jnp.float32))
    origin = jnp.where(first, source_col, down_f)
    listed_from = jnp.sum(jnp.where(placed, origin, 0.0), axis=0, keepdims=True)
    listed_row = jnp.sum(
        jnp.where(placed, piv_col - start_f, 0.0), axis=0, keepdims=True
    )
    listed_top = jnp.sum(jnp.where(placed, source_col, 0.0), axis=0, keepdims=True)
    count = jnp.sum(moved_row, axis=1, keepdims=True)
    table_ref[...] = jnp.zeros_like(table_ref)
    table_ref[PICK : PICK + 1, :] = pick
    table_ref[FROM : FROM + 1, :] = listed_from.astype(jnp.int32)
    table_ref[ROW : ROW + 1, :] = listed_row.astype(jnp.int32)
    near = jnp.where(pivots_ref[...] - start < row_dev // 2, moved_row, 0.0)
    early = jnp.sum(near, axis=1, keepdims=True)
    table_ref[EARLY : EARLY + 1, :] = jnp.broadcast_to(early.astype(jnp.int32), (1, nb))
    table_ref[TOP : TOP + 1, :] = listed_top.astype(jnp.int32)
    table_ref[COUNT : COUNT + 1, :] = jnp.broadcast_to(
        count.astype(jnp.int32), (1, nb)
    )
    owner_ref[...] = piv_col[:, :LANES].astype(jnp.int32) // row_dev


def gather_kernel(table_ref, matrix_ref, out_ref):
    nb = out_ref.shape[0]

    @pl.loop(0, nb, step=8)
    def _(base):
        rows = [matrix_ref[pl.ds(table_ref[PICK, base + k], 1), :] for k in range(8)]
        for k, row in enumerate(rows):
            out_ref[pl.ds(base + k, 1), :] = row


def merge_kernel(where_ref, owner_ref, held_ref, *refs, log, halves):
    arrived, (merged_ref, half_ref) = refs[: 2 if halves else 1], refs[-2:]
    me = where_ref[0]
    mine, theirs = me >> log, (me >> log) ^ 1
    odd = me & 1
    nb, cols = held_ref.shape
    half = nb // 2

    def merge(rows, piece):
        group = owner_ref[rows, :] >> log
        take = (group == theirs) | ((theirs == 0) & (group != mine))
        for q in range(cols // LANES):
            lane = slice(q * LANES, (q + 1) * LANES)
            merged_ref[rows, lane] = jnp.where(take, piece[:, lane], held_ref[rows, lane])

    low, high = slice(0, half), slice(half, nb)
    if halves:
        @pl.when(odd == 0)
        def _():
            merge(low, arrived[0])
            merge(high, arrived[1])

        @pl.when(odd == 1)
        def _():
            merge(low, arrived[1])
            merge(high, arrived[0])
    else:
        merge(slice(0, nb), arrived[0])

    @pl.when(odd == 0)
    def _():
        half_ref[...] = merged_ref[low, :]

    @pl.when(odd == 1)
    def _():
        half_ref[...] = merged_ref[high, :]


def split(x):
    hi = x.astype(jnp.bfloat16)
    return hi, (x - hi.astype(jnp.float32)).astype(jnp.bfloat16)


def product(a, b):
    dot = functools.partial(jnp.dot, preferred_element_type=jnp.float32)
    return dot(a[1], b[0]) + dot(a[0], b[1]) + dot(a[0], b[0])


def factor_kernel(where_ref, top_in_ref, lower_ref, upper_ref, weights_ref, top_ref):
    nb = top_in_ref.shape[0]
    u = product(split(lower_ref[...]), split(top_in_ref[...]))
    top_ref[...] = u
    weights_ref[...] = product(split(upper_ref[...]), split(u))

    @pl.when(where_ref[1] == 0)
    def _():
        top_ref[:, :nb] = top_in_ref[:, :nb]
        weights_ref[:, :nb] = -upper_ref[...]


def fetch(choice_ref, bufs, place, sem, n_cols, parts, pairs):
    for i in range(pairs):
        for h in range(2):
            for b in sorted({arrival(p, i, h, n_cols, parts) for p in range(1, n_cols)}):
                @pl.when(choice_ref[2 * i + h] == b)
                def _():
                    pltpu.make_async_copy(bufs[b], place(i, h), sem(i)).start()


def old_top_kernel(where_ref, choice_ref, matrix_ref, *refs, used, n_cols, parts, pairs):
    bufs, top_ref, sem = dict(zip(used, refs)), refs[-2], refs[-1]
    nb = top_ref.shape[0]
    chunk = nb // (2 * pairs)
    from_matrix = pltpu.make_async_copy(
        matrix_ref.at[pl.ds(0, nb), pl.ds(0, nb)], top_ref, sem
    )

    @pl.when(where_ref[0] == 0)
    def _():
        @pl.when(where_ref[1] == 0)
        def _():
            from_matrix.start()

        @pl.when(where_ref[1] > 0)
        def _():
            fetch(
                choice_ref, bufs,
                lambda i, h: top_ref.at[pl.ds((2 * i + h) * chunk, chunk), :],
                lambda i: sem, n_cols, parts, pairs,
            )

        from_matrix.wait()


def final_kernel(
    where_ref, table_ref, choice_ref, displaced_ref, weights_ref, top_ref, matrix_ref,
    *refs, n_bufs, n_tops, n_cols, parts, block,
):
    bufs, tops, out_ref = refs[:n_bufs], refs[n_bufs : n_bufs + n_tops], refs[n_bufs + n_tops]
    mat, pan, low, w_hi, w_lo, result, in_sem, low_sem, mat_sem, out_sem = refs[
        n_bufs + n_tops + 1 :
    ]
    rows, cols = matrix_ref.shape
    nb = weights_ref.shape[0]
    half = nb // 2
    chunk = rows // (2 * parts)
    row = where_ref[0]
    first_row, first_col = row == 0, where_ref[1] == 0

    middle = rows // 2
    sides = [pl.ds(0, middle), pl.ds(middle, middle)]
    loads = [
        pltpu.make_async_copy(matrix_ref.at[side, :], mat.at[side, :], mat_sem.at[k])
        for k, side in enumerate(sides)
    ]
    panels = [
        pltpu.make_async_copy(matrix_ref.at[side, pl.ds(0, nb)], pan.at[side, :], in_sem.at[k])
        for k, side in enumerate(sides)
    ]
    loads[0].start()

    @pl.when(first_col)
    def _():
        for panel in panels:
            panel.start()

    @pl.when(jnp.logical_not(first_col))
    def _():
        fetch(
            choice_ref, bufs, lambda i, h: pan.at[pl.ds((2 * i + h) * chunk, chunk), :],
            lambda i: in_sem.at[2 * i // parts], n_cols, parts, parts,
        )

    @pl.when(row == 1)
    def _():
        pltpu.make_async_copy(tops[0], low, low_sem).start()

    for log in range(1, (n_tops + 1) // 2):
        for odd in range(2):
            @pl.when(((row >> log) == 1) & ((row & 1) == odd))
            def _():
                for part, ref in enumerate(tops[2 * log - 1 : 2 * log + 1]):
                    at = half * (part ^ odd)
                    pltpu.make_async_copy(ref, low.at[pl.ds(at, half), :], low_sem).start()

    loads[1].start()
    w = weights_ref[...]
    w_hi[...] = w.astype(jnp.bfloat16)
    w_lo[...] = (w - w_hi[...].astype(jnp.float32)).astype(jnp.bfloat16)

    @pl.when(jnp.logical_not(first_row))
    def _():
        pltpu.make_async_copy(tops[0], low, low_sem).wait()

    def swap(from_mat, from_pan, begin, end):
        def body(turn, _):
            at = [jnp.minimum(begin + 4 * turn + k, end - 1) for k in range(4)]
            mats = [from_mat[pl.ds(table_ref[FROM, k], 1), :] for k in at]
            pans = [from_pan[pl.ds(table_ref[TOP, k], 1), :] for k in at]
            for k, row_mat, row_pan in zip(at, mats, pans):
                mat[pl.ds(table_ref[ROW, k], 1), :] = row_mat
                pan[pl.ds(table_ref[ROW, k], 1), :] = row_pan
            return 0

        lax.fori_loop(0, (end - begin + 3) // 4, body, 0)

    copies = []
    for b in range(rows // block):
        span = pl.ds(b * block, block)
        if b * block % middle == 0:
            k = b * block // middle
            panels[k].wait()
            loads[k].wait()
            begin = table_ref[EARLY, 0] if k else 0
            end = table_ref[COUNT if k else EARLY, 0]

            @pl.when(first_row)
            def _():
                swap(mat, pan, begin, end)

            @pl.when(jnp.logical_not(first_row))
            def _():
                swap(displaced_ref, low, begin, end)

            @pl.when(first_col)
            def _():
                mat[sides[k], :nb] = jnp.zeros((middle, nb), jnp.float32)

        def update():
            p = pan[span, :]
            p_hi = p.astype(jnp.bfloat16)
            p_lo = (p - p_hi.astype(jnp.float32)).astype(jnp.bfloat16)
            dot = functools.partial(jnp.dot, preferred_element_type=jnp.float32)
            total = dot(p_lo, w_hi[...]) + dot(p_hi, w_lo[...]) + dot(p_hi, w_hi[...])
            result[span, :] = mat[span, :] - total

        if (b + 1) * block <= nb:
            pl.when(jnp.logical_not(first_row))(update)

            @pl.when(first_row)
            def _():
                result[span, :] = top_ref[span, :]
        else:
            update()
        copy = pltpu.make_async_copy(result.at[span, :], out_ref.at[span, :], out_sem)
        copy.start()
        copies.append(copy)
    for copy in copies:
        copy.wait()


LAG = 2


def steps(n_cols, parts):
    depth = n_cols // 2
    return parts + LAG * (depth - 1), max(2 * parts, parts + LAG * depth)


def arrival(p, i, h, n_cols, parts):
    z, y = divmod(p, 2)
    cross = steps(n_cols, parts)[0]
    if z == 0:
        return cross + i + h * parts
    if y == 0:
        return cross + i + LAG * (z + 1) if h == 0 else i + LAG * (z - 1)
    return i + LAG * z if h == 0 else cross + i + LAG * z


def spread(pieces, col, n_cols, riders):
    parts = len(pieces)
    n_chain, n_cross = steps(n_cols, parts)
    along = [(p, p + 2) for p in range(n_cols - 2)]
    across = [(0, 1)] + [(p, p ^ 1) for p in range(2, n_cols)]
    chain, cross = [], []
    waiting = [(rider, next(rider)(chain, cross)) for rider in riders]
    for s in range(n_cross):
        ahead = pieces[min(s, parts - 1)][1]
        aside = pieces[s][0] if s < parts else pieces[min(s - parts, parts - 1)][1]
        if s >= LAG:
            came = chain[s - LAG] if s - LAG < n_chain else chain[-1]
            due = [k for k, (_, (at, _)) in enumerate(waiting) if at == s]
            tied = [waiting[k][1][1] for k in due]
            (came, fed), tied = lax.optimization_barrier(((came, cross[s - LAG]), tied))
            ahead = jnp.where(col == 0, ahead, jnp.where(col == 1, fed, came))
            aside = jnp.where(col == 0, aside, came)
        if s < n_chain:
            chain.append(lax.ppermute(ahead, "pcol", along))
        cross.append(lax.ppermute(aside, "pcol", across))
        if s >= LAG:
            for k, values in zip(due, tied):
                rider = waiting[k][0]
                waiting[k] = (rider, resume(rider, values, chain, cross))
    results = []
    for rider, (at, values) in waiting:
        while at != DONE:
            at, values = resume(rider, values, chain, cross)
        results.append(values)
    return chain, cross, results


DONE = -1


def resume(rider, values, chain, cross):
    return rider.send(values)(chain, cross)


def give(at, values):
    return lambda chain, cross: (at, values)


def local(matrix, pivots, lower_inverse, upper_inverse, *, n_rows, n_cols, parts):
    row_dev, cols = matrix.shape
    nb = pivots.shape[0]
    f32 = jnp.float32
    row, col = lax.axis_index("prow"), lax.axis_index("pcol")
    here = jnp.stack([row, col]).astype(jnp.int32)
    odd = row % 2 == 1

    chunk = row_dev // (2 * parts)
    flat = [
        lax.slice(matrix, (k * chunk, 0), ((k + 1) * chunk, nb)) for k in range(2 * parts)
    ]
    flat = flat[:2] + list(lax.optimization_barrier(tuple(flat[2:])))
    choice = jnp.asarray(
        [
            [0] * (2 * parts) if p == 0 else
            [arrival(p, i, h, n_cols, parts) for i in range(parts) for h in range(2)]
            for p in range(n_cols)
        ],
        jnp.int32,
    )[col]

    pairs = nb // (2 * chunk)
    used = sorted({
        arrival(p, i, h, n_cols, parts)
        for p in range(1, n_cols) for i in range(pairs) for h in range(2)
    })
    n_chain = steps(n_cols, parts)[0]
    last = max(b - n_chain if b >= n_chain else b for b in used)

    def both_halves(one, two):
        return jnp.concatenate([jnp.where(odd, two, one), jnp.where(odd, one, two)], axis=0)

    def old_top_rider():
        at = last + LAG

        def start(chain, cross):
            return at, [chain[b] if b < n_chain else cross[b - n_chain] for b in used]

        arrived = yield give(at - 1, ())
        arrived = yield start
        old_top = call(
            functools.partial(
                old_top_kernel, used=used, n_cols=n_cols, parts=parts, pairs=pairs
            ),
            jax.ShapeDtypeStruct((nb, nb), f32),
            [SMEM, SMEM, ANY] + [ANY] * len(used), ANY, [pltpu.SemaphoreType.DMA],
            vmem=4 << 20,
        )(here, choice, matrix, *arrived)
        tops = []
        log = 0
        while (1 << log) < n_rows:
            d = 1 << log
            far = [(p, p + d) for p in range(d)]
            if log == 0:
                at += 2
                whole = yield give(at, lax.ppermute(old_top, "prow", far))
                tops.append(whole)
            else:
                half = jnp.where(odd, old_top[nb // 2 :], old_top[: nb // 2])
                at += 3
                one = yield give(at, lax.ppermute(half, "prow", far))
                two = lax.ppermute(one, "prow", [(p, p ^ 1) for p in range(d, 2 * d)])
                tops += [one, two]
                whole = both_halves(one, two)
            old_top = jnp.where((row >> log) == 1, whole, old_top)
            log += 1
        yield give(DONE, tops)

    slot = jax.ShapeDtypeStruct((nb, cols), f32)
    half_slot = jax.ShapeDtypeStruct((nb // 2, cols), f32)

    def exchange_rider():
        table, owner = yield give(2, call(
            functools.partial(index_kernel, row_dev=row_dev),
            (jax.ShapeDtypeStruct((8, nb), jnp.int32), jax.ShapeDtypeStruct((nb, LANES), jnp.int32)),
            [SMEM, VMEM], (VMEM, VMEM),
        )(here, pivots.reshape(1, nb)))
        held = yield give(3, call(gather_kernel, slot, [SMEM, VMEM], VMEM)(table, matrix))
        at = 5
        displaced = held
        log = 0
        half = None
        while (1 << log) < n_rows:
            d = 1 << log
            far = [(p, p ^ d) for p in range(n_rows)]
            if log == 0:
                whole = yield give(at, lax.ppermute(held, "prow", far))
                arrived = [whole]
            else:
                near = [(p, p ^ 1) for p in range(n_rows)]
                one = yield give(at + 4, lax.ppermute(half, "prow", far))
                at += 5
                two = yield give(at, lax.ppermute(one, "prow", near))
                arrived = [one, two]
                whole = both_halves(one, two)
            held, half = call(
                functools.partial(merge_kernel, log=log, halves=log > 0),
                (slot, half_slot), [SMEM] + [VMEM] * (2 + len(arrived)), (VMEM, VMEM),
            )(here, owner, held, *arrived)
            displaced = jnp.where((row >> log) == 1, whole, displaced)
            log += 1
        held, displaced = yield give(at + 1, (held, displaced))
        weights, top = yield give(at + 2, call(
            factor_kernel, (slot, slot), [SMEM, VMEM, VMEM, VMEM], (VMEM, VMEM),
            flops=4 * nb * nb * cols * 6,
        )(here, held, lower_inverse, upper_inverse))
        yield give(DONE, (table, displaced, weights, top))

    chain, cross, (tops, (table, displaced, weights, top)) = spread(
        [(flat[2 * i], flat[2 * i + 1]) for i in range(parts)], col, n_cols,
        [old_top_rider(), exchange_rider()],
    )
    bufs = chain + cross

    return call(
        functools.partial(
            final_kernel, n_bufs=len(bufs), n_tops=len(tops), n_cols=n_cols, parts=parts,
            block=256,
        ),
        jax.ShapeDtypeStruct(matrix.shape, f32),
        [SMEM, SMEM, SMEM, VMEM, VMEM, VMEM, ANY] + [ANY] * (len(bufs) + len(tops)),
        ANY,
        [
            pltpu.VMEM((row_dev, cols), f32),
            pltpu.VMEM((row_dev, nb), f32),
            pltpu.VMEM((nb, nb), f32),
            pltpu.VMEM((nb, cols), jnp.bfloat16),
            pltpu.VMEM((nb, cols), jnp.bfloat16),
            pltpu.VMEM((row_dev, cols), f32),
            pltpu.SemaphoreType.DMA((2,)),
            pltpu.SemaphoreType.DMA,
            pltpu.SemaphoreType.DMA((2,)),
            pltpu.SemaphoreType.DMA,
        ],
        vmem=30 << 20,
        flops=2 * row_dev * nb * cols * 3,
        moved=4 * row_dev * (2 * cols + nb),
    )(here, table, choice, displaced, weights, top, matrix, *bufs, *tops)


def solution(mesh):
    n_rows, n_cols = mesh.shape["prow"], mesh.shape["pcol"]
    return jax.shard_map(
        functools.partial(local, n_rows=n_rows, n_cols=n_cols, parts=8),
        mesh=mesh,
        in_specs=(P("prow", "pcol"), P(), P(), P()),
        out_specs=P("prow", "pcol"),
        check_vma=False,
    )
```

```python
import functools

import jax
import jax.numpy as jnp
from jax import lax
from jax.experimental import pallas as pl
from jax.experimental.pallas import tpu as pltpu
from jax.sharding import PartitionSpec as P

VMEM = pl.BlockSpec(memory_space=pltpu.VMEM)
SMEM = pl.BlockSpec(memory_space=pltpu.SMEM)
ANY = pl.BlockSpec(memory_space=pl.ANY)
LANES = 128
PICK, FROM, ROW, COUNT, TOP, EARLY = 0, 1, 2, 3, 4, 5


def call(kernel, out, ins, outs, scratch=(), vmem=16 << 20, flops=0, moved=0):
    return pl.pallas_call(
        kernel,
        out_shape=out,
        in_specs=ins,
        out_specs=outs,
        scratch_shapes=list(scratch),
        compiler_params=pltpu.CompilerParams(vmem_limit_bytes=vmem),
        cost_estimate=pl.CostEstimate(
            flops=flops, bytes_accessed=moved, transcendentals=0
        ),
    )


def index_kernel(where_ref, pivots_ref, table_ref, owner_ref, *, row_dev):
    nb = pivots_ref.shape[1]
    start = where_ref[0] * row_dev
    first = where_ref[0] == 0
    down = lax.broadcasted_iota(jnp.int32, (nb, nb), 0)
    across = lax.broadcasted_iota(jnp.int32, (nb, nb), 1)
    piv_row = jnp.broadcast_to(pivots_ref[...], (nb, nb))

    def column(full):
        return jnp.sum(jnp.where(down == across, full, 0.0), axis=1, keepdims=True)

    piv_f = piv_row.astype(jnp.float32)
    piv_col = jnp.broadcast_to(column(piv_f), (nb, nb))
    upto = (down <= across).astype(jnp.bfloat16)
    below = (piv_row >= nb).astype(jnp.float32)
    vacancy = jnp.dot(
        below[:8].astype(jnp.bfloat16), upto, preferred_element_type=jnp.float32
    )[:1]
    taken = jnp.max((piv_row == down).astype(jnp.float32), axis=1, keepdims=True)
    freed = jnp.broadcast_to(1.0 - taken, (nb, LANES))
    rank = jnp.dot(
        (across <= down).astype(jnp.bfloat16),
        freed.astype(jnp.bfloat16),
        preferred_element_type=jnp.float32,
    )[:, :1]
    down_f = down.astype(jnp.float32)
    pair = (rank == vacancy) & (freed[:, :1] > 0.5)
    source = jnp.sum(jnp.where(pair, down_f, 0.0), axis=0, keepdims=True)
    source_col = jnp.broadcast_to(column(jnp.broadcast_to(source, (nb, nb))), (nb, nb))

    own_row = (pivots_ref[...] >= start) & (pivots_ref[...] < start + row_dev)
    pick = jnp.where(own_row, pivots_ref[...] - start, source.astype(jnp.int32))
    moved_row = (own_row & (pivots_ref[...] >= nb)).astype(jnp.float32)
    start_f = start.astype(jnp.float32)
    moved_col = (
        (piv_col >= start_f) & (piv_col < start_f + row_dev) & (piv_col >= nb)
    )
    order = jnp.sum(
        jnp.where(piv_f < piv_col, jnp.broadcast_to(moved_row, (nb, nb)), 0.0),
        axis=1,
        keepdims=True,
    )
    placed = moved_col & (order == across.astype(jnp.float32))
    origin = jnp.where(first, source_col, down_f)
    listed_from = jnp.sum(jnp.where(placed, origin, 0.0), axis=0, keepdims=True)
    listed_row = jnp.sum(
        jnp.where(placed, piv_col - start_f, 0.0), axis=0, keepdims=True
    )
    listed_top = jnp.sum(jnp.where(placed, source_col, 0.0), axis=0, keepdims=True)
    count = jnp.sum(moved_row, axis=1, keepdims=True)
    table_ref[...] = jnp.zeros_like(table_ref)
    table_ref[PICK : PICK + 1, :] = pick
    table_ref[FROM : FROM + 1, :] = listed_from.astype(jnp.int32)
    table_ref[ROW : ROW + 1, :] = listed_row.astype(jnp.int32)
    near = jnp.where(pivots_ref[...] - start < row_dev // 2, moved_row, 0.0)
    early = jnp.sum(near, axis=1, keepdims=True)
    table_ref[EARLY : EARLY + 1, :] = jnp.broadcast_to(early.astype(jnp.int32), (1, nb))
    table_ref[TOP : TOP + 1, :] = listed_top.astype(jnp.int32)
    table_ref[COUNT : COUNT + 1, :] = jnp.broadcast_to(
        count.astype(jnp.int32), (1, nb)
    )
    owner_ref[...] = piv_col[:, :LANES].astype(jnp.int32) // row_dev


def gather_kernel(table_ref, matrix_ref, out_ref):
    nb = out_ref.shape[0]

    @pl.loop(0, nb, step=8)
    def _(base):
        rows = [matrix_ref[pl.ds(table_ref[PICK, base + k], 1), :] for k in range(8)]
        for k, row in enumerate(rows):
            out_ref[pl.ds(base + k, 1), :] = row


def merge_kernel(where_ref, owner_ref, held_ref, *refs, log, halves):
    arrived, (merged_ref, half_ref) = refs[: 2 if halves else 1], refs[-2:]
    me = where_ref[0]
    mine, theirs = me >> log, (me >> log) ^ 1
    odd = me & 1
    nb, cols = held_ref.shape
    half = nb // 2

    def merge(rows, piece):
        group = owner_ref[rows, :] >> log
        take = (group == theirs) | ((theirs == 0) & (group != mine))
        for q in range(cols // LANES):
            lane = slice(q * LANES, (q + 1) * LANES)
            merged_ref[rows, lane] = jnp.where(take, piece[:, lane], held_ref[rows, lane])

    low, high = slice(0, half), slice(half, nb)
    if halves:
        @pl.when(odd == 0)
        def _():
            merge(low, arrived[0])
            merge(high, arrived[1])

        @pl.when(odd == 1)
        def _():
            merge(low, arrived[1])
            merge(high, arrived[0])
    else:
        merge(slice(0, nb), arrived[0])

    @pl.when(odd == 0)
    def _():
        half_ref[...] = merged_ref[low, :]

    @pl.when(odd == 1)
    def _():
        half_ref[...] = merged_ref[high, :]


def split(x):
    hi = x.astype(jnp.bfloat16)
    return hi, (x - hi.astype(jnp.float32)).astype(jnp.bfloat16)


def product(a, b):
    dot = functools.partial(jnp.dot, preferred_element_type=jnp.float32)
    return dot(a[1], b[0]) + dot(a[0], b[1]) + dot(a[0], b[0])


def factor_kernel(where_ref, top_in_ref, lower_ref, upper_ref, weights_ref, top_ref):
    nb = top_in_ref.shape[0]
    u = product(split(lower_ref[...]), split(top_in_ref[...]))
    top_ref[...] = u
    weights_ref[...] = product(split(upper_ref[...]), split(u))

    @pl.when(where_ref[1] == 0)
    def _():
        top_ref[:, :nb] = top_in_ref[:, :nb]
        weights_ref[:, :nb] = -upper_ref[...]


def fetch(choice_ref, bufs, place, sem, n_cols, parts, pairs):
    for i in range(pairs):
        for h in range(2):
            for b in sorted({arrival(p, i, h, n_cols, parts) for p in range(1, n_cols)}):
                @pl.when(choice_ref[2 * i + h] == b)
                def _():
                    pltpu.make_async_copy(bufs[b], place(i, h), sem(i)).start()


def old_top_kernel(where_ref, choice_ref, matrix_ref, *refs, used, n_cols, parts, pairs):
    bufs, top_ref, sem = dict(zip(used, refs)), refs[-2], refs[-1]
    nb = top_ref.shape[0]
    chunk = nb // (2 * pairs)
    from_matrix = pltpu.make_async_copy(
        matrix_ref.at[pl.ds(0, nb), pl.ds(0, nb)], top_ref, sem
    )

    @pl.when(where_ref[0] == 0)
    def _():
        @pl.when(where_ref[1] == 0)
        def _():
            from_matrix.start()

        @pl.when(where_ref[1] > 0)
        def _():
            fetch(
                choice_ref, bufs,
                lambda i, h: top_ref.at[pl.ds((2 * i + h) * chunk, chunk), :],
                lambda i: sem, n_cols, parts, pairs,
            )

        from_matrix.wait()


def final_kernel(
    where_ref, table_ref, choice_ref, displaced_ref, weights_ref, top_ref, matrix_ref,
    *refs, n_bufs, n_tops, n_cols, parts, block,
):
    bufs, tops, out_ref = refs[:n_bufs], refs[n_bufs : n_bufs + n_tops], refs[n_bufs + n_tops]
    mat, pan, low, w_hi, w_lo, result, in_sem, low_sem, mat_sem, out_sem = refs[
        n_bufs + n_tops + 1 :
    ]
    rows, cols = matrix_ref.shape
    nb = weights_ref.shape[0]
    half = nb // 2
    chunk = rows // (2 * parts)
    row = where_ref[0]
    first_row, first_col = row == 0, where_ref[1] == 0

    middle = rows // 2
    sides = [pl.ds(0, middle), pl.ds(middle, middle)]
    loads = [
        pltpu.make_async_copy(matrix_ref.at[side, :], mat.at[side, :], mat_sem.at[k])
        for k, side in enumerate(sides)
    ]
    panels = [
        pltpu.make_async_copy(matrix_ref.at[side, pl.ds(0, nb)], pan.at[side, :], in_sem.at[k])
        for k, side in enumerate(sides)
    ]
    loads[0].start()

    @pl.when(first_col)
    def _():
        for panel in panels:
            panel.start()

    @pl.when(jnp.logical_not(first_col))
    def _():
        fetch(
            choice_ref, bufs, lambda i, h: pan.at[pl.ds((2 * i + h) * chunk, chunk), :],
            lambda i: in_sem.at[2 * i // parts], n_cols, parts, parts,
        )

    @pl.when(row == 1)
    def _():
        pltpu.make_async_copy(tops[0], low, low_sem).start()

    for log in range(1, (n_tops + 1) // 2):
        for odd in range(2):
            @pl.when(((row >> log) == 1) & ((row & 1) == odd))
            def _():
                for part, ref in enumerate(tops[2 * log - 1 : 2 * log + 1]):
                    at = half * (part ^ odd)
                    pltpu.make_async_copy(ref, low.at[pl.ds(at, half), :], low_sem).start()

    loads[1].start()
    w = weights_ref[...]
    w_hi[...] = w.astype(jnp.bfloat16)
    w_lo[...] = (w - w_hi[...].astype(jnp.float32)).astype(jnp.bfloat16)

    @pl.when(jnp.logical_not(first_row))
    def _():
        pltpu.make_async_copy(tops[0], low, low_sem).wait()

    def swap(from_mat, from_pan, begin, end):
        def body(turn, _):
            at = [jnp.minimum(begin + 4 * turn + k, end - 1) for k in range(4)]
            mats = [from_mat[pl.ds(table_ref[FROM, k], 1), :] for k in at]
            pans = [from_pan[pl.ds(table_ref[TOP, k], 1), :] for k in at]
            for k, row_mat, row_pan in zip(at, mats, pans):
                mat[pl.ds(table_ref[ROW, k], 1), :] = row_mat
                pan[pl.ds(table_ref[ROW, k], 1), :] = row_pan
            return 0

        lax.fori_loop(0, (end - begin + 3) // 4, body, 0)

    copies = []
    for b in range(rows // block):
        span = pl.ds(b * block, block)
        if b * block % middle == 0:
            k = b * block // middle
            panels[k].wait()
            loads[k].wait()
            begin = table_ref[EARLY, 0] if k else 0
            end = table_ref[COUNT if k else EARLY, 0]

            @pl.when(first_row)
            def _():
                swap(mat, pan, begin, end)

            @pl.when(jnp.logical_not(first_row))
            def _():
                swap(displaced_ref, low, begin, end)

            @pl.when(first_col)
            def _():
                mat[sides[k], :nb] = jnp.zeros((middle, nb), jnp.float32)

        def update():
            p = pan[span, :]
            p_hi = p.astype(jnp.bfloat16)
            p_lo = (p - p_hi.astype(jnp.float32)).astype(jnp.bfloat16)
            dot = functools.partial(jnp.dot, preferred_element_type=jnp.float32)
            total = dot(p_lo, w_hi[...]) + dot(p_hi, w_lo[...]) + dot(p_hi, w_hi[...])
            result[span, :] = mat[span, :] - total

        if (b + 1) * block <= nb:
            pl.when(jnp.logical_not(first_row))(update)

            @pl.when(first_row)
            def _():
                result[span, :] = top_ref[span, :]
        else:
            update()
        copy = pltpu.make_async_copy(result.at[span, :], out_ref.at[span, :], out_sem)
        copy.start()
        copies.append(copy)
    for copy in copies:
        copy.wait()


LAG = 2


def steps(n_cols, parts):
    depth = n_cols // 2
    return parts + LAG * (depth - 1), max(2 * parts, parts + LAG * depth)


def arrival(p, i, h, n_cols, parts):
    z, y = divmod(p, 2)
    cross = steps(n_cols, parts)[0]
    if z == 0:
        return cross + i + h * parts
    if y == 0:
        return cross + i + LAG * (z + 1) if h == 0 else i + LAG * (z - 1)
    return i + LAG * z if h == 0 else cross + i + LAG * z


def spread(pieces, col, n_cols, riders):
    parts = len(pieces)
    n_chain, n_cross = steps(n_cols, parts)
    along = [(p, p + 2) for p in range(n_cols - 2)]
    across = [(0, 1)] + [(p, p ^ 1) for p in range(2, n_cols)]
    chain, cross = [], []
    waiting = [(rider, next(rider)(chain, cross)) for rider in riders]
    for s in range(n_cross):
        ahead = pieces[min(s, parts - 1)][1]
        aside = pieces[s][0] if s < parts else pieces[min(s - parts, parts - 1)][1]
        if s >= LAG:
            came = chain[s - LAG] if s - LAG < n_chain else chain[-1]
            due = [k for k, (_, (at, _)) in enumerate(waiting) if at == s]
            tied = [waiting[k][1][1] for k in due]
            (came, fed), tied = lax.optimization_barrier(((came, cross[s - LAG]), tied))
            ahead = jnp.where(col == 0, ahead, jnp.where(col == 1, fed, came))
            aside = jnp.where(col == 0, aside, came)
        if s < n_chain:
            chain.append(lax.ppermute(ahead, "pcol", along))
        cross.append(lax.ppermute(aside, "pcol", across))
        if s >= LAG:
            for k, values in zip(due, tied):
                rider = waiting[k][0]
                waiting[k] = (rider, resume(rider, values, chain, cross))
    results = []
    for rider, (at, values) in waiting:
        while at != DONE:
            at, values = resume(rider, values, chain, cross)
        results.append(values)
    return chain, cross, results


DONE = -1


def resume(rider, values, chain, cross):
    return rider.send(values)(chain, cross)


def give(at, values):
    return lambda chain, cross: (at, values)


def local(matrix, pivots, lower_inverse, upper_inverse, *, n_rows, n_cols, parts):
    row_dev, cols = matrix.shape
    nb = pivots.shape[0]
    f32 = jnp.float32
    row, col = lax.axis_index("prow"), lax.axis_index("pcol")
    here = jnp.stack([row, col]).astype(jnp.int32)
    odd = row % 2 == 1

    chunk = row_dev // (2 * parts)
    flat = [
        lax.slice(matrix, (k * chunk, 0), ((k + 1) * chunk, nb)) for k in range(2 * parts)
    ]
    flat = flat[:2] + list(lax.optimization_barrier(tuple(flat[2:])))
    choice = jnp.asarray(
        [
            [0] * (2 * parts) if p == 0 else
            [arrival(p, i, h, n_cols, parts) for i in range(parts) for h in range(2)]
            for p in range(n_cols)
        ],
        jnp.int32,
    )[col]

    pairs = nb // (2 * chunk)
    used = sorted({
        arrival(p, i, h, n_cols, parts)
        for p in range(1, n_cols) for i in range(pairs) for h in range(2)
    })
    n_chain = steps(n_cols, parts)[0]
    last = max(b - n_chain if b >= n_chain else b for b in used)

    def both_halves(one, two):
        return jnp.concatenate([jnp.where(odd, two, one), jnp.where(odd, one, two)], axis=0)

    def old_top_rider():
        at = last + LAG

        def start(chain, cross):
            return at, [chain[b] if b < n_chain else cross[b - n_chain] for b in used]

        arrived = yield give(at - 1, ())
        arrived = yield start
        old_top = call(
            functools.partial(
                old_top_kernel, used=used, n_cols=n_cols, parts=parts, pairs=pairs
            ),
            jax.ShapeDtypeStruct((nb, nb), f32),
            [SMEM, SMEM, ANY] + [ANY] * len(used), ANY, [pltpu.SemaphoreType.DMA],
            vmem=4 << 20,
        )(here, choice, matrix, *arrived)
        tops = []
        log = 0
        while (1 << log) < n_rows:
            d = 1 << log
            far = [(p, p + d) for p in range(d)]
            if log == 0:
                at += 2
                whole = yield give(at, lax.ppermute(old_top, "prow", far))
                tops.append(whole)
            else:
                half = jnp.where(odd, old_top[nb // 2 :], old_top[: nb // 2])
                at += 3
                one = yield give(at, lax.ppermute(half, "prow", far))
                two = lax.ppermute(one, "prow", [(p, p ^ 1) for p in range(d, 2 * d)])
                tops += [one, two]
                whole = both_halves(one, two)
            old_top = jnp.where((row >> log) == 1, whole, old_top)
            log += 1
        yield give(DONE, tops)

    slot = jax.ShapeDtypeStruct((nb, cols), f32)
    half_slot = jax.ShapeDtypeStruct((nb // 2, cols), f32)

    def exchange_rider():
        table, owner = yield give(2, call(
            functools.partial(index_kernel, row_dev=row_dev),
            (jax.ShapeDtypeStruct((8, nb), jnp.int32), jax.ShapeDtypeStruct((nb, LANES), jnp.int32)),
            [SMEM, VMEM], (VMEM, VMEM),
        )(here, pivots.reshape(1, nb)))
        held = yield give(3, call(gather_kernel, slot, [SMEM, VMEM], VMEM)(table, matrix))
        at = 5
        displaced = held
        log = 0
        half = None
        while (1 << log) < n_rows:
            d = 1 << log
            far = [(p, p ^ d) for p in range(n_rows)]
            if log == 0:
                whole = yield give(at, lax.ppermute(held, "prow", far))
                arrived = [whole]
            else:
                near = [(p, p ^ 1) for p in range(n_rows)]
                one = yield give(at + 4, lax.ppermute(half, "prow", far))
                at += 5
                two = yield give(at, lax.ppermute(one, "prow", near))
                arrived = [one, two]
                whole = both_halves(one, two)
            held, half = call(
                functools.partial(merge_kernel, log=log, halves=log > 0),
                (slot, half_slot), [SMEM] + [VMEM] * (2 + len(arrived)), (VMEM, VMEM),
            )(here, owner, held, *arrived)
            displaced = jnp.where((row >> log) == 1, whole, displaced)
            log += 1
        held, displaced = yield give(at + 1, (held, displaced))
        weights, top = yield give(at + 2, call(
            factor_kernel, (slot, slot), [SMEM, VMEM, VMEM, VMEM], (VMEM, VMEM),
            flops=4 * nb * nb * cols * 6,
        )(here, held, lower_inverse, upper_inverse))
        yield give(DONE, (table, displaced, weights, top))

    chain, cross, (tops, (table, displaced, weights, top)) = spread(
        [(flat[2 * i], flat[2 * i + 1]) for i in range(parts)], col, n_cols,
        [old_top_rider(), exchange_rider()],
    )
    bufs = chain + cross

    return call(
        functools.partial(
            final_kernel, n_bufs=len(bufs), n_tops=len(tops), n_cols=n_cols, parts=parts,
            block=512,
        ),
        jax.ShapeDtypeStruct(matrix.shape, f32),
        [SMEM, SMEM, SMEM, VMEM, VMEM, VMEM, ANY] + [ANY] * (len(bufs) + len(tops)),
        ANY,
        [
            pltpu.VMEM((row_dev, cols), f32),
            pltpu.VMEM((row_dev, nb), f32),
            pltpu.VMEM((nb, nb), f32),
            pltpu.VMEM((nb, cols), jnp.bfloat16),
            pltpu.VMEM((nb, cols), jnp.bfloat16),
            pltpu.VMEM((row_dev, cols), f32),
            pltpu.SemaphoreType.DMA((2,)),
            pltpu.SemaphoreType.DMA,
            pltpu.SemaphoreType.DMA((2,)),
            pltpu.SemaphoreType.DMA,
        ],
        vmem=30 << 20,
        flops=2 * row_dev * nb * cols * 3,
        moved=4 * row_dev * (2 * cols + nb),
    )(here, table, choice, displaced, weights, top, matrix, *bufs, *tops)


def solution(mesh):
    n_rows, n_cols = mesh.shape["prow"], mesh.shape["pcol"]
    return jax.shard_map(
        functools.partial(local, n_rows=n_rows, n_cols=n_cols, parts=8),
        mesh=mesh,
        in_specs=(P("prow", "pcol"), P(), P(), P()),
        out_specs=P("prow", "pcol"),
        check_vma=False,
    )
```
